32 devices in a mesh: dp: 8 (over z, x), seq: 4 (over y, core).
Axes of the slice: x: 2, y: 2, z: 4, core: 2. Of those that a mesh axis runs over, the one named last changes fastest.
Arguments:
- tokens: bfloat16 [24, 280, 768], P('dp', 'seq'), may hold values from -6 to 6
- cotangent: bfloat16 [24, 280, 768], P('dp', 'seq'), may hold values from -6 to 6
- text_mask: int32 [24, 40], P('dp'), may hold values from 0 to 1, as said below
- patch_count: int32 [24], P('dp'), may hold values from 100 to 240, as said below
- w_query: bfloat16 [768, 768], P('dp', 'seq'), may hold values from -0.21875 to 0.21875
- w_key: bfloat16 [768, 768], P('dp', 'seq'), may hold values from -0.21875 to 0.21875
- w_value: bfloat16 [768, 768], P('dp', 'seq'), may hold values from -0.21875 to 0.21875
- w_out: bfloat16 [768, 768], P('dp', 'seq'), may hold values from -0.875 to 0.875
- w_up: bfloat16 [768, 3072], P('dp', 'seq'), may hold values from -0.21875 to 0.21875
- w_down: bfloat16 [3072, 768], P('dp', 'seq'), may hold values from -0.109375 to 0.109375
- norm1_gain: bfloat16 [768], P('dp'), may hold values from 0.25 to 1.75
- norm1_bias: bfloat16 [768], P('dp'), may hold values from -4 to 4
- query_bias: bfloat16 [768], P('dp'), may hold values from -4 to 4
- value_bias: bfloat16 [768], P('dp'), may hold values from -3 to 3
- out_bias: bfloat16 [768], P('dp'), may hold values from -4 to 4
- norm2_gain: bfloat16 [768], P('dp'), may hold values from 0.25 to 1.75
- norm2_bias: bfloat16 [768], P('dp'), may hold values from -4 to 4
- up_bias: bfloat16 [3072], P('dp'), may hold values from -6 to 6
- down_bias: bfloat16 [768], P('dp'), may hold values from -4 to 4
Outputs:
- result: bfloat16 [24, 280, 768], P('dp', 'seq')
- input_grad: bfloat16 [24, 280, 768], P('dp', 'seq')
- g_query: float32 [768, 768], P('dp', 'seq')
- g_key: float32 [768, 768], P('dp', 'seq')
- g_value: float32 [768, 768], P('dp', 'seq')
- g_out: float32 [768, 768], P('dp', 'seq')
- g_up: float32 [768, 3072], P('dp', 'seq')
- g_down: float32 [3072, 768], P('dp', 'seq')
- g_norm1_gain: float32 [768], P('dp')
- g_norm1_bias: float32 [768], P('dp')
- g_query_bias: float32 [768], P('dp')
- g_value_bias: float32 [768], P('dp')
- g_out_bias: float32 [768], P('dp')
- g_norm2_gain: float32 [768], P('dp')
- g_norm2_bias: float32 [768], P('dp')
- g_up_bias: float32 [3072], P('dp')
- g_down_bias: float32 [768], P('dp')
The draws below stay inside these ranges and needn't reach their ends.
Inputs may be any that keep to these rules, and one draw needn't show every extreme that they name: `text_mask`: each item's word slots that hold words are a prefix of its 40 slots, and slot 0 always holds one. `patch_count`: in every aligned block of 3 items one item has all 240 patches.
All inputs are finite; a program needn't handle non-finite values.
Results may differ from the reference program's by a relative error of at most 0.015.
Values may be sent and summed in bfloat16 or wider, within the bound.
No kernel may reach another device: no remote copies, remote signals or barrier semaphores. Data moves between devices by JAX's collectives and lax.ppermute only.
A program may use at most 256 MiB of HBM per device.

```python
import jax
import jax.numpy as jnp
from jax import lax

D = 768
HEADS = 12
FF = 3072
TXT = 40
PATCH = 240
PMIN = 100
ITEM_DEV = 3
ITEMS = 24
LENGTH = 280


def draw_patch_count(key, part):
    key = jax.random.fold_in(key, 11)
    first_key, second_key = jax.random.split(key)
    counts = jax.random.randint(first_key, (ITEMS,), PMIN, PATCH + 1)
    picked = jax.random.randint(second_key, (ITEMS // ITEM_DEV,), 0, ITEM_DEV)
    slots = jnp.arange(ITEMS, dtype=jnp.int32) % ITEM_DEV
    full = slots == jnp.repeat(picked, ITEM_DEV)
    return jnp.where(full, PATCH, counts).astype(jnp.int32)


def draw_text_mask(key, part):
    key = jax.random.fold_in(key, 23)
    lengths = jax.random.randint(key, (ITEMS, 1), 1, TXT + 1)
    return (jnp.arange(TXT, dtype=jnp.int32)[None, :] < lengths).astype(jnp.int32)


def steps_of(stream_key, extent, shards, least, high):
    def one(dim, parts):
        draws = jax.random.uniform(jax.random.fold_in(jax.random.fold_in(stream_key, 6), dim), (parts,), jnp.float32, least / len(shards), high / len(shards))
        return jnp.repeat(jnp.exp(draws), extent[dim] // parts).reshape((-1,) + (1,) * (len(extent) - dim - 1))

    level = one(*shards[0])
    for cut in shards[1:]:
        level = level * one(*cut)
    return level


def noise(stream_key, extent, spread, limit, pieces=(), kind=jnp.bfloat16):
    array = spread * jax.random.normal(stream_key, extent, jnp.float32)
    if pieces:
        array = array * steps_of(stream_key, extent, pieces, -0.22, 0.18)
    return jnp.clip(array, -limit, limit).astype(kind)


def setup_inputs(seed: int = 0) -> dict:
    streams_of = jax.random.split(jax.random.key(seed), 20)
    return {
        "tokens": noise(streams_of[0], (ITEMS, LENGTH, D), 1.0, 6.0, ((0, 8), (1, 4))),
        "cotangent": noise(streams_of[1], (ITEMS, LENGTH, D), 1.0, 6.0, ((0, 8), (1, 4))),
        "text_mask": draw_text_mask(jax.random.fold_in(streams_of[19], 71), 0),
        "patch_count": draw_patch_count(jax.random.fold_in(streams_of[19], 71), 0),
        "w_query": noise(streams_of[4], (D, D), D ** -0.5, 0.21875, ((0, 8), (1, 4))),
        "w_key": noise(streams_of[5], (D, D), D ** -0.5, 0.21875, ((0, 8), (1, 4))),
        "w_value": noise(streams_of[6], (D, D), D ** -0.5, 0.21875, ((0, 8), (1, 4))),
        "w_out": noise(streams_of[7], (D, D), (D // 16) ** -0.5, 0.875, ((0, 8), (1, 4))),
        "w_up": noise(streams_of[8], (D, FF), D ** -0.5, 0.21875, ((0, 8), (1, 4))),
        "w_down": noise(streams_of[9], (FF, D), FF ** -0.5, 0.109375, ((0, 8), (1, 4))),
        "norm1_gain": jnp.clip(1.0 + 0.15 * jax.random.normal(streams_of[10], (D,), jnp.float32), 0.25, 1.75).astype(jnp.bfloat16),
        "norm1_bias": noise(streams_of[11], (D,), 0.3, 4.0, ((0, 8),)),
        "query_bias": noise(streams_of[12], (D,), 0.3, 4.0, ((0, 8),)),
        "value_bias": noise(streams_of[13], (D,), 0.2, 3.0, ((0, 8),)),
        "out_bias": noise(streams_of[14], (D,), 0.3, 4.0, ((0, 8),)),
        "norm2_gain": jnp.clip(1.0 + 0.15 * jax.random.normal(streams_of[15], (D,), jnp.float32), 0.25, 1.75).astype(jnp.bfloat16),
        "norm2_bias": noise(streams_of[16], (D,), 0.3, 4.0, ((0, 8),)),
        "up_bias": noise(streams_of[17], (FF,), 0.5, 6.0, ((0, 8),)),
        "down_bias": noise(streams_of[18], (D,), 0.3, 4.0, ((0, 8),)),
    }


@jax.custom_vjp
def low(v):
    return lax.optimization_barrier(v.astype(jnp.bfloat16)).astype(jnp.float32)

@jax.custom_vjp
def low_back(v):
    return v

def low_keep(v):
    return (low(v), None)

def low_pass(kept, grad):
    return (grad,)

def back_keep(v):
    return (v, None)

def back_low(kept, grad):
    return (low(grad),)
low.defvjp(low_keep, low_pass)
low_back.defvjp(back_keep, back_low)
HIGH = lax.Precision.HIGHEST
EPS = 1e-05

def layer_norm(values):
    center = values - lax.optimization_barrier(jnp.mean(values, axis=-1, keepdims=True))
    return center * lax.rsqrt(lax.optimization_barrier(jnp.mean(center * center, axis=-1, keepdims=True)) + EPS)

def norm_affine(values, gain, shift):
    return layer_norm(values) * gain + shift

def dense(values, weight):
    return jnp.einsum('gld,de->gle', values, weight, precision=HIGH)

def key_valid(text_mask, patch_count, length):
    rows = lax.iota(jnp.int32, length)
    text_len = text_mask.shape[1]
    onehot = (rows[:, None] == lax.iota(jnp.int32, text_len)[None, :]).astype(jnp.int32)
    text_ok = lax.optimization_barrier(jnp.sum(text_mask[:, None, :] * onehot[None, :, :], axis=-1)) > 0
    patch_ok = rows[None, :] - text_len < patch_count[:, None]
    return jnp.where(rows[None, :] < text_len, text_ok, patch_ok)

def forward(inputs, w_query, w_key, w_value, w_out, w_up, w_down, norm1_gain, norm1_bias, query_bias, value_bias, out_bias, norm2_gain, norm2_bias, up_bias, down_bias, valid):
    batch, length, width = inputs.shape
    head = width // HEADS
    scale = head ** (-0.5)
    normed1 = low(norm_affine(inputs, norm1_gain, norm1_bias))
    queries = low(low_back(dense(normed1, w_query) + query_bias)).reshape(batch, length, HEADS, head)
    keys = low(low_back(dense(normed1, w_key))).reshape(batch, length, HEADS, head)
    values = low(low_back(dense(normed1, w_value) + value_bias)).reshape(batch, length, HEADS, head)
    scores = low_back(jnp.einsum('bqhd,bkhd->bhqk', queries, keys, precision=HIGH) * scale)
    scores = jnp.where(valid[:, None, None, :], scores, -1e+30)
    top = lax.optimization_barrier(jnp.max(scores, axis=-1, keepdims=True))
    expo = jnp.exp(scores - top)
    probs = low(expo / lax.optimization_barrier(jnp.sum(expo, axis=-1, keepdims=True)))
    mixed = jnp.einsum('bhqk,bkhd->bqhd', probs, values, precision=HIGH)
    mixed = low(low_back(mixed)).reshape(batch, length, width)
    attended = low_back(dense(mixed, w_out) + out_bias)
    resid = inputs + attended
    normed2 = low(norm_affine(resid, norm2_gain, norm2_bias))
    hidden = low_back(dense(normed2, w_up) + up_bias)
    active = low(jax.nn.gelu(hidden, approximate=False))
    branch = low_back(dense(active, w_down) + down_bias)
    return resid + branch

def reference(tokens, cotangent, text_mask, patch_count, w_query, w_key, w_value, w_out, w_up, w_down, norm1_gain, norm1_bias, query_bias, value_bias, out_bias, norm2_gain, norm2_bias, up_bias, down_bias):
    params = tuple((piece.astype(jnp.float32) for piece in (w_query, w_key, w_value, w_out, w_up, w_down, norm1_gain, norm1_bias, query_bias, value_bias, out_bias, norm2_gain, norm2_bias, up_bias, down_bias)))
    length = TXT + PATCH
    groups = ITEMS // ITEM_DEV
    token_groups = tokens.reshape(groups, ITEM_DEV, length, D)
    cot_groups = cotangent.reshape(groups, ITEM_DEV, length, D)
    mask_groups = text_mask.reshape(groups, ITEM_DEV, TXT)
    count_groups = patch_count.reshape(groups, ITEM_DEV)

    def group_step(summed, inputs):
        token_block, cot_block, mask_block, count_block = inputs
        valid = key_valid(mask_block, count_block, length)

        def local_forward(values, *weights):
            return forward(values, *weights, valid)
        output, backward = jax.vjp(local_forward, token_block.astype(jnp.float32), *params)
        grads = backward(cot_block.astype(jnp.float32))
        updated = tuple((first + second for first, second in zip(summed, grads[1:])))
        return (updated, (output.astype(jnp.bfloat16), grads[0].astype(jnp.bfloat16)))
    start = tuple((jnp.zeros(piece.shape, jnp.float32) for piece in params))
    summed, (outputs, input_grads) = lax.scan(group_step, start, (token_groups, cot_groups, mask_groups, count_groups))
    result = outputs.reshape(ITEMS, length, D)
    input_grad = input_grads.reshape(ITEMS, length, D)
    return (result, input_grad, summed[0], summed[1], summed[2], summed[3], summed[4], summed[5], summed[6], summed[7], summed[8], summed[9], summed[10], summed[11], summed[12], summed[13], summed[14])
```

```python
import functools
from types import SimpleNamespace

import jax
import jax.numpy as jnp
from jax import lax
from jax.experimental import pallas as pl
from jax.experimental.pallas import tpu as pltpu
from jax.sharding import PartitionSpec as P

HEADS = 12
EPS = 1e-05
LOW = jnp.bfloat16
F32 = jnp.float32
VECS = 16
SQRT_HALF = 0.7071067811865476
PDF_SCALE = 0.3989422804014327


def dot(left, right):
    return jnp.dot(left, right, preferred_element_type=F32)


def dot_t(left, right):
    return lax.dot_general(left, right, (((1,), (1,)), ((), ())), preferred_element_type=F32)


def t_dot(left, right):
    return lax.dot_general(left, right, (((0,), (0,)), ((), ())), preferred_element_type=F32)


def col_sum(values):
    return jnp.sum(values, axis=0, keepdims=True)


def ds(start, size, align=16):
    if not isinstance(start, int):
        start = pl.multiple_of(start, align)
    return pl.ds(start, size)


def pallas(body, outs, ins, scratch=(), flops=0, smem=1, name=None):
    nbytes = sum(a.size * a.dtype.itemsize for a in ins)
    nbytes += sum(s.size * jnp.dtype(s.dtype).itemsize for s in outs)
    return pl.pallas_call(
        body,
        out_shape=outs,
        in_specs=[pl.BlockSpec(memory_space=pltpu.SMEM)] * smem
        + [pl.BlockSpec(memory_space=pltpu.VMEM)] * (len(ins) - smem),
        out_specs=[pl.BlockSpec(memory_space=pltpu.VMEM)] * len(outs),
        scratch_shapes=list(scratch),
        compiler_params=pltpu.CompilerParams(vmem_limit_bytes=56 * 2**20),
        cost_estimate=pl.CostEstimate(flops=flops, bytes_accessed=nbytes, transcendentals=0),
        name=name,
    )(*ins)


def shape(*dims, dtype=LOW):
    return jax.ShapeDtypeStruct(dims, dtype)


def part_index(m, sc, part):
    z, x = sc[1], sc[2]
    k = part % m.nz
    side = x if part < m.nz else 1 - x
    return lax.rem(z - k + m.nz, m.nz) * 2 + side


def layer_norm(x):
    center = x - jnp.mean(x, axis=-1, keepdims=True)
    rstd = lax.rsqrt(jnp.mean(center * center, axis=-1, keepdims=True) + EPS)
    return center * rstd, rstd


def norm_back(grad, gain, xhat, rstd):
    scaled = grad * gain
    first = jnp.mean(scaled, axis=-1, keepdims=True)
    second = jnp.mean(scaled * xhat, axis=-1, keepdims=True)
    return rstd * (scaled - first - xhat * second)


def attend_kernel(m, nparts, *refs):
    sc, counts = refs[:2]
    tokens = refs[2 : 2 + m.S]
    parts = refs[2 + m.S : 2 + m.S + nparts]
    qkv, xhat_ref, normed, probs, packed, vecs, w_ref, x_scr = refs[2 + m.S + nparts :]
    me = sc[0]
    if nparts == 1:
        w_ref[...] = parts[0][...]
    else:
        for p, part in enumerate(parts):
            w_ref[ds(part_index(m, sc, p) * m.rows, m.rows), :] = part[...]
    base = (3 * m.WH) // 128 * 128
    turned = w_ref[:, base : base + 128].astype(F32).T
    vecs[...] = turned[3 * m.WH - base : 3 * m.WH - base + VECS]
    gain, shift = vecs[0:1, :], vecs[1:2, :]
    q_bias = jnp.zeros((1, m.WH), F32)
    v_bias = jnp.zeros((1, m.WH), F32)
    for c in range(m.S):
        here = me == c
        q_bias = jnp.where(here, vecs[2:3, c * m.WH : (c + 1) * m.WH], q_bias)
        v_bias = jnp.where(here, vecs[3:4, c * m.WH : (c + 1) * m.WH], v_bias)
    bias = jnp.concatenate([q_bias, jnp.zeros((1, m.WH), F32), v_bias], axis=1)

    lane = lax.broadcasted_iota(jnp.int32, (1, m.IT), 1)
    place = jnp.full((1, m.IT), 1 << 20, jnp.int32)
    for d in range(m.S):
        row = lane - d * m.RP
        here = jnp.where(row < m.R, (me ^ d) * m.R + row, 1 << 20)
        place = jnp.where(row < 0, place, here)
    x_scr[...] = jnp.zeros_like(x_scr)

    def item(b, carry):
        at = ds(b * m.IT, m.IT)
        for d in range(m.S):
            x_scr[d * m.RP : d * m.RP + m.R, :] = tokens[d][b].astype(F32)
        xhat, _ = layer_norm(x_scr[...])
        low = (xhat * gain + shift).astype(LOW)
        xhat_ref[at, :] = xhat.astype(LOW)
        normed[at, :] = low
        qkv[at, :] = (dot(low, w_ref[:, : 3 * m.WH]) + bias).astype(LOW)
        masked = jnp.where(
            place < m.TXT,
            jnp.where(place < counts[b], 0.0, -1e30),
            jnp.where(place - m.TXT < counts[m.B + b], 0.0, -1e30),
        )
        half = m.IT // 2
        for h in range(m.H):
            q = qkv[at, h * m.hd : (h + 1) * m.hd] * LOW(m.hd**-0.5)
            k = qkv[at, m.WH + h * m.hd : m.WH + (h + 1) * m.hd]
            v = qkv[at, 2 * m.WH + h * m.hd : 2 * m.WH + (h + 1) * m.hd]
            s = dot_t(q, k) + masked
            e = jnp.exp(s - jnp.max(s, axis=-1, keepdims=True))
            p = (e * (1.0 / jnp.sum(e, axis=-1, keepdims=True))).astype(LOW)
            probs[b * m.H + h] = p
            o = dot(p, v).astype(LOW)
            packed[ds(b * half, half), h * m.hd : (h + 1) * m.hd] = o[:half]
            packed[ds(b * half, half), m.WH + h * m.hd : m.WH + (h + 1) * m.hd] = o[half:]
        return carry

    lax.fori_loop(0, m.B, item, 0)


def early_kernel(m, nparts, *refs):
    sc = refs[0]
    cots = refs[1 : 1 + m.S]
    parts = refs[1 + m.S : 1 + m.S + nparts]
    w_up, w_down, w_out, cot, g_act = refs[1 + m.S + nparts :]
    me = sc[0]
    if nparts == 1:
        whole = parts[0]
        w_up[...] = whole[0]
        w_down[...] = whole[1]
        for e in range(m.S):
            w_out[e * m.WH : (e + 1) * m.WH, :] = whole[2, ds((me ^ e) * m.WH, m.WH), :]
    else:
        per = m.N // m.S
        for p, part in enumerate(parts):
            i = part_index(m, sc, p)
            w_up[ds(i * m.rows, m.rows), :] = part[0]
            w_down[ds(i * m.hrows, m.hrows), :] = part[1]
            block = me ^ lax.div(i, per)
            w_out[ds(block * m.WH + lax.rem(i, per) * m.rows, m.rows), :] = part[2]
    cot[...] = jnp.zeros_like(cot)
    for b in range(m.B):
        for d in range(m.S):
            start = (b * m.S + d) * m.RP
            cot[start : start + m.R, :] = cots[d][b]

    def item(b, carry):
        at = ds(b * m.IT, m.IT)
        g_act[at, :] = dot_t(cot[at, :], w_down[...])
        return carry

    lax.fori_loop(0, m.B, item, 0)


def forward_kernel(m, *refs):
    sc = refs[0]
    tokens = refs[1 : 1 + m.S]
    packed = refs[1 + m.S : 1 + 2 * m.S]
    w_out, w_up, g_act, vecs = refs[1 + 2 * m.S : 5 + 2 * m.S]
    (normed, active, g_hidden, mixed, keep0, keep1, send, resid_own, xhat_own, rstd_own, x_scr) = refs[
        5 + 2 * m.S :
    ]
    me = sc[0]
    out_bias, gain, shift = vecs[4:5, :], vecs[5:6, :], vecs[6:7, :]
    up_bias = vecs[pl.ds(8 + me, 1), :]
    x_scr[...] = jnp.zeros_like(x_scr)

    def item(b, carry):
        at = ds(b * m.IT, m.IT)
        half = m.IT // 2
        for d in range(m.S):
            x_scr[d * m.RP : d * m.RP + m.R, :] = tokens[d][b].astype(F32)
        for e in range(m.S):
            for side in range(2):
                piece = packed[e][ds(b * half, half), side * m.WH : (side + 1) * m.WH]
                for t in range(2):
                    d = (2 * side + t) ^ e
                    mixed[ds(b * m.IT + d * m.RP, m.RP), e * m.WH : (e + 1) * m.WH] = piece[
                        t * m.RP : (t + 1) * m.RP
                    ]
        resid = x_scr[...] + (dot(mixed[at, :], w_out[...]) + out_bias)
        xhat, rstd = layer_norm(resid)
        own = ds(b * m.RP, m.RP)
        resid_own[own, :] = resid[: m.RP]
        xhat_own[own, :] = xhat[: m.RP]
        rstd_own[own, :] = jnp.broadcast_to(rstd[: m.RP], (m.RP, 128))
        low = (xhat * gain + shift).astype(LOW)
        normed[at, :] = low
        hidden = dot(low, w_up[...]) + up_bias
        cdf = 0.5 + 0.5 * lax.erf(hidden * SQRT_HALF)
        active[at, :] = (hidden * cdf).astype(LOW)
        slope = cdf + hidden * (PDF_SCALE * jnp.exp(-0.5 * hidden * hidden))
        back = (g_act[at, :] * slope).astype(LOW)
        g_hidden[at, :] = back
        grad = dot_t(back, w_up[...]).astype(LOW)
        keep0[own, :] = grad[: m.RP]
        send[0, own, :] = grad[m.RP : 2 * m.RP]
        keep1[own, :] = grad[2 * m.RP : 3 * m.RP]
        send[1, own, :] = grad[3 * m.RP : 4 * m.RP]
        return carry

    lax.fori_loop(0, m.B, item, 0)


def give_shards(m, sc, total, keep, send, first, rows):
    for k in range(m.nz):
        z = lax.rem(sc[1] + k, m.nz)
        here = (2 * z + sc[2]) * rows
        there = (2 * z + 1 - sc[2]) * rows
        keep[k, first : first + rows, :] = total[ds(here, rows), :].astype(LOW)
        send[k, first : first + rows, :] = total[ds(there, rows), :].astype(LOW)


def ff_grads_kernel(m, *refs):
    sc, active, g_hidden, normed, cot, w_down = refs[:6]
    keep0, keep1, send, vec, g_first, g_second, total = refs[6:]
    vec[...] = jnp.zeros_like(vec)

    def item(b, carry):
        at = ds(b * m.IT, m.IT)
        own = ds(b * m.RP, m.RP)
        part = dot(active[at, :], w_down[...]).astype(LOW)
        keep0[own, :] = part[: m.RP]
        send[0, own, :] = part[m.RP : 2 * m.RP]
        keep1[own, :] = part[2 * m.RP : 3 * m.RP]
        send[1, own, :] = part[3 * m.RP : 4 * m.RP]
        vec[0:1, :] += col_sum(cot[ds(b * m.IT, m.RP), :].astype(F32))
        vec[1:2, :] += col_sum(g_hidden[at, :].astype(F32))
        return carry

    lax.fori_loop(0, m.B, item, 0)
    step = 256
    for pair in ((normed, g_hidden), (active, cot)):
        first = pair[0] is active
        for begin in range(0, m.D, step):
            total[begin : begin + step, :] = t_dot(pair[0][:, begin : begin + step], pair[1][...])
        if m.fast:
            give_shards(m, sc, total, g_first, g_second, m.rows if first else 0, m.rows)
        elif first:
            g_second[...] = total[...].astype(LOW)
        else:
            g_first[...] = total[...].astype(LOW)


def middle_kernel(m, *refs):
    sc, keep0, core, far, xhat_own, rstd_own, cot, w_out, vecs = refs[:9]
    g_resid = refs[9]
    blocks = refs[10 : 10 + m.S]
    vec, low_scr = refs[10 + m.S :]
    me = sc[0]
    gain = vecs[5:6, :]
    grad = keep0[...].astype(F32) + core[0].astype(F32) + far[...].astype(F32)
    xhat = xhat_own[...]
    back = norm_back(grad, gain, xhat, rstd_own[:, 0:1])
    vec[...] = jnp.zeros_like(vec)
    vec[0:1, :] = col_sum(grad * xhat)
    vec[1:2, :] = col_sum(grad)
    for b in range(m.B):
        own = slice(b * m.RP, (b + 1) * m.RP)
        full = back[own] + cot[b * m.IT : b * m.IT + m.RP, :].astype(F32)
        g_resid[own, :] = full
        low_scr[own, :] = full.astype(LOW)
    low = low_scr[...]
    vec[2:3, :] = col_sum(low.astype(F32))
    g_mixed = dot_t(low, w_out[...]).astype(LOW)
    for e in range(m.S):
        blocks[e][:, : m.WH] = g_mixed[:, e * m.WH : (e + 1) * m.WH]
        picked = low[:, : m.WH]
        for c in range(1, m.S):
            picked = jnp.where((me ^ e) == c, low[:, c * m.WH : (c + 1) * m.WH], picked)
        blocks[e][:, m.WH :] = picked


def attend_back_kernel(m, *refs):
    sc, qkv, probs = refs[:3]
    blocks = refs[3 : 3 + m.S]
    normed, xhat, mixed, w, vec_mid, vec_ff = refs[3 + m.S : 9 + m.S]
    keep0, keep1, send, g_first, g_second, g_scr, ga_scr, v_scr, total = refs[9 + m.S :]
    me = sc[0]
    own_rows = m.B * m.RP
    v_scr[...] = jnp.zeros_like(v_scr)
    scale = m.hd**-0.5

    def item(b, carry):
        at = ds(b * m.IT, m.IT)
        own = ds(b * m.RP, m.RP)
        for d in range(m.S):
            ga_scr[ds(b * m.IT + d * m.RP, m.RP), :] = blocks[d][own, m.WH :]
        gm_all = jnp.concatenate([blocks[d][own, : m.WH] for d in range(m.S)], axis=0)
        for h in range(m.H):
            lanes = slice(h * m.hd, (h + 1) * m.hd)
            q = qkv[at, h * m.hd : (h + 1) * m.hd]
            k = qkv[at, m.WH + h * m.hd : m.WH + (h + 1) * m.hd]
            v = qkv[at, 2 * m.WH + h * m.hd : 2 * m.WH + (h + 1) * m.hd]
            gm = gm_all[:, lanes]
            low = probs[b * m.H + h]
            p = low.astype(F32)
            gp = dot_t(gm, v)
            gs = (p * (gp - jnp.sum(p * gp, axis=-1, keepdims=True))).astype(LOW)
            gq = (dot(gs, k) * scale).astype(LOW)
            gk = (t_dot(gs, q) * scale).astype(LOW)
            gv = t_dot(low, gm).astype(LOW)
            g_scr[at, h * m.hd : (h + 1) * m.hd] = gq
            g_scr[at, m.WH + h * m.hd : m.WH + (h + 1) * m.hd] = gk
            g_scr[at, 2 * m.WH + h * m.hd : 2 * m.WH + (h + 1) * m.hd] = gv
        grad = dot_t(g_scr[at, :], w[:, : 3 * m.WH])
        v_scr[0:1, :] += col_sum(grad * xhat[at, :].astype(F32))
        v_scr[1:2, :] += col_sum(grad)
        grad = grad.astype(LOW)
        keep0[own, :] = grad[: m.RP]
        send[0, own, :] = grad[m.RP : 2 * m.RP]
        keep1[own, :] = grad[2 * m.RP : 3 * m.RP]
        send[1, own, :] = grad[3 * m.RP : 4 * m.RP]
        return carry

    lax.fori_loop(0, m.B, item, 0)
    sums = col_sum(g_scr[...].astype(F32))
    for c in range(m.S):
        here = me == c
        lanes = slice(c * m.WH, (c + 1) * m.WH)
        v_scr[2:3, lanes] = jnp.where(here, sums[:, : m.WH], 0.0)
        v_scr[3:4, lanes] = jnp.where(here, sums[:, 2 * m.WH :], 0.0)
        v_scr[8 + c : 9 + c, :] = jnp.where(here, vec_ff[1:2, :], 0.0)
    v_scr[4:5, :] = vec_mid[2:3, :]
    v_scr[5:6, :] = vec_mid[0:1, :]
    v_scr[6:7, :] = vec_mid[1:2, :]
    v_scr[7:8, :] = vec_ff[0:1, :]
    values = v_scr[...].astype(LOW)
    tail = slice(own_rows, own_rows + VECS)
    keep0[tail, :] = values
    keep1[tail, :] = values
    send[0, tail, :] = values
    send[1, tail, :] = values
    total[:, : 3 * m.WH] = t_dot(normed[...], g_scr[...])
    g_out = t_dot(mixed[...], ga_scr[...])
    for e in range(m.S):
        total[ds((me ^ e) * m.WH, m.WH), 3 * m.WH :] = g_out[e * m.WH : (e + 1) * m.WH]
    if m.fast:
        give_shards(m, sc, total, g_first, g_second, 0, m.rows)
    else:
        g_first[...] = total[...].astype(LOW)
        g_second[...] = jnp.zeros_like(g_second)


def finish_kernel(m, *refs):
    keep0, core, far, tokens, g_resid, vecs, b_keep, b_core, b_far, resid = refs[1:11]
    result, input_grad = refs[11:]
    gain, down_bias = vecs[0:1, :], vecs[7:8, :]
    for b in range(m.B):
        own = slice(b * m.RP, b * m.RP + m.R)
        grad = keep0[own, :].astype(F32) + core[0, own, :].astype(F32) + far[own, :].astype(F32)
        xhat, rstd = layer_norm(tokens[b].astype(F32))
        back = norm_back(grad, gain, xhat, rstd)
        input_grad[b] = (g_resid[own, :] + back).astype(LOW)
        branch = b_keep[own, :].astype(F32) + b_core[0, own, :].astype(F32) + b_far[own, :].astype(F32)
        result[b] = (resid[own, :] + (branch + down_bias)).astype(LOW)


def plan(mesh, tokens, text_mask, w_query, w_up):
    m = SimpleNamespace()
    m.N, m.S = mesh.shape["dp"], mesh.shape["seq"]
    m.B, m.R, m.D = tokens.shape
    m.RP = -(-m.R // 16) * 16
    m.IT = m.S * m.RP
    m.RA = m.B * m.IT
    m.OWN = m.B * m.RP
    m.TXT = text_mask.shape[1]
    m.rows, m.WH = w_query.shape
    m.hd = m.D // HEADS
    m.H = HEADS // m.S
    m.FD = w_up.shape[1]
    m.hrows = m.FD // m.N
    m.fast = m.N == 8
    m.nz = m.N // 2
    m.vcols = 8 + m.S
    return m


def local(
    mesh,
    tokens,
    cotangent,
    text_mask,
    patch_count,
    w_query,
    w_key,
    w_value,
    w_out,
    w_up,
    w_down,
    norm1_gain,
    norm1_bias,
    query_bias,
    value_bias,
    out_bias,
    norm2_gain,
    norm2_bias,
    up_bias,
    down_bias,
):
    m = plan(mesh, tokens, text_mask, w_query, w_up)
    N, S, rows, WH, D = m.N, m.S, m.rows, m.WH, m.D
    dp = lax.axis_index("dp").astype(jnp.int32)
    me = lax.axis_index("seq").astype(jnp.int32)
    sc = jnp.stack([me, dp // 2, dp % 2])
    counts = jnp.concatenate([jnp.sum(text_mask, axis=1), patch_count])

    def seq_to(x, e):
        return lax.ppermute(x, "seq", [(i, i ^ e) for i in range(S)])

    def x_swap(x):
        return lax.ppermute(x, "dp", [(i, i ^ 1) for i in range(N)])

    def z_shift(x, k):
        return lax.ppermute(x, "dp", [(i, (i + 2 * k) % N) for i in range(N)])

    def gather_dp(x, axis):
        if not m.fast:
            return [lax.all_gather(x, "dp", axis=axis, tiled=True)]
        same = [x] + [z_shift(x, k) for k in range(1, m.nz)]
        return same + [x_swap(v) for v in same]

    def gather_seq(x):
        far = seq_to(x, 2)
        return [x, seq_to(x, 1), far, seq_to(far, 1)]

    vec_cols = jnp.stack(
        [norm1_gain, norm1_bias, query_bias, value_bias, out_bias, norm2_gain, norm2_bias, down_bias], axis=1
    )
    vec_cols = jnp.concatenate([vec_cols, up_bias.reshape(S, m.hrows).T], axis=1)
    wide = -(-(3 * WH + VECS) // 128) * 128
    first = jnp.concatenate(
        [w_query, w_key, w_value, vec_cols, jnp.zeros((rows, wide - 3 * WH - m.vcols), LOW)], axis=1
    )
    first_parts = gather_dp(first, 0)
    token_blocks = gather_seq(tokens)
    cot_blocks = gather_seq(cotangent)

    per = N // S
    up_parts = w_up.reshape(rows, per, S, m.hrows).transpose(2, 0, 1, 3).reshape(S, rows, WH)
    down_parts = w_down.reshape(S, m.hrows, WH)
    out_parts = jnp.broadcast_to(w_out, (S, rows, WH))
    mixed_parts = jnp.stack([up_parts, down_parts, out_parts], axis=1)
    swapped = lax.all_to_all(mixed_parts, "seq", 0, 0, tiled=True)
    second = swapped.transpose(1, 2, 0, 3).reshape(3, rows, D)
    second_parts = gather_dp(second, 1)

    qkv, xhat, normed, probs, packed, vecs, w_first = pallas(
        functools.partial(attend_kernel, m, len(first_parts)),
        [
            shape(m.RA, 3 * WH),
            shape(m.RA, D),
            shape(m.RA, D),
            shape(m.B * m.H, m.IT, m.IT),
            shape(m.B * m.IT // 2, 2 * WH),
            shape(VECS, D, dtype=F32),
            shape(D, wide),
        ],
        [sc, counts, *token_blocks, *first_parts],
        [pltpu.VMEM((m.IT, D), F32)],
        flops=2 * m.RA * D * 3 * WH + 4 * m.B * m.H * m.IT * m.IT * m.hd,
        smem=2,
        name="attend",
    )
    packed_blocks = gather_seq(packed)

    w_up_all, w_down_all, w_out_all, cot, g_act = pallas(
        functools.partial(early_kernel, m, len(second_parts)),
        [shape(D, m.FD), shape(m.FD, D), shape(D, D), shape(m.RA, D), shape(m.RA, m.FD, dtype=F32)],
        [sc, *cot_blocks, *second_parts],
        flops=2 * m.RA * D * m.FD,
        name="early",
    )

    normed2, active, g_hidden, mixed, keep0, keep1, send, resid, xhat2, rstd2 = pallas(
        functools.partial(forward_kernel, m),
        [
            shape(m.RA, D),
            shape(m.RA, m.FD),
            shape(m.RA, m.FD),
            shape(m.RA, D),
            shape(m.OWN, D),
            shape(m.OWN, D),
            shape(2, m.OWN, D),
            shape(m.OWN, D, dtype=F32),
            shape(m.OWN, D, dtype=F32),
            shape(m.OWN, 128, dtype=F32),
        ],
        [sc, *token_blocks, *packed_blocks, w_out_all, w_up_all, g_act, vecs],
        [pltpu.VMEM((m.IT, D), F32)],
        flops=2 * m.RA * D * (D + 2 * m.FD),
        name="forward",
    )

    def add_pair(left, right):
        return (left.astype(F32) + right.astype(F32)).astype(LOW)

    def reduce_seq(keep1, send):
        core = seq_to(send, 1)
        return core, seq_to(add_pair(keep1, core[1]), 2)

    core2, far2 = reduce_seq(keep1, send)

    if m.fast:
        ff_shapes = [shape(m.nz, 2 * rows, D), shape(m.nz, 2 * rows, D)]
        a_shapes = [shape(m.nz, rows, D), shape(m.nz, rows, D)]
    else:
        ff_shapes = [shape(D, m.FD), shape(m.FD, D)]
        a_shapes = [shape(D, D), shape(8, 128)]

    b_keep0, b_keep1, b_send, vec_ff, ff_keep, ff_send = pallas(
        functools.partial(ff_grads_kernel, m),
        [
            shape(m.OWN, D),
            shape(m.OWN, D),
            shape(2, m.OWN, D),
            shape(8, D, dtype=F32),
            *ff_shapes,
        ],
        [sc, active, g_hidden, normed2, cot, w_down_all],
        [pltpu.VMEM((D, D), F32)],
        flops=2 * m.RA * D * 3 * m.FD,
        name="ff_grads",
    )

    g_resid, *blocks, vec_mid = pallas(
        functools.partial(middle_kernel, m),
        [
            shape(m.OWN, D, dtype=F32),
            *[shape(m.OWN, 2 * WH)] * S,
            shape(8, D, dtype=F32),
        ],
        [sc, keep0, core2, far2, xhat2, rstd2, cot, w_out_all, vecs],
        [pltpu.VMEM((m.OWN, D), LOW)],
        flops=2 * m.OWN * D * D,
        name="middle",
    )
    blocks = [blocks[0]] + [seq_to(blocks[e], e) for e in range(1, S)]

    def scatter_dp(keep, send):
        got = x_swap(send)
        total = keep.astype(F32) + got.astype(F32)
        low = total.astype(LOW)
        out = total[0]
        for k in range(1, m.nz):
            out = out + z_shift(low[k], k).astype(F32)
        return out

    if m.fast:
        g_ff = scatter_dp(ff_keep, ff_send)
    else:
        g_ff = jnp.concatenate(
            [lax.psum_scatter(g, "dp", scatter_dimension=0, tiled=True) for g in (ff_keep, ff_send)], axis=0
        ).astype(F32)
    g_ff = lax.all_to_all(g_ff.astype(LOW).reshape(2 * rows, S, WH).transpose(1, 0, 2), "seq", 0, 0, tiled=True)
    g_ff = g_ff.astype(F32)
    g_up = g_ff[:, :rows].reshape(S, rows, per, m.hrows).transpose(1, 2, 0, 3).reshape(rows, m.FD)
    g_down = g_ff[:, rows:].reshape(S * m.hrows, WH)

    keep0, keep1, send, a_keep, a_send = pallas(
        functools.partial(attend_back_kernel, m),
        [
            shape(m.OWN + VECS, D),
            shape(m.OWN + VECS, D),
            shape(2, m.OWN + VECS, D),
            *a_shapes,
        ],
        [sc, qkv, probs, *blocks, normed, xhat, mixed, w_first, vec_mid, vec_ff],
        [
            pltpu.VMEM((m.RA, 3 * WH), LOW),
            pltpu.VMEM((m.RA, WH), LOW),
            pltpu.VMEM((VECS, D), F32),
            pltpu.VMEM((D, D), F32),
        ],
        flops=2 * m.RA * D * 7 * WH + 8 * m.B * m.H * m.IT * m.IT * m.hd,
        name="attend_back",
    )
    if m.fast:
        g_a = scatter_dp(a_keep, a_send)
    else:
        g_a = lax.psum_scatter(a_keep, "dp", scatter_dimension=0, tiled=True).astype(F32)
    core1, far1 = reduce_seq(keep1, send)
    b_core, b_far = reduce_seq(b_keep1, b_send)

    vec = keep0[m.OWN :].astype(F32) + core1[0, m.OWN :].astype(F32) + far1[m.OWN :].astype(F32)
    if m.fast:
        vec = vec + x_swap(vec)
        vec = vec + sum(z_shift(vec, k) for k in range(1, m.nz))
    else:
        vec = lax.psum(vec, "dp")
    vec = lax.dynamic_slice(vec, (0, dp * rows), (VECS, rows))

    result, input_grad = pallas(
        functools.partial(finish_kernel, m),
        [shape(m.B, m.R, D), shape(m.B, m.R, D)],
        [sc, keep0, core1, far1, tokens, g_resid, vecs, b_keep0, b_core, b_far, resid],
        name="finish",
    )
    return (
        result,
        input_grad,
        g_a[:, :WH],
        g_a[:, WH : 2 * WH],
        g_a[:, 2 * WH : 3 * WH],
        g_a[:, 3 * WH :],
        g_up,
        g_down,
        vec[0],
        vec[1],
        vec[2],
        vec[3],
        vec[4],
        vec[5],
        vec[6],
        vec[8 : 8 + S].reshape(-1),
        vec[7],
    )


def solution(mesh):
    rows3, mat, vec = P("dp", "seq", None), P("dp", "seq"), P("dp")
    return jax.shard_map(
        functools.partial(local, mesh),
        mesh=mesh,
        in_specs=(rows3, rows3, P("dp", None), vec) + (mat,) * 6 + (vec,) * 9,
        out_specs=(rows3, rows3) + (mat,) * 6 + (vec,) * 9,
        check_vma=False,
    )
```

```python
import functools
from types import SimpleNamespace

import jax
import jax.numpy as jnp
from jax import lax
from jax.experimental import pallas as pl
from jax.experimental.pallas import tpu as pltpu
from jax.sharding import PartitionSpec as P

HEADS = 12
EPS = 1e-05
LOW = jnp.bfloat16
F32 = jnp.float32
VECS = 16
UP_BIAS = 12
SQRT_HALF = 0.7071067811865476
PDF_SCALE = 0.3989422804014327


def dot(left, right):
    return jnp.dot(left, right, preferred_element_type=F32)


def dot_t(left, right):
    return lax.dot_general(left, right, (((1,), (1,)), ((), ())), preferred_element_type=F32)


def t_dot(left, right):
    return lax.dot_general(left, right, (((0,), (0,)), ((), ())), preferred_element_type=F32)


def col_sum(values):
    return jnp.sum(values, axis=0, keepdims=True)


def ds(start, size, align=16):
    if not isinstance(start, int):
        start = pl.multiple_of(start, align)
    return pl.ds(start, size)


def pallas(body, outs, ins, scratch=(), smem=0, here=False, name=None, mib=8, long=False):
    flops = 10**10 if long else 1000
    nbytes = sum(a.size * a.dtype.itemsize for a in ins)
    nbytes += sum(s.size * jnp.dtype(s.dtype).itemsize for s in outs)
    near = pl.BlockSpec(memory_space=pltpu.VMEM)

    def run(*refs):
        if here:
            dp = lax.axis_index("dp")
            body((lax.axis_index("seq"), lax.div(dp, 2), lax.rem(dp, 2)), *refs)
        else:
            body(*refs)

    return pl.pallas_call(
        run,
        out_shape=outs,
        in_specs=[pl.BlockSpec(memory_space=pltpu.SMEM)] * smem + [near] * (len(ins) - smem),
        out_specs=[near] * len(outs),
        scratch_shapes=list(scratch),
        compiler_params=pltpu.CompilerParams(vmem_limit_bytes=mib * 2**20),
        cost_estimate=pl.CostEstimate(flops=flops, bytes_accessed=nbytes, transcendentals=0),
        name=name,
    )(*ins)


def shape(*dims, dtype=LOW):
    return jax.ShapeDtypeStruct(dims, dtype)


def part_index(m, sc, part):
    z, x = sc[1], sc[2]
    k = part % m.nz
    side = x if part < m.nz else 1 - x
    return lax.rem(z - k + m.nz, m.nz) * 2 + side


def layer_norm(x):
    center = x - jnp.mean(x, axis=-1, keepdims=True)
    rstd = lax.rsqrt(jnp.mean(center * center, axis=-1, keepdims=True) + EPS)
    return center * rstd, rstd


def norm_back(grad, gain, xhat, rstd):
    scaled = grad * gain
    first = jnp.mean(scaled, axis=-1, keepdims=True)
    second = jnp.mean(scaled * xhat, axis=-1, keepdims=True)
    return rstd * (scaled - first - xhat * second)


def pack_kernel(m, query, key, value, *refs):
    vecs, first, rows = refs[:9], refs[9], refs[10]
    first[:, : m.WH] = query[...]
    first[:, m.WH : 2 * m.WH] = key[...]
    first[:, 2 * m.WH : 3 * m.WH] = value[...]
    first[:, 3 * m.WH :] = jnp.zeros((m.rows, m.wide - 3 * m.WH), LOW)
    rows[...] = jnp.zeros_like(rows)
    for k in range(8):
        rows[k : k + 1, :] = vecs[k][...].astype(F32).reshape(1, m.rows)
    up_bias = vecs[8][...].astype(F32).reshape(1, m.S * m.hrows)
    for c in range(m.S):
        rows[8 + c : 9 + c, :] = up_bias[:, c * m.hrows : (c + 1) * m.hrows]
    first[:, 3 * m.WH : 3 * m.WH + VECS] = rows[...].T.astype(LOW)


def pack_up_kernel(m, up, out, far, packed):
    half = m.rows // 2
    packed[: m.rows, :] = up[...]
    for side in range(2):
        at = slice(side * half, (side + 1) * half)
        packed[m.rows :, 2 * side * m.WH : (2 * side + 1) * m.WH] = out[at, :]
        packed[m.rows :, (2 * side + 1) * m.WH : (2 * side + 2) * m.WH] = far[at, :]


def split_down_kernel(m, sc, down_t, first, second):
    half = m.WH // 2
    for x in range(2):

        @pl.when(sc[2] == x)
        def _(x=x):
            first[...] = down_t[x * half : (x + 1) * half, :]
            second[...] = down_t[(1 - x) * half : (2 - x) * half, :]


def join_down_kernel(m, sc, first, second, down):
    width = m.FD // 2
    for x in range(2):

        @pl.when(sc[2] == x)
        def _(x=x):
            down[:, x * width : (x + 1) * width] = first[...]
            down[:, (1 - x) * width : (2 - x) * width] = second[...]


def norm_kernel(m, *refs):
    tokens, (xhat, x_scr) = refs[: m.S], refs[m.S :]
    x_scr[...] = jnp.zeros_like(x_scr)

    def item(b, carry):
        for d in range(m.S):
            x_scr[d * m.RP : d * m.RP + m.R, :] = tokens[d][b].astype(F32)
        xhat[ds(b * m.IT, m.IT), :], _ = layer_norm(x_scr[...])
        return carry

    lax.fori_loop(0, m.B, item, 0)


def attend_kernel(m, nparts, *refs):
    sc, text_mask, patch_count, xhat_ref = refs[:4]
    parts = refs[4 : 4 + nparts]
    qkv, normed, probs, packed, vecs, w_ref = refs[4 + nparts :]
    me = sc[0]
    if nparts == 1:
        w_ref[...] = parts[0][...]
    else:
        for p, part in enumerate(parts):
            w_ref[ds(part_index(m, sc, p) * m.rows, m.rows), :] = part[...]
    base = (3 * m.WH) // 128 * 128
    turned = w_ref[:, base : base + 128].astype(F32).T
    vecs[...] = turned[3 * m.WH - base : 3 * m.WH - base + VECS]
    for c in range(m.S):

        @pl.when(me == c)
        def _(c=c):
            for t in range(m.N // m.S):
                for k in range(m.S):
                    lanes = slice((t * m.S + k) * m.hrows, (t * m.S + k + 1) * m.hrows)
                    begin = c * m.WH + t * m.rows
                    vecs[UP_BIAS : UP_BIAS + 1, lanes] = vecs[8 + k : 9 + k, begin : begin + m.rows]

    gain, shift = vecs[0:1, :], vecs[1:2, :]
    q_bias = jnp.zeros((1, m.WH), F32)
    v_bias = jnp.zeros((1, m.WH), F32)
    for c in range(m.S):
        here = me == c
        q_bias = jnp.where(here, vecs[2:3, c * m.WH : (c + 1) * m.WH], q_bias)
        v_bias = jnp.where(here, vecs[3:4, c * m.WH : (c + 1) * m.WH], v_bias)
    bias = jnp.concatenate([q_bias, jnp.zeros((1, m.WH), F32), v_bias], axis=1)

    lane = lax.broadcasted_iota(jnp.int32, (1, m.IT), 1)
    place = jnp.full((1, m.IT), 1 << 20, jnp.int32)
    for d in range(m.S):
        row = lane - d * m.RP
        here = jnp.where(row < m.R, (me ^ d) * m.R + row, 1 << 20)
        place = jnp.where(row < 0, place, here)

    def item(b, carry):
        at = ds(b * m.IT, m.IT)
        low = (xhat_ref[at, :] * gain + shift).astype(LOW)
        normed[at, :] = low
        qkv[at, :] = (dot(low, w_ref[:, : 3 * m.WH]) + bias).astype(LOW)
        words = text_mask[b, 0]
        for k in range(1, m.TXT):
            words = words + text_mask[b, k]
        masked = jnp.where(
            place < m.TXT,
            jnp.where(place < words, 0.0, -1e30),
            jnp.where(place - m.TXT < patch_count[b], 0.0, -1e30),
        )
        half = m.IT // 2
        for h in range(m.H):
            q = qkv[at, h * m.hd : (h + 1) * m.hd] * LOW(m.hd**-0.5)
            k = qkv[at, m.WH + h * m.hd : m.WH + (h + 1) * m.hd]
            v = qkv[at, 2 * m.WH + h * m.hd : 2 * m.WH + (h + 1) * m.hd]
            s = dot_t(q, k) + masked
            e = jnp.exp(s - jnp.max(s, axis=-1, keepdims=True))
            p = (e * (1.0 / jnp.sum(e, axis=-1, keepdims=True))).astype(LOW)
            probs[b * m.H + h] = p
            o = dot(p, v).astype(LOW)
            packed[ds(b * half, half), h * m.hd : (h + 1) * m.hd] = o[:half]
            packed[ds(b * half, half), m.WH + h * m.hd : m.WH + (h + 1) * m.hd] = o[half:]
        return carry

    lax.fori_loop(0, m.B, item, 0)


def assemble_kernel(m, nparts, *refs):
    sc = refs[0]
    parts = refs[1 : 1 + nparts]
    w_up, w_out = refs[1 + nparts :]
    half = m.rows // 2
    per = m.N // m.S
    for p, part in enumerate(parts):
        i = part_index(m, sc, p)
        w_up[ds(i * m.rows, m.rows), :] = part[: m.rows]
        start = (sc[0] ^ lax.div(i, per)) * m.WH + lax.rem(i, per) * m.rows
        w_out[ds(start, half), :] = part[m.rows :, : 2 * m.WH]
        w_out[ds(start + half, half), :] = part[m.rows :, 2 * m.WH :]


def join_kernel(m, sc, own, other, *refs):
    cots = refs[: m.S]
    w_out, cot = refs[m.S :]
    for c in range(m.S):

        @pl.when(sc[0] == c)
        def _(c=c):
            for d in range(m.S):
                half = (own, other)[d % 2]
                lanes = slice((c ^ d) * m.WH, ((c ^ d) + 1) * m.WH)
                for e in range(m.S):
                    rows = slice((e ^ (d % 2)) * m.WH, ((e ^ (d % 2)) + 1) * m.WH)
                    w_out[e * m.WH : (e + 1) * m.WH, lanes] = half[rows, d // 2 * m.WH : (d // 2 + 1) * m.WH]

    pad_cot(m, cots, cot)


def pad_cot(m, cots, cot):
    cot[...] = jnp.zeros_like(cot)
    for b in range(m.B):
        for d in range(m.S):
            start = (b * m.S + d) * m.RP
            cot[start : start + m.R, :] = cots[d][b]


def forward_kernel(m, *refs):
    sc = refs[0]
    tokens = refs[1 : 1 + m.S]
    packed = refs[1 + m.S : 1 + 2 * m.S]
    w_out, w_up, vecs = refs[1 + 2 * m.S : 4 + 2 * m.S]
    normed, active, slope, mixed, resid_own, xhat_own, rstd_own, x_scr = refs[4 + 2 * m.S :]
    me = sc[0]
    out_bias, gain, shift = vecs[4:5, :], vecs[5:6, :], vecs[6:7, :]
    up_bias = vecs[UP_BIAS : UP_BIAS + 1, :]
    x_scr[...] = jnp.zeros_like(x_scr)

    def item(b, carry):
        at = ds(b * m.IT, m.IT)
        half = m.IT // 2
        for d in range(m.S):
            x_scr[d * m.RP : d * m.RP + m.R, :] = tokens[d][b].astype(F32)
        for e in range(m.S):
            for side in range(2):
                piece = packed[e][ds(b * half, half), side * m.WH : (side + 1) * m.WH]
                for t in range(2):
                    d = (2 * side + t) ^ e
                    mixed[ds(b * m.IT + d * m.RP, m.RP), e * m.WH : (e + 1) * m.WH] = piece[
                        t * m.RP : (t + 1) * m.RP
                    ]
        resid = x_scr[...] + (dot(mixed[at, :], w_out[...]) + out_bias)
        xhat, rstd = layer_norm(resid)
        own = ds(b * m.RP, m.RP)
        resid_own[own, :] = resid[: m.RP]
        xhat_own[own, :] = xhat[: m.RP]
        rstd_own[own, :] = jnp.broadcast_to(rstd[: m.RP], (m.RP, 128))
        low = (xhat * gain + shift).astype(LOW)
        normed[at, :] = low
        hidden = dot(low, w_up[...]) + up_bias
        cdf = 0.5 + 0.5 * lax.erf(hidden * SQRT_HALF)
        active[at, :] = (hidden * cdf).astype(LOW)
        slope[at, :] = cdf + hidden * (PDF_SCALE * jnp.exp(-0.5 * hidden * hidden))
        return carry

    lax.fori_loop(0, m.B, item, 0)


def hidden_back_kernel(m, nparts, *refs):
    sc, cot, slope, w_up = refs[:4]
    parts = refs[4 : 4 + nparts]
    g_hidden, w_down, keep0, keep1, send = refs[4 + nparts :]
    if nparts == 1:
        w_down[...] = parts[0][...]
    else:
        for p, part in enumerate(parts):
            w_down[ds(part_index(m, sc, p) * m.rows, m.rows), :] = part[...]

    def item(b, carry):
        at = ds(b * m.IT, m.IT)
        back = (dot(cot[at, :], w_down[...]) * slope[at, :]).astype(LOW)
        g_hidden[at, :] = back
        give_rows(m, b, dot_t(back, w_up[...]).astype(LOW), keep0, keep1, send)
        return carry

    lax.fori_loop(0, m.B, item, 0)


def give_shards(m, sc, total, keep, send):
    for k in range(m.nz):
        z = lax.rem(sc[1] + k, m.nz)
        keep[k] = total[ds((2 * z + sc[2]) * m.rows, m.rows), :].astype(LOW)
        send[k] = total[ds((2 * z + 1 - sc[2]) * m.rows, m.rows), :].astype(LOW)


def give(m, sc, total, keep, send):
    if m.fast:
        give_shards(m, sc, total, keep, send)
    else:
        keep[...] = total[...].astype(LOW)
        send[...] = jnp.zeros_like(send)


def give_rows(m, b, values, keep0, keep1, send):
    own = ds(b * m.RP, m.RP)
    keep0[own, :] = values[: m.RP]
    send[0, own, :] = values[m.RP : 2 * m.RP]
    keep1[own, :] = values[2 * m.RP : 3 * m.RP]
    send[1, own, :] = values[3 * m.RP : 4 * m.RP]


def weight_grad_kernel(m, sc, left, right, keep, send, total):
    step = 256
    for begin in range(0, m.D, step):
        total[begin : begin + step, :] = t_dot(left[:, begin : begin + step], right[...])
    give(m, sc, total, keep, send)


def branch_kernel(m, active, w_down, g_hidden, cot, keep0, keep1, send, vec):
    vec[...] = jnp.zeros_like(vec)

    def item(b, carry):
        at = ds(b * m.IT, m.IT)
        give_rows(m, b, dot_t(active[at, :], w_down[...]).astype(LOW), keep0, keep1, send)
        vec[0:1, :] += col_sum(cot[ds(b * m.IT, m.RP), :].astype(F32))
        vec[1:2, :] += col_sum(g_hidden[at, :].astype(F32))
        return carry

    lax.fori_loop(0, m.B, item, 0)


def pair_kernel(m, keep, core, out):
    out[...] = (keep[...].astype(F32) + core[1].astype(F32)).astype(LOW)


def add_kernel(m, left, right, out):
    out[...] = left[...] + right[...]


def middle_kernel(m, *refs):
    sc, keep0, core, far, xhat_own, rstd_own, cot, w_out, vecs = refs[:9]
    g_resid = refs[9]
    blocks = refs[10 : 10 + m.S]
    vec, low_scr = refs[10 + m.S :]
    me = sc[0]
    gain = vecs[5:6, :]
    grad = keep0[...].astype(F32) + core[0].astype(F32) + far[...].astype(F32)
    xhat = xhat_own[...]
    back = norm_back(grad, gain, xhat, rstd_own[:, 0:1])
    vec[...] = jnp.zeros_like(vec)
    vec[0:1, :] = col_sum(grad * xhat)
    vec[1:2, :] = col_sum(grad)
    for b in range(m.B):
        own = slice(b * m.RP, (b + 1) * m.RP)
        full = back[own] + cot[b * m.IT : b * m.IT + m.RP, :].astype(F32)
        g_resid[own, :] = full
        low_scr[own, :] = full.astype(LOW)
    low = low_scr[...]
    vec[2:3, :] = col_sum(low.astype(F32))
    g_mixed = dot_t(low, w_out[...]).astype(LOW)
    for e in range(m.S):
        blocks[e][:, : m.WH] = g_mixed[:, e * m.WH : (e + 1) * m.WH]
        picked = low[:, : m.WH]
        for c in range(1, m.S):
            picked = jnp.where((me ^ e) == c, low[:, c * m.WH : (c + 1) * m.WH], picked)
        blocks[e][:, m.WH :] = picked


def value_back_kernel(m, *refs):
    sc, probs = refs[:2]
    blocks = refs[2 : 2 + m.S]
    normed, mixed = refs[2 + m.S : 4 + m.S]
    g_value, g_mixed, keep, send, ga_scr, total = refs[4 + m.S :]

    def item(b, carry):
        at = ds(b * m.IT, m.IT)
        own = ds(b * m.RP, m.RP)
        for d in range(m.S):
            ga_scr[ds(b * m.IT + d * m.RP, m.RP), :] = blocks[d][own, m.WH :]
            g_mixed[ds(b * m.IT + d * m.RP, m.RP), :] = blocks[d][own, : m.WH]
        for h in range(m.H):
            lanes = slice(h * m.hd, (h + 1) * m.hd)
            g_value[at, lanes] = t_dot(probs[b * m.H + h], g_mixed[at, lanes]).astype(LOW)
        return carry

    lax.fori_loop(0, m.B, item, 0)
    total[:, : m.WH] = t_dot(normed[...], g_value[...])
    g_out = t_dot(mixed[...], ga_scr[...])
    for e in range(m.S):
        total[ds((sc[0] ^ e) * m.WH, m.WH), m.WH :] = g_out[e * m.WH : (e + 1) * m.WH]
    give(m, sc, total, keep, send)


def attend_back_kernel(m, qkv, probs, g_mixed, g_qk):
    scale = m.hd**-0.5

    def item(b, carry):
        at = ds(b * m.IT, m.IT)
        for h in range(m.H):
            lanes = slice(h * m.hd, (h + 1) * m.hd)
            q = qkv[at, h * m.hd : (h + 1) * m.hd]
            k = qkv[at, m.WH + h * m.hd : m.WH + (h + 1) * m.hd]
            v = qkv[at, 2 * m.WH + h * m.hd : 2 * m.WH + (h + 1) * m.hd]
            p = probs[b * m.H + h].astype(F32)
            gp = dot_t(g_mixed[at, lanes], v)
            gs = (p * (gp - jnp.sum(p * gp, axis=-1, keepdims=True))).astype(LOW)
            g_qk[at, h * m.hd : (h + 1) * m.hd] = (dot(gs, k) * scale).astype(LOW)
            g_qk[at, m.WH + h * m.hd : m.WH + (h + 1) * m.hd] = (t_dot(gs, q) * scale).astype(LOW)
        return carry

    lax.fori_loop(0, m.B, item, 0)


def input_back_kernel(m, sc, g_qk, g_value, xhat, w, vec_mid, vec_ff, b_keep1, b_send, keep0, keep1, send, v_scr):
    me = sc[0]
    v_scr[...] = jnp.zeros_like(v_scr)

    def item(b, carry):
        at = ds(b * m.IT, m.IT)
        grad = dot_t(g_qk[at, :], w[:, : 2 * m.WH]) + dot_t(g_value[at, :], w[:, 2 * m.WH : 3 * m.WH])
        v_scr[0:1, :] += col_sum(grad * xhat[at, :])
        v_scr[1:2, :] += col_sum(grad)
        give_rows(m, b, grad.astype(LOW), keep0, keep1, send)
        return carry

    lax.fori_loop(0, m.B, item, 0)
    q_sum = col_sum(g_qk[:, : m.WH].astype(F32))
    v_sum = col_sum(g_value[...].astype(F32))
    for c in range(m.S):
        here = me == c
        lanes = slice(c * m.WH, (c + 1) * m.WH)
        v_scr[2:3, lanes] = jnp.where(here, q_sum, 0.0)
        v_scr[3:4, lanes] = jnp.where(here, v_sum, 0.0)
        for t in range(m.N // m.S):
            for k in range(m.S):
                begin = c * m.WH + t * m.rows
                part = vec_ff[1:2, (t * m.S + k) * m.hrows : (t * m.S + k + 1) * m.hrows]
                v_scr[8 + k : 9 + k, begin : begin + m.rows] = jnp.where(here, part, 0.0)
    v_scr[4:5, :] = vec_mid[2:3, :]
    v_scr[5:6, :] = vec_mid[0:1, :]
    v_scr[6:7, :] = vec_mid[1:2, :]
    v_scr[7:8, :] = vec_ff[0:1, :]
    keep1[m.OWN :, :] = b_keep1[...]
    send[0, m.OWN :, :] = b_send[0]
    send[1, m.OWN :, :] = b_send[1]


def sum_x_kernel(m, keep, got, own, *outs):
    own[...] = keep[0].astype(F32) + got[0].astype(F32)
    for k, out in enumerate(outs):
        out[...] = (keep[k + 1].astype(F32) + got[k + 1].astype(F32)).astype(LOW)


def last_x_kernel(m, keep, got, vec, vec_got, own, vec_own, *outs):
    own[...] = keep[0].astype(F32) + got[0].astype(F32)
    values = vec[...] + vec_got[...]
    half = m.D // 2
    vec_own[:VECS, :] = values[:, :half]
    vec_own[VECS:, :] = values[:, half:]
    for k, out in enumerate(outs):
        out[: m.rows, :] = (keep[k + 1].astype(F32) + got[k + 1].astype(F32)).astype(LOW)
        out[m.rows :, :] = vec_own[...].astype(LOW)


def sum_z_kernel(m, *refs):
    own, rest, outs = refs[0], refs[1 : m.nz], refs[m.nz :]
    total = own[...]
    for r in rest:
        total = total + r[...].astype(F32)
    outs[0][...] = total[:, : m.WH]
    outs[1][...] = total[:, m.WH :]


def last_z_kernel(m, sc, own, vec_own, *refs):
    rest, (first, second), vecs, picked = refs[: m.nz - 1], refs[m.nz - 1 : m.nz + 1], refs[m.nz + 1 : -1], refs[-1]
    total, values = own[...], vec_own[...]
    for r in rest:
        total = total + r[: m.rows, :].astype(F32)
        values = values + r[m.rows :, :].astype(F32)
    first[...] = total[:, : m.WH]
    second[...] = total[:, m.WH :]
    for i in range(m.N):

        @pl.when(2 * sc[1] + sc[2] == i)
        def _(i=i):
            side, lane = divmod(i * m.rows, m.D // 2)
            picked[...] = values[side * VECS : (side + 1) * VECS, lane : lane + m.rows]

    for k in range(8):
        vecs[k][...] = picked[k : k + 1, :].reshape(m.rows)
    vecs[8][...] = jnp.concatenate([picked[8 + c : 9 + c, :] for c in range(m.S)], axis=1).reshape(m.S * m.rows)


def sum_down_kernel(m, sc, own, *refs):
    rest, (first, second) = refs[:-2], refs[-2:]
    total = own[...]
    for r in rest:
        total = total + r[...].astype(F32)
    width = m.FD // 2
    for x in range(2):

        @pl.when(sc[2] == x)
        def _(x=x):
            first[...] = total[:, x * width : (x + 1) * width].astype(LOW)
            second[...] = total[:, (1 - x) * width : (2 - x) * width].astype(LOW)


def sum_up_kernel(m, own, *refs):
    rest, out = refs[:-1], refs[-1]
    total = own[...]
    for r in rest:
        total = total + r[...].astype(F32)
    out[...] = total


def give_down_kernel(m, sc, first, second, g_down):
    for x in range(2):

        @pl.when(sc[2] == x)
        def _(x=x):
            g_down[x * m.rows : (x + 1) * m.rows, :] = first[...].astype(F32)
            g_down[(1 - x) * m.rows : (2 - x) * m.rows, :] = second[...].astype(F32)


def finish_kernel(m, *refs):
    keep0, core, far, tokens, g_resid, vecs, b_keep, resid = refs[:8]
    result, input_grad = refs[8:]
    gain, down_bias = vecs[0:1, :], vecs[7:8, :]
    for b in range(m.B):
        own = slice(b * m.RP, b * m.RP + m.R)
        also = slice(m.OWN + b * m.RP, m.OWN + b * m.RP + m.R)
        grad = keep0[own, :].astype(F32) + core[0, own, :].astype(F32) + far[own, :].astype(F32)
        xhat, rstd = layer_norm(tokens[b].astype(F32))
        back = norm_back(grad, gain, xhat, rstd)
        input_grad[b] = (g_resid[own, :] + back).astype(LOW)
        branch = b_keep[own, :].astype(F32) + core[0, also, :].astype(F32) + far[also, :].astype(F32)
        result[b] = (resid[own, :] + (branch + down_bias)).astype(LOW)


def plan(mesh, tokens, text_mask, w_query, w_up):
    m = SimpleNamespace()
    m.N, m.S = mesh.shape["dp"], mesh.shape["seq"]
    m.B, m.R, m.D = tokens.shape
    m.RP = -(-m.R // 16) * 16
    m.IT = m.S * m.RP
    m.RA = m.B * m.IT
    m.OWN = m.B * m.RP
    m.TXT = text_mask.shape[1]
    m.rows, m.WH = w_query.shape
    m.hd = m.D // HEADS
    m.H = HEADS // m.S
    m.FD = w_up.shape[1]
    m.hrows = m.FD // m.N
    m.fast = m.N == 2 * m.S
    m.nz = m.N // 2
    m.wide = -(-(3 * m.WH + VECS) // 128) * 128
    m.up_rows = m.rows + m.rows // 2
    return m


def local(
    mesh,
    tokens,
    cotangent,
    text_mask,
    patch_count,
    w_query,
    w_key,
    w_value,
    w_out,
    w_up,
    w_down,
    norm1_gain,
    norm1_bias,
    query_bias,
    value_bias,
    out_bias,
    norm2_gain,
    norm2_bias,
    up_bias,
    down_bias,
):
    m = plan(mesh, tokens, text_mask, w_query, w_up)
    N, S, rows, WH, D, nz = m.N, m.S, m.rows, m.WH, m.D, m.nz
    dp = lax.axis_index("dp").astype(jnp.int32)
    me = lax.axis_index("seq").astype(jnp.int32)
    fn = functools.partial

    def seq_to(x, e):
        return lax.ppermute(x, "seq", [(i, i ^ e) for i in range(S)])

    def x_swap(x):
        return lax.ppermute(x, "dp", [(i, i ^ 1) for i in range(N)])

    def z_shift(x, k):
        return lax.ppermute(x, "dp", [(i, (i + 2 * k) % N) for i in range(N)])

    def gate(x, *others):
        return lax.optimization_barrier((x, *others))[0]

    def direct(x):
        same = [x] + [z_shift(x, k) for k in range(1, nz)]
        return same + [x_swap(v) for v in same]

    def around(x):
        a, b = z_shift(x, 1), z_shift(x, nz - 1)
        return [x, a, z_shift(a, 1), b]

    def exchange(x, k):
        pairs = []
        for i in range(N):
            for j in range(S):
                to = 2 * j + (i + k) % 2
                pairs.append((i * S + j, to * S + i // 2))
        return lax.ppermute(x, ("dp", "seq"), pairs)

    def gather_seq(x):
        far = seq_to(x, 2)
        return [x, seq_to(x, 1), far, seq_to(far, 1)]

    vectors = [norm1_gain, norm1_bias, query_bias, value_bias, out_bias, norm2_gain, norm2_bias, down_bias, up_bias]
    if m.fast:
        out_far = seq_to(w_out, 2)
        (first,) = pallas(
            fn(pack_kernel, m),
            [shape(rows, m.wide)],
            [w_query, w_key, w_value, *vectors],
            [pltpu.VMEM((VECS, rows), F32)],
            name="pack",
            mib=60,
        )
        first_parts = direct(first)
        (up_out,) = pallas(
            fn(pack_up_kernel, m), [shape(m.up_rows, D)], [gate(w_up, first), w_out, out_far], name="pack_up"
        )
        halves = pallas(
            fn(split_down_kernel, m),
            [shape(WH // 2, S * m.hrows)] * 2,
            [gate(w_down.T, first)],
            here=True,
            name="split_down",
        )
        (down,) = pallas(
            fn(join_down_kernel, m),
            [shape(rows, m.FD)],
            [exchange(halves[k], k) for k in range(2)],
            here=True,
            name="join_down",
        )
        token_blocks = gather_seq(gate(tokens, first))
        cot_blocks = gather_seq(gate(cotangent, token_blocks[2]))
        up_same = around(up_out)
        up_side = x_swap(up_out)
        down_same = around(down)
        down_side = x_swap(down)
        norm_after = [up_out]
        held = []
    else:
        token_blocks = gather_seq(tokens)
        cot_blocks = gather_seq(cotangent)
        held = norm_after = []
        pad = jnp.zeros((rows, m.wide - 3 * WH - VECS), LOW)
        vec_rows = jnp.concatenate(vectors + [jnp.zeros(((VECS - 8 - S) * rows,), LOW)]).reshape(VECS, rows)
        first = jnp.concatenate([w_query, w_key, w_value, vec_rows.T, pad], axis=1)
        first_parts = [lax.all_gather(first, "dp", axis=0, tiled=True)]
        up_all = lax.all_gather(w_up, "dp", axis=0, tiled=True)
        down_all = lax.all_gather(w_down, "dp", axis=0, tiled=True)
        down_parts = [lax.all_to_all(down_all, "seq", 0, 1, tiled=True).T]
        heads = lax.all_gather(lax.all_gather(w_out, "seq", axis=1, tiled=True), "dp", axis=0, tiled=True)
        heads = heads.reshape(S, WH, D)
        out_all = jnp.concatenate([lax.dynamic_index_in_dim(heads, me ^ e, keepdims=False) for e in range(S)])

    (xhat,) = pallas(
        fn(norm_kernel, m),
        [shape(m.RA, D, dtype=F32)],
        [gate(token_blocks[0], *norm_after), *token_blocks[1:]],
        [pltpu.VMEM((m.IT, D), F32)],
        name="norm",
        long=False,
    )
    qkv, normed, probs, packed, vecs, w_first = pallas(
        fn(attend_kernel, m, len(first_parts)),
        [
            shape(m.RA, 3 * WH),
            shape(m.RA, D),
            shape(m.B * m.H, m.IT, m.IT),
            shape(m.B * m.IT // 2, 2 * WH),
            shape(VECS, D, dtype=F32),
            shape(D, m.wide),
        ],
        [text_mask, patch_count, gate(xhat, *held), *first_parts],
        long=False,
        smem=2,
        here=True,
        name="attend",
    )
    packed_blocks = gather_seq(packed)
    if m.fast:
        up_parts = up_same + [up_side] + [x_swap(v) for v in up_same[1:]]
        down_parts = down_same + [down_side] + [x_swap(v) for v in down_same[1:]]

    if m.fast:
        up_all, half = pallas(
            fn(assemble_kernel, m, len(up_parts)),
            [shape(D, m.FD), shape(D, 2 * WH)],
            [*up_parts],
            here=True,
            name="assemble",
        )
        out_all, cot = pallas(
            fn(join_kernel, m),
            [shape(D, D), shape(m.RA, D)],
            [half, seq_to(half, 1), *cot_blocks],
            here=True,
            name="join",
        )
    else:

        def only_pad(*refs):
            pad_cot(m, refs[:S], refs[S])

        (cot,) = pallas(only_pad, [shape(m.RA, D)], cot_blocks, name="pad_cot")

    normed2, active, slope, mixed, resid, xhat2, rstd2 = pallas(
        fn(forward_kernel, m),
        [
            shape(m.RA, D),
            shape(m.RA, m.FD),
            shape(m.RA, m.FD, dtype=F32),
            shape(m.RA, D),
            shape(m.OWN, D, dtype=F32),
            shape(m.OWN, D, dtype=F32),
            shape(m.OWN, 128, dtype=F32),
        ],
        [*token_blocks, *packed_blocks, out_all, up_all, vecs],
        [pltpu.VMEM((m.IT, D), F32)],
        here=True,
        name="forward",
    )
    def shards(width, height=D):
        if m.fast:
            return [shape(nz, rows, width)] * 2
        return [shape(height, width), shape(8, 128)]

    def weight_grad(left, right, name):
        return pallas(
            fn(weight_grad_kernel, m),
            shards(D),
            [left, right],
            [pltpu.VMEM((D, D), F32)],
            here=True,
            name=name,
            long=name == "up_grad",
        )

    down_keep, down_send = weight_grad(cot, active, "down_grad")
    g_hidden, down_all, keep0, keep1, send = pallas(
        fn(hidden_back_kernel, m, len(down_parts)),
        [shape(m.RA, m.FD), shape(D, m.FD), shape(m.OWN, D), shape(m.OWN, D), shape(2, m.OWN, D)],
        [cot, gate(slope, down_keep), up_all, *down_parts],
        here=True,
        name="hidden_back",
    )

    def add_pair(keep, core):
        (out,) = pallas(fn(pair_kernel, m), [shape(*keep.shape)], [keep, core], name="pair")
        return out

    def add(left, right):
        (out,) = pallas(fn(add_kernel, m), [shape(*left.shape, dtype=F32)], [left, right], name="add")
        return out

    core2 = seq_to(send, 1)
    pair2 = add_pair(keep1, core2)
    far2 = seq_to(pair2, 2)

    up_keep, up_send = weight_grad(normed2, gate(g_hidden, pair2), "up_grad")
    b_keep0, b_keep1, b_send, vec_ff = pallas(
        fn(branch_kernel, m),
        [shape(m.OWN, D), shape(m.OWN, D), shape(2, m.OWN, D), shape(8, D, dtype=F32)],
        [gate(active, up_keep), down_all, g_hidden, cot],
        name="branch",
        long=True,
    )

    g_resid, *blocks, vec_mid = pallas(
        fn(middle_kernel, m),
        [shape(m.OWN, D, dtype=F32), *[shape(m.OWN, 2 * WH)] * S, shape(8, D, dtype=F32)],
        [gate(keep0, b_keep0), core2, far2, xhat2, rstd2, cot, out_all, vecs],
        [pltpu.VMEM((m.OWN, D), LOW)],
        here=True,
        name="middle",
    )
    blocks = [blocks[0]] + [seq_to(blocks[e], e) for e in range(1, S)]

    def sum_x(keep, got, width):
        return pallas(
            fn(sum_x_kernel, m),
            [shape(rows, width, dtype=F32)] + [shape(rows, width)] * (nz - 1),
            [keep, got],
            name="sum_x",
        )

    def to_z(parts):
        return [z_shift(part, k + 1) for k, part in enumerate(parts)]

    def scatter(full):
        return lax.psum_scatter(full, "dp", scatter_dimension=0, tiled=True).astype(F32)

    if m.fast:
        down_got, up_got = x_swap(down_send), x_swap(up_send)
        down_own, *down_sums = sum_x(gate(down_keep, blocks[0]), down_got, D)
        down_z = to_z(down_sums)
        blocks[0] = gate(blocks[0], down_own)
    g_value, g_mixed, vo_keep, vo_send = pallas(
        fn(value_back_kernel, m),
        [shape(m.RA, WH), shape(m.RA, WH), *shards(2 * WH)],
        [probs, *blocks, normed, mixed],
        [pltpu.VMEM((m.RA, WH), LOW), pltpu.VMEM((D, 2 * WH), F32)],
        here=True,
        name="value_back",
        long=True,
    )
    if m.fast:
        vo_got = x_swap(vo_send)
        up_own, *up_sums = sum_x(gate(up_keep, g_value), up_got, D)
        up_z = to_z(up_sums)
        g_mixed = gate(g_mixed, up_own)

        def sum_down(after):
            return pallas(
                fn(sum_down_kernel, m),
                [shape(rows, m.FD // 2)] * 2,
                [gate(down_own, after), *down_z],
                here=True,
                name="sum_down",
            )

    (g_qk,) = pallas(
        fn(attend_back_kernel, m),
        [shape(m.RA, 2 * WH)],
        [qkv, probs, g_mixed],
        name="attend_back",
        long=True,
    )
    g_last = g_qk
    if m.fast:
        halves = sum_down(g_qk)
        down_halves = [exchange(halves[k], k) for k in range(2)]
        g_last = gate(g_qk, halves[0])
    qk_keep, qk_send = pallas(
        fn(weight_grad_kernel, m),
        shards(2 * WH),
        [normed, g_last],
        [pltpu.VMEM((D, 2 * WH), F32)],
        here=True,
        name="qk_grad",
    )
    keep0, keep1, send, vec = pallas(
        fn(input_back_kernel, m),
        [shape(m.OWN, D), shape(2 * m.OWN, D), shape(2, 2 * m.OWN, D), shape(VECS, D, dtype=F32)],
        [gate(g_qk, qk_keep), g_value, xhat, w_first, vec_mid, vec_ff, b_keep1, b_send],
        here=True,
        name="input_back",
    )
    vec_core, core1 = seq_to(vec, 1), seq_to(send, 1)
    vec = add(vec, vec_core)
    vec_far = seq_to(vec, 2)
    if m.fast:
        vo_own, *vo_sums = sum_x(gate(vo_keep, vec), vo_got, 2 * WH)
        vo_z = to_z(vo_sums)
        keep1 = gate(keep1, vo_own)
    pair1 = add_pair(gate(keep1, vec), core1)
    far1 = seq_to(pair1, 2)
    if m.fast:
        qk_got = x_swap(qk_send)
        (g_up,) = pallas(
            fn(sum_up_kernel, m), [shape(rows, m.FD, dtype=F32)], [gate(up_own, pair1), *up_z], name="sum_up"
        )
        vec = add(gate(vec, g_up), vec_far)
        vec_got = x_swap(vec)
        qk_own, vec_own, *qk_sums = pallas(
            fn(last_x_kernel, m),
            [shape(rows, 2 * WH, dtype=F32), shape(2 * VECS, D // 2, dtype=F32)]
            + [shape(rows + 2 * VECS, 2 * WH)] * (nz - 1),
            [qk_keep, qk_got, vec, vec_got],
            name="last_x",
        )
        qk_z = to_z(qk_sums)
        keep0 = gate(keep0, qk_own)
    else:
        vec = lax.psum(vec + vec_far, "dp")
        vec = lax.dynamic_slice(vec, (0, dp * rows), (VECS, rows))
        g_vo, g_qk = scatter(vo_keep), scatter(qk_keep)
        g_value, g_out, g_query, g_key = g_vo[:, :WH], g_vo[:, WH:], g_qk[:, :WH], g_qk[:, WH:]
        g_up = scatter(up_keep)
        g_down = scatter(lax.all_to_all(down_keep.T, "seq", 1, 0, tiled=True))
        vec_outs = [vec[k] for k in range(8)] + [vec[8 : 8 + S].reshape(-1)]

    result, input_grad = pallas(
        fn(finish_kernel, m),
        [shape(m.B, m.R, D), shape(m.B, m.R, D)],
        [keep0, core1, far1, tokens, g_resid, vecs, b_keep0, resid],
        name="finish",
    )
    if m.fast:
        g_value, g_out = pallas(
            fn(sum_z_kernel, m),
            [shape(rows, WH, dtype=F32)] * 2,
            [gate(vo_own, result), *vo_z],
            name="value_out",
        )
        (g_down,) = pallas(
            fn(give_down_kernel, m),
            [shape(WH, S * m.hrows, dtype=F32)],
            [gate(down_halves[0], g_value), down_halves[1]],
            here=True,
            name="give_down",
        )
        g_down = g_down.T
        g_query, g_key, *vec_outs = pallas(
            fn(last_z_kernel, m),
            [shape(rows, WH, dtype=F32)] * 2 + [shape(rows, dtype=F32)] * 8 + [shape(S * m.hrows, dtype=F32)],
            [gate(qk_own, g_down), vec_own, *qk_z],
            [pltpu.VMEM((VECS, rows), F32)],
            here=True,
            name="query_key",
        )
    return (
        result,
        input_grad,
        g_query,
        g_key,
        g_value,
        g_out,
        g_up,
        g_down,
        *vec_outs[:7],
        vec_outs[8],
        vec_outs[7],
    )


def solution(mesh):
    rows3, mat, vec = P("dp", "seq", None), P("dp", "seq"), P("dp")
    return jax.shard_map(
        functools.partial(local, mesh),
        mesh=mesh,
        in_specs=(rows3, rows3, P("dp", None), vec) + (mat,) * 6 + (vec,) * 9,
        out_specs=(rows3, rows3) + (mat,) * 6 + (vec,) * 9,
        check_vma=False,
    )
```

```python
import functools
from types import SimpleNamespace

import jax
import jax.numpy as jnp
from jax import lax
from jax.experimental import pallas as pl
from jax.experimental.pallas import tpu as pltpu
from jax.sharding import PartitionSpec as P

HEADS = 12
COST = {'up_grad': 10000000000, 'branch': 10000000000, 'value_back': 10000000000, 'attend_back': 10000000000, 'finish': 10000000000, 'pack': 3000000000, 'sum_down': 1000, 'sum_up': 1000, 'last_x': 30000000000, 'hidden_back': 3000000000, 'qk_grad': 1000000000}
CFG = {'pair': 1, 'add': 1, 'za': 'direct', 'zu': 'bidir', 'zd': 'bidir', 'xu': 0, 'xd': 0, 'norm': 3, 'held': 0, 'split': 3, 'cot': 1, 'tok': 1, 'ord': 1, 'up': 0, 'vo': 0, 'br': 1, 'both': 0, 'og': 3, 'sa': 'each', 'su': 'each', 'sd': 'rest', 'gd': 2}
EPS = 1e-05
LOW = jnp.bfloat16
F32 = jnp.float32
VECS = 16
UP_BIAS = 12
SQRT_HALF = 0.7071067811865476
PDF_SCALE = 0.3989422804014327


def dot(left, right):
    return jnp.dot(left, right, preferred_element_type=F32)


def dot_t(left, right):
    return lax.dot_general(left, right, (((1,), (1,)), ((), ())), preferred_element_type=F32)


def t_dot(left, right):
    return lax.dot_general(left, right, (((0,), (0,)), ((), ())), preferred_element_type=F32)


def col_sum(values):
    return jnp.sum(values, axis=0, keepdims=True)


def ds(start, size, align=16):
    if not isinstance(start, int):
        start = pl.multiple_of(start, align)
    return pl.ds(start, size)


def pallas(body, outs, ins, scratch=(), smem=0, here=False, name=None, mib=8):
    flops = COST.get(name, 1000)
    nbytes = sum(a.size * a.dtype.itemsize for a in ins)
    nbytes += sum(s.size * jnp.dtype(s.dtype).itemsize for s in outs)
    near = pl.BlockSpec(memory_space=pltpu.VMEM)

    def run(*refs):
        if here:
            dp = lax.axis_index("dp")
            body((lax.axis_index("seq"), lax.div(dp, 2), lax.rem(dp, 2)), *refs)
        else:
            body(*refs)

    return pl.pallas_call(
        run,
        out_shape=outs,
        in_specs=[pl.BlockSpec(memory_space=pltpu.SMEM)] * smem + [near] * (len(ins) - smem),
        out_specs=[near] * len(outs),
        scratch_shapes=list(scratch),
        compiler_params=pltpu.CompilerParams(vmem_limit_bytes=mib * 2**20),
        cost_estimate=pl.CostEstimate(flops=flops, bytes_accessed=nbytes, transcendentals=0),
        name=name,
    )(*ins)


def shape(*dims, dtype=LOW):
    return jax.ShapeDtypeStruct(dims, dtype)


def part_index(m, sc, part):
    z, x = sc[1], sc[2]
    k = part % m.nz
    side = x if part < m.nz else 1 - x
    return lax.rem(z - k + m.nz, m.nz) * 2 + side


def spread(parts):
    out = []
    for part in parts:
        out += [part.at[k] for k in range(part.shape[0])] if len(part.shape) == 3 else [part]
    return out


def layer_norm(x):
    center = x - jnp.mean(x, axis=-1, keepdims=True)
    rstd = lax.rsqrt(jnp.mean(center * center, axis=-1, keepdims=True) + EPS)
    return center * rstd, rstd


def norm_back(grad, gain, xhat, rstd):
    scaled = grad * gain
    first = jnp.mean(scaled, axis=-1, keepdims=True)
    second = jnp.mean(scaled * xhat, axis=-1, keepdims=True)
    return rstd * (scaled - first - xhat * second)


def pack_kernel(m, query, key, value, *refs):
    vecs, first, rows = refs[:9], refs[9], refs[10]
    first[:, : m.WH] = query[...]
    first[:, m.WH : 2 * m.WH] = key[...]
    first[:, 2 * m.WH : 3 * m.WH] = value[...]
    first[:, 3 * m.WH :] = jnp.zeros((m.rows, m.wide - 3 * m.WH), LOW)
    rows[...] = jnp.zeros_like(rows)
    for k in range(8):
        rows[k : k + 1, :] = vecs[k][...].astype(F32).reshape(1, m.rows)
    up_bias = vecs[8][...].astype(F32).reshape(1, m.S * m.hrows)
    for c in range(m.S):
        rows[8 + c : 9 + c, :] = up_bias[:, c * m.hrows : (c + 1) * m.hrows]
    first[:, 3 * m.WH : 3 * m.WH + VECS] = rows[...].T.astype(LOW)


def pack_up_kernel(m, up, out, far, packed):
    half = m.rows // 2
    packed[: m.rows, :] = up[...]
    for side in range(2):
        at = slice(side * half, (side + 1) * half)
        packed[m.rows :, 2 * side * m.WH : (2 * side + 1) * m.WH] = out[at, :]
        packed[m.rows :, (2 * side + 1) * m.WH : (2 * side + 2) * m.WH] = far[at, :]


def split_down_kernel(m, sc, down_t, first, second):
    half = m.WH // 2
    for x in range(2):

        @pl.when(sc[2] == x)
        def _(x=x):
            first[...] = down_t[x * half : (x + 1) * half, :]
            second[...] = down_t[(1 - x) * half : (2 - x) * half, :]


def join_down_kernel(m, sc, first, second, down):
    width = m.FD // 2
    for x in range(2):

        @pl.when(sc[2] == x)
        def _(x=x):
            down[:, x * width : (x + 1) * width] = first[...]
            down[:, (1 - x) * width : (2 - x) * width] = second[...]


def stack_kernel(m, *refs):
    for k, ref in enumerate(refs[:-1]):
        refs[-1][k] = ref[...]


def norm_kernel(m, *refs):
    tokens, (xhat, x_scr) = refs[: m.S], refs[m.S :]
    x_scr[...] = jnp.zeros_like(x_scr)

    def item(b, carry):
        for d in range(m.S):
            x_scr[d * m.RP : d * m.RP + m.R, :] = tokens[d][b].astype(F32)
        xhat[ds(b * m.IT, m.IT), :], _ = layer_norm(x_scr[...])
        return carry

    lax.fori_loop(0, m.B, item, 0)


def attend_kernel(m, nparts, *refs):
    sc, text_mask, patch_count, xhat_ref = refs[:4]
    parts = refs[4 : 4 + nparts]
    qkv, normed, probs, packed, vecs, w_ref = refs[4 + nparts :]
    me = sc[0]
    if nparts == 1:
        w_ref[...] = parts[0][...]
    else:
        for p, part in enumerate(spread(parts)):
            w_ref[ds(part_index(m, sc, p) * m.rows, m.rows), :] = part[...]
    base = (3 * m.WH) // 128 * 128
    turned = w_ref[:, base : base + 128].astype(F32).T
    vecs[...] = turned[3 * m.WH - base : 3 * m.WH - base + VECS]
    for c in range(m.S):

        @pl.when(me == c)
        def _(c=c):
            for t in range(m.N // m.S):
                for k in range(m.S):
                    lanes = slice((t * m.S + k) * m.hrows, (t * m.S + k + 1) * m.hrows)
                    begin = c * m.WH + t * m.rows
                    vecs[UP_BIAS : UP_BIAS + 1, lanes] = vecs[8 + k : 9 + k, begin : begin + m.rows]

    gain, shift = vecs[0:1, :], vecs[1:2, :]
    q_bias = jnp.zeros((1, m.WH), F32)
    v_bias = jnp.zeros((1, m.WH), F32)
    for c in range(m.S):
        here = me == c
        q_bias = jnp.where(here, vecs[2:3, c * m.WH : (c + 1) * m.WH], q_bias)
        v_bias = jnp.where(here, vecs[3:4, c * m.WH : (c + 1) * m.WH], v_bias)
    bias = jnp.concatenate([q_bias, jnp.zeros((1, m.WH), F32), v_bias], axis=1)

    lane = lax.broadcasted_iota(jnp.int32, (1, m.IT), 1)
    place = jnp.full((1, m.IT), 1 << 20, jnp.int32)
    for d in range(m.S):
        row = lane - d * m.RP
        here = jnp.where(row < m.R, (me ^ d) * m.R + row, 1 << 20)
        place = jnp.where(row < 0, place, here)

    def item(b, carry):
        at = ds(b * m.IT, m.IT)
        low = (xhat_ref[at, :] * gain + shift).astype(LOW)
        normed[at, :] = low
        qkv[at, :] = (dot(low, w_ref[:, : 3 * m.WH]) + bias).astype(LOW)
        words = text_mask[b, 0]
        for k in range(1, m.TXT):
            words = words + text_mask[b, k]
        masked = jnp.where(
            place < m.TXT,
            jnp.where(place < words, 0.0, -1e30),
            jnp.where(place - m.TXT < patch_count[b], 0.0, -1e30),
        )
        half = m.IT // 2
        for h in range(m.H):
            q = qkv[at, h * m.hd : (h + 1) * m.hd] * LOW(m.hd**-0.5)
            k = qkv[at, m.WH + h * m.hd : m.WH + (h + 1) * m.hd]
            v = qkv[at, 2 * m.WH + h * m.hd : 2 * m.WH + (h + 1) * m.hd]
            s = dot_t(q, k) + masked
            e = jnp.exp(s - jnp.max(s, axis=-1, keepdims=True))
            p = (e * (1.0 / jnp.sum(e, axis=-1, keepdims=True))).astype(LOW)
            probs[b * m.H + h] = p
            o = dot(p, v).astype(LOW)
            packed[ds(b * half, half), h * m.hd : (h + 1) * m.hd] = o[:half]
            packed[ds(b * half, half), m.WH + h * m.hd : m.WH + (h + 1) * m.hd] = o[half:]
        return carry

    lax.fori_loop(0, m.B, item, 0)


def assemble_kernel(m, nparts, *refs):
    sc = refs[0]
    parts = refs[1 : 1 + nparts]
    w_up, w_out = refs[1 + nparts :]
    half = m.rows // 2
    per = m.N // m.S
    for p, part in enumerate(spread(parts)):
        i = part_index(m, sc, p)
        w_up[ds(i * m.rows, m.rows), :] = part[: m.rows]
        start = (sc[0] ^ lax.div(i, per)) * m.WH + lax.rem(i, per) * m.rows
        w_out[ds(start, half), :] = part[m.rows :, : 2 * m.WH]
        w_out[ds(start + half, half), :] = part[m.rows :, 2 * m.WH :]


def join_kernel(m, sc, own, other, *refs):
    cots = refs[: m.S]
    w_out, cot = refs[m.S :]
    for c in range(m.S):

        @pl.when(sc[0] == c)
        def _(c=c):
            for d in range(m.S):
                half = (own, other)[d % 2]
                lanes = slice((c ^ d) * m.WH, ((c ^ d) + 1) * m.WH)
                for e in range(m.S):
                    rows = slice((e ^ (d % 2)) * m.WH, ((e ^ (d % 2)) + 1) * m.WH)
                    w_out[e * m.WH : (e + 1) * m.WH, lanes] = half[rows, d // 2 * m.WH : (d // 2 + 1) * m.WH]

    pad_cot(m, cots, cot)


def pad_cot(m, cots, cot):
    cot[...] = jnp.zeros_like(cot)
    for b in range(m.B):
        for d in range(m.S):
            start = (b * m.S + d) * m.RP
            cot[start : start + m.R, :] = cots[d][b]


def forward_kernel(m, *refs):
    sc = refs[0]
    tokens = refs[1 : 1 + m.S]
    packed = refs[1 + m.S : 1 + 2 * m.S]
    w_out, w_up, vecs = refs[1 + 2 * m.S : 4 + 2 * m.S]
    normed, active, slope, mixed, resid_own, xhat_own, rstd_own, x_scr = refs[4 + 2 * m.S :]
    me = sc[0]
    out_bias, gain, shift = vecs[4:5, :], vecs[5:6, :], vecs[6:7, :]
    up_bias = vecs[UP_BIAS : UP_BIAS + 1, :]
    x_scr[...] = jnp.zeros_like(x_scr)

    def item(b, carry):
        at = ds(b * m.IT, m.IT)
        half = m.IT // 2
        for d in range(m.S):
            x_scr[d * m.RP : d * m.RP + m.R, :] = tokens[d][b].astype(F32)
        for e in range(m.S):
            for side in range(2):
                piece = packed[e][ds(b * half, half), side * m.WH : (side + 1) * m.WH]
                for t in range(2):
                    d = (2 * side + t) ^ e
                    mixed[ds(b * m.IT + d * m.RP, m.RP), e * m.WH : (e + 1) * m.WH] = piece[
                        t * m.RP : (t + 1) * m.RP
                    ]
        resid = x_scr[...] + (dot(mixed[at, :], w_out[...]) + out_bias)
        xhat, rstd = layer_norm(resid)
        own = ds(b * m.RP, m.RP)
        resid_own[own, :] = resid[: m.RP]
        xhat_own[own, :] = xhat[: m.RP]
        rstd_own[own, :] = jnp.broadcast_to(rstd[: m.RP], (m.RP, 128))
        low = (xhat * gain + shift).astype(LOW)
        normed[at, :] = low
        hidden = dot(low, w_up[...]) + up_bias
        cdf = 0.5 + 0.5 * lax.erf(hidden * SQRT_HALF)
        active[at, :] = (hidden * cdf).astype(LOW)
        slope[at, :] = cdf + hidden * (PDF_SCALE * jnp.exp(-0.5 * hidden * hidden))
        return carry

    lax.fori_loop(0, m.B, item, 0)


def hidden_back_kernel(m, nparts, *refs):
    sc, cot, slope, w_up = refs[:4]
    parts = refs[4 : 4 + nparts]
    g_hidden, w_down, keep0, keep1, send = refs[4 + nparts :]
    if nparts == 1:
        w_down[...] = parts[0][...]
    else:
        for p, part in enumerate(spread(parts)):
            w_down[ds(part_index(m, sc, p) * m.rows, m.rows), :] = part[...]

    def item(b, carry):
        at = ds(b * m.IT, m.IT)
        back = (dot(cot[at, :], w_down[...]) * slope[at, :]).astype(LOW)
        g_hidden[at, :] = back
        give_rows(m, b, dot_t(back, w_up[...]).astype(LOW), keep0, keep1, send)
        return carry

    lax.fori_loop(0, m.B, item, 0)


def give_shards(m, sc, total, keep, send):
    for k in range(m.nz):
        z = lax.rem(sc[1] + k, m.nz)
        keep[k] = total[ds((2 * z + sc[2]) * m.rows, m.rows), :].astype(LOW)
        send[k] = total[ds((2 * z + 1 - sc[2]) * m.rows, m.rows), :].astype(LOW)


def give(m, sc, total, keep, send):
    if m.fast:
        give_shards(m, sc, total, keep, send)
    else:
        keep[...] = total[...].astype(LOW)
        send[...] = jnp.zeros_like(send)


def give_rows(m, b, values, keep0, keep1, send):
    own = ds(b * m.RP, m.RP)
    keep0[own, :] = values[: m.RP]
    send[0, own, :] = values[m.RP : 2 * m.RP]
    keep1[own, :] = values[2 * m.RP : 3 * m.RP]
    send[1, own, :] = values[3 * m.RP : 4 * m.RP]


def weight_grad_kernel(m, sc, left, right, keep, send, total):
    step = 256
    for begin in range(0, m.D, step):
        total[begin : begin + step, :] = t_dot(left[:, begin : begin + step], right[...])
    give(m, sc, total, keep, send)


def branch_kernel(m, active, w_down, g_hidden, cot, keep0, keep1, send, vec):
    vec[...] = jnp.zeros_like(vec)

    def item(b, carry):
        at = ds(b * m.IT, m.IT)
        give_rows(m, b, dot_t(active[at, :], w_down[...]).astype(LOW), keep0, keep1, send)
        vec[0:1, :] += col_sum(cot[ds(b * m.IT, m.RP), :].astype(F32))
        vec[1:2, :] += col_sum(g_hidden[at, :].astype(F32))
        return carry

    lax.fori_loop(0, m.B, item, 0)


def pair_kernel(m, keep, core, out):
    out[...] = (keep[...].astype(F32) + core[1].astype(F32)).astype(LOW)


def add_kernel(m, left, right, out):
    out[...] = left[...] + right[...]


def middle_kernel(m, *refs):
    sc, keep0, core, far, xhat_own, rstd_own, cot, w_out, vecs = refs[:9]
    g_resid = refs[9]
    blocks = refs[10 : 10 + m.S]
    vec, low_scr = refs[10 + m.S :]
    me = sc[0]
    gain = vecs[5:6, :]
    grad = keep0[...].astype(F32) + core[0].astype(F32) + far[...].astype(F32)
    xhat = xhat_own[...]
    back = norm_back(grad, gain, xhat, rstd_own[:, 0:1])
    vec[...] = jnp.zeros_like(vec)
    vec[0:1, :] = col_sum(grad * xhat)
    vec[1:2, :] = col_sum(grad)
    for b in range(m.B):
        own = slice(b * m.RP, (b + 1) * m.RP)
        full = back[own] + cot[b * m.IT : b * m.IT + m.RP, :].astype(F32)
        g_resid[own, :] = full
        low_scr[own, :] = full.astype(LOW)
    low = low_scr[...]
    vec[2:3, :] = col_sum(low.astype(F32))
    g_mixed = dot_t(low, w_out[...]).astype(LOW)
    for e in range(m.S):
        blocks[e][:, : m.WH] = g_mixed[:, e * m.WH : (e + 1) * m.WH]
        picked = low[:, : m.WH]
        for c in range(1, m.S):
            picked = jnp.where((me ^ e) == c, low[:, c * m.WH : (c + 1) * m.WH], picked)
        blocks[e][:, m.WH :] = picked


def value_back_kernel(m, *refs):
    sc, probs = refs[:2]
    blocks = refs[2 : 2 + m.S]
    normed, mixed = refs[2 + m.S : 4 + m.S]
    g_value, g_mixed, keep, send, ga_scr, total = refs[4 + m.S :]

    def item(b, carry):
        at = ds(b * m.IT, m.IT)
        own = ds(b * m.RP, m.RP)
        for d in range(m.S):
            ga_scr[ds(b * m.IT + d * m.RP, m.RP), :] = blocks[d][own, m.WH :]
            g_mixed[ds(b * m.IT + d * m.RP, m.RP), :] = blocks[d][own, : m.WH]
        for h in range(m.H):
            lanes = slice(h * m.hd, (h + 1) * m.hd)
            g_value[at, lanes] = t_dot(probs[b * m.H + h], g_mixed[at, lanes]).astype(LOW)
        return carry

    lax.fori_loop(0, m.B, item, 0)
    total[:, : m.WH] = t_dot(normed[...], g_value[...])
    g_out = t_dot(mixed[...], ga_scr[...])
    for e in range(m.S):
        total[ds((sc[0] ^ e) * m.WH, m.WH), m.WH :] = g_out[e * m.WH : (e + 1) * m.WH]
    give(m, sc, total, keep, send)


def attend_back_kernel(m, qkv, probs, g_mixed, g_qk):
    scale = m.hd**-0.5

    def item(b, carry):
        at = ds(b * m.IT, m.IT)
        for h in range(m.H):
            lanes = slice(h * m.hd, (h + 1) * m.hd)
            q = qkv[at, h * m.hd : (h + 1) * m.hd]
            k = qkv[at, m.WH + h * m.hd : m.WH + (h + 1) * m.hd]
            v = qkv[at, 2 * m.WH + h * m.hd : 2 * m.WH + (h + 1) * m.hd]
            p = probs[b * m.H + h].astype(F32)
            gp = dot_t(g_mixed[at, lanes], v)
            gs = (p * (gp - jnp.sum(p * gp, axis=-1, keepdims=True))).astype(LOW)
            g_qk[at, h * m.hd : (h + 1) * m.hd] = (dot(gs, k) * scale).astype(LOW)
            g_qk[at, m.WH + h * m.hd : m.WH + (h + 1) * m.hd] = (t_dot(gs, q) * scale).astype(LOW)
        return carry

    lax.fori_loop(0, m.B, item, 0)


def input_back_kernel(m, sc, g_qk, g_value, xhat, w, vec_mid, vec_ff, b_keep1, b_send, keep0, keep1, send, v_scr):
    me = sc[0]
    v_scr[...] = jnp.zeros_like(v_scr)

    def item(b, carry):
        at = ds(b * m.IT, m.IT)
        grad = dot_t(g_qk[at, :], w[:, : 2 * m.WH]) + dot_t(g_value[at, :], w[:, 2 * m.WH : 3 * m.WH])
        v_scr[0:1, :] += col_sum(grad * xhat[at, :])
        v_scr[1:2, :] += col_sum(grad)
        give_rows(m, b, grad.astype(LOW), keep0, keep1, send)
        return carry

    lax.fori_loop(0, m.B, item, 0)
    q_sum = col_sum(g_qk[:, : m.WH].astype(F32))
    v_sum = col_sum(g_value[...].astype(F32))
    for c in range(m.S):
        here = me == c
        lanes = slice(c * m.WH, (c + 1) * m.WH)
        v_scr[2:3, lanes] = jnp.where(here, q_sum, 0.0)
        v_scr[3:4, lanes] = jnp.where(here, v_sum, 0.0)
        for t in range(m.N // m.S):
            for k in range(m.S):
                begin = c * m.WH + t * m.rows
                part = vec_ff[1:2, (t * m.S + k) * m.hrows : (t * m.S + k + 1) * m.hrows]
                v_scr[8 + k : 9 + k, begin : begin + m.rows] = jnp.where(here, part, 0.0)
    v_scr[4:5, :] = vec_mid[2:3, :]
    v_scr[5:6, :] = vec_mid[0:1, :]
    v_scr[6:7, :] = vec_mid[1:2, :]
    v_scr[7:8, :] = vec_ff[0:1, :]
    keep1[m.OWN :, :] = b_keep1[...]
    send[0, m.OWN :, :] = b_send[0]
    send[1, m.OWN :, :] = b_send[1]


def sum_x_kernel(m, keep, got, own, *outs):
    own[...] = keep[0].astype(F32) + got[0].astype(F32)
    for k, out in enumerate(outs):
        out[...] = (keep[k + 1].astype(F32) + got[k + 1].astype(F32)).astype(LOW)


def both_x_kernel(m, up_keep, up_got, vo_keep, vo_got, up_own, vo_own, *outs):
    half = m.rows // 2
    up_own[...] = up_keep[0].astype(F32) + up_got[0].astype(F32)
    vo_own[...] = vo_keep[0].astype(F32) + vo_got[0].astype(F32)
    for k, out in enumerate(outs):
        out[: m.rows, :] = (up_keep[k + 1].astype(F32) + up_got[k + 1].astype(F32)).astype(LOW)
        total = (vo_keep[k + 1].astype(F32) + vo_got[k + 1].astype(F32)).astype(LOW)
        out[m.rows :, : 2 * m.WH] = total[:half]
        out[m.rows :, 2 * m.WH :] = total[half:]


def both_z_kernel(m, up_own, vo_own, *refs):
    rest, (g_up, first, second) = refs[: m.nz - 1], refs[m.nz - 1 :]
    half = m.rows // 2
    total = up_own[...]
    for r in rest:
        total = total + r[: m.rows, :].astype(F32)
    g_up[...] = total
    for side in range(2):
        at = slice(side * half, (side + 1) * half)
        total = vo_own[at, :]
        for r in rest:
            total = total + r[m.rows :, 2 * m.WH * side : 2 * m.WH * (side + 1)].astype(F32)
        first[at, :] = total[:, : m.WH]
        second[at, :] = total[:, m.WH :]


def last_x_kernel(m, keep, got, vec, vec_got, own, vec_own, *outs):
    own[...] = keep[0].astype(F32) + got[0].astype(F32)
    values = vec[...] + vec_got[...]
    half = m.D // 2
    vec_own[:VECS, :] = values[:, :half]
    vec_own[VECS:, :] = values[:, half:]
    for k, out in enumerate(outs):
        out[: m.rows, :] = (keep[k + 1].astype(F32) + got[k + 1].astype(F32)).astype(LOW)
        out[m.rows :, :] = vec_own[...].astype(LOW)


def sum_z_kernel(m, *refs):
    own, rest, outs = refs[0], refs[1 : m.nz], refs[m.nz :]
    total = own[...]
    for r in rest:
        total = total + r[...].astype(F32)
    outs[0][...] = total[:, : m.WH]
    outs[1][...] = total[:, m.WH :]


def last_z_kernel(m, sc, own, vec_own, *refs):
    rest, (first, second), vecs, picked = refs[: m.nz - 1], refs[m.nz - 1 : m.nz + 1], refs[m.nz + 1 : -1], refs[-1]
    total, values = own[...], vec_own[...]
    for r in rest:
        total = total + r[: m.rows, :].astype(F32)
        values = values + r[m.rows :, :].astype(F32)
    first[...] = total[:, : m.WH]
    second[...] = total[:, m.WH :]
    for i in range(m.N):

        @pl.when(2 * sc[1] + sc[2] == i)
        def _(i=i):
            side, lane = divmod(i * m.rows, m.D // 2)
            picked[...] = values[side * VECS : (side + 1) * VECS, lane : lane + m.rows]

    for k in range(8):
        vecs[k][...] = picked[k : k + 1, :].reshape(m.rows)
    vecs[8][...] = jnp.concatenate([picked[8 + c : 9 + c, :] for c in range(m.S)], axis=1).reshape(m.S * m.rows)


def sum_down_kernel(m, sc, own, *refs):
    rest, (first, second) = refs[:-2], refs[-2:]
    total = own[...]
    for r in rest:
        total = total + r[...].astype(F32)
    width = m.FD // 2
    for x in range(2):

        @pl.when(sc[2] == x)
        def _(x=x):
            first[...] = total[:, x * width : (x + 1) * width].astype(LOW)
            second[...] = total[:, (1 - x) * width : (2 - x) * width].astype(LOW)


def sum_up_kernel(m, own, *refs):
    rest, out = refs[:-1], refs[-1]
    total = own[...]
    for r in rest:
        total = total + r[...].astype(F32)
    out[...] = total


def give_down_kernel(m, sc, first, second, g_down):
    for x in range(2):

        @pl.when(sc[2] == x)
        def _(x=x):
            g_down[x * m.rows : (x + 1) * m.rows, :] = first[...].astype(F32)
            g_down[(1 - x) * m.rows : (2 - x) * m.rows, :] = second[...].astype(F32)


def finish_kernel(m, *refs):
    keep0, core, far, tokens, g_resid, vecs, b_keep, resid = refs[:8]
    result, input_grad = refs[8:]
    gain, down_bias = vecs[0:1, :], vecs[7:8, :]
    for b in range(m.B):
        own = slice(b * m.RP, b * m.RP + m.R)
        also = slice(m.OWN + b * m.RP, m.OWN + b * m.RP + m.R)
        grad = keep0[own, :].astype(F32) + core[0, own, :].astype(F32) + far[own, :].astype(F32)
        xhat, rstd = layer_norm(tokens[b].astype(F32))
        back = norm_back(grad, gain, xhat, rstd)
        input_grad[b] = (g_resid[own, :] + back).astype(LOW)
        branch = b_keep[own, :].astype(F32) + core[0, also, :].astype(F32) + far[also, :].astype(F32)
        result[b] = (resid[own, :] + (branch + down_bias)).astype(LOW)


def plan(mesh, tokens, text_mask, w_query, w_up):
    m = SimpleNamespace()
    m.N, m.S = mesh.shape["dp"], mesh.shape["seq"]
    m.B, m.R, m.D = tokens.shape
    m.RP = -(-m.R // 16) * 16
    m.IT = m.S * m.RP
    m.RA = m.B * m.IT
    m.OWN = m.B * m.RP
    m.TXT = text_mask.shape[1]
    m.rows, m.WH = w_query.shape
    m.hd = m.D // HEADS
    m.H = HEADS // m.S
    m.FD = w_up.shape[1]
    m.hrows = m.FD // m.N
    m.fast = m.N == 2 * m.S
    m.nz = m.N // 2
    m.wide = -(-(3 * m.WH + VECS) // 128) * 128
    m.up_rows = m.rows + m.rows // 2
    return m


def local(
    mesh,
    tokens,
    cotangent,
    text_mask,
    patch_count,
    w_query,
    w_key,
    w_value,
    w_out,
    w_up,
    w_down,
    norm1_gain,
    norm1_bias,
    query_bias,
    value_bias,
    out_bias,
    norm2_gain,
    norm2_bias,
    up_bias,
    down_bias,
):
    m = plan(mesh, tokens, text_mask, w_query, w_up)
    N, S, rows, WH, D, nz = m.N, m.S, m.rows, m.WH, m.D, m.nz
    dp = lax.axis_index("dp").astype(jnp.int32)
    me = lax.axis_index("seq").astype(jnp.int32)
    fn = functools.partial

    def seq_to(x, e):
        return lax.ppermute(x, "seq", [(i, i ^ e) for i in range(S)])

    def x_swap(x):
        return lax.ppermute(x, "dp", [(i, i ^ 1) for i in range(N)])

    def z_shift(x, k):
        return lax.ppermute(x, "dp", [(i, (i + 2 * k) % N) for i in range(N)])

    def gate(x, *others):
        return lax.optimization_barrier((x, *others))[0]

    def direct(x):
        same = [x] + [z_shift(x, k) for k in range(1, nz)]
        return same + [x_swap(v) for v in same]

    def around(x, kind):
        if kind == "direct":
            return [x] + [z_shift(x, k) for k in range(1, nz)]
        if kind == "ring":
            out = [x]
            for _ in range(1, nz):
                out.append(z_shift(out[-1], 1))
            return out
        a, b = z_shift(x, 1), z_shift(x, nz - 1)
        return [x, a, z_shift(a, 1), b]

    def swapped(same, kind, name, after=()):
        if kind == "each":
            return [x_swap(same[0])] + [x_swap(gate(v, *after)) for v in same[1:]]
        begin = 1 if kind == "rest" else 0
        rest = [gate(same[begin], *after), *same[begin + 1 :]]
        (stacked,) = pallas(fn(stack_kernel, m), [shape(len(rest), *same[0].shape)], rest, name=name)
        return [x_swap(same[0])] * begin + [x_swap(stacked)]

    def exchange(x, k):
        pairs = []
        for i in range(N):
            for j in range(S):
                to = 2 * j + (i + k) % 2
                pairs.append((i * S + j, to * S + i // 2))
        return lax.ppermute(x, ("dp", "seq"), pairs)

    def gather_seq(x):
        far = seq_to(x, 2)
        return [x, seq_to(x, 1), far, seq_to(far, 1)]

    vectors = [norm1_gain, norm1_bias, query_bias, value_bias, out_bias, norm2_gain, norm2_bias, down_bias, up_bias]
    if m.fast:
        (first,) = pallas(
            fn(pack_kernel, m),
            [shape(rows, m.wide)],
            [w_query, w_key, w_value, *vectors],
            [pltpu.VMEM((VECS, rows), F32)],
            name="pack",
            mib=60,
        )
        first_same = around(first, CFG["za"])
        first_parts = first_same + swapped(first_same, CFG["sa"], "stack_first")
        out_far = seq_to(gate(w_out, *{0: [], 1: [first_parts[nz]], 2: [first_same[1]], 3: [first]}[CFG["og"]]), 2)
        (up_out,) = pallas(
            fn(pack_up_kernel, m), [shape(m.up_rows, D)], [gate(w_up, first), w_out, out_far], name="pack_up"
        )
        halves = pallas(
            fn(split_down_kernel, m),
            [shape(WH // 2, S * m.hrows)] * 2,
            [gate(w_down.T, *{0: [], 1: [first], 2: [up_out], 3: [first_same[1]], 4: first_same[1:]}[CFG["split"]])],
            here=True,
            name="split_down",
        )
        (down,) = pallas(
            fn(join_down_kernel, m),
            [shape(rows, m.FD)],
            [exchange(halves[k], k) for k in range(2)],
            here=True,
            name="join_down",
        )
        token_blocks = gather_seq(gate(tokens, *{0: [], 1: [first]}[CFG["tok"]]))
        cot_blocks = gather_seq(gate(cotangent, *{0: [first], 1: [token_blocks[2]], 2: [up_out]}[CFG["cot"]]))
        up_same = around(up_out, CFG["zu"])
        down_same = around(down, CFG["zd"])
        norm_after = {0: [], 1: [up_out], 2: [up_out, down], 3: [up_out, *first_same[1:]], 4: [up_out, down, *first_same[1:]]}[CFG["norm"]]
        held = {0: [], 1: [cot_blocks[2]], 2: [up_same[1]], 3: [up_same[1], up_same[-1]], 4: [down]}[CFG["held"]]
    else:
        token_blocks = gather_seq(tokens)
        cot_blocks = gather_seq(cotangent)
        held = norm_after = []
        pad = jnp.zeros((rows, m.wide - 3 * WH - VECS), LOW)
        vec_rows = jnp.concatenate(vectors + [jnp.zeros(((VECS - 8 - S) * rows,), LOW)]).reshape(VECS, rows)
        first = jnp.concatenate([w_query, w_key, w_value, vec_rows.T, pad], axis=1)
        first_parts = [lax.all_gather(first, "dp", axis=0, tiled=True)]
        up_all = lax.all_gather(w_up, "dp", axis=0, tiled=True)
        down_all = lax.all_gather(w_down, "dp", axis=0, tiled=True)
        down_parts = [lax.all_to_all(down_all, "seq", 0, 1, tiled=True).T]
        heads = lax.all_gather(lax.all_gather(w_out, "seq", axis=1, tiled=True), "dp", axis=0, tiled=True)
        heads = heads.reshape(S, WH, D)
        out_all = jnp.concatenate([lax.dynamic_index_in_dim(heads, me ^ e, keepdims=False) for e in range(S)])

    (xhat,) = pallas(
        fn(norm_kernel, m),
        [shape(m.RA, D, dtype=F32)],
        [gate(token_blocks[0], *norm_after), *token_blocks[1:]],
        [pltpu.VMEM((m.IT, D), F32)],
        name="norm",
    )
    qkv, normed, probs, packed, vecs, w_first = pallas(
        fn(attend_kernel, m, len(first_parts)),
        [
            shape(m.RA, 3 * WH),
            shape(m.RA, D),
            shape(m.B * m.H, m.IT, m.IT),
            shape(m.B * m.IT // 2, 2 * WH),
            shape(VECS, D, dtype=F32),
            shape(D, m.wide),
        ],
        [text_mask, patch_count, gate(xhat, *held), *first_parts],
        smem=2,
        here=True,
        name="attend",
    )
    packed_blocks = gather_seq(packed)
    if m.fast:
        after = [packed] if CFG["xu"] else []
        up_parts = up_same + swapped(up_same, CFG["su"], "stack_up", after)
        after = [packed] if CFG["xd"] else []
        down_parts = down_same + swapped(down_same, CFG["sd"], "stack_down", after)

    if m.fast:
        up_all, half = pallas(
            fn(assemble_kernel, m, len(up_parts)),
            [shape(D, m.FD), shape(D, 2 * WH)],
            [*up_parts],
            here=True,
            name="assemble",
        )
        out_all, cot = pallas(
            fn(join_kernel, m),
            [shape(D, D), shape(m.RA, D)],
            [half, seq_to(half, 1), *cot_blocks],
            here=True,
            name="join",
        )
    else:

        def only_pad(*refs):
            pad_cot(m, refs[:S], refs[S])

        (cot,) = pallas(only_pad, [shape(m.RA, D)], cot_blocks, name="pad_cot")

    normed2, active, slope, mixed, resid, xhat2, rstd2 = pallas(
        fn(forward_kernel, m),
        [
            shape(m.RA, D),
            shape(m.RA, m.FD),
            shape(m.RA, m.FD, dtype=F32),
            shape(m.RA, D),
            shape(m.OWN, D, dtype=F32),
            shape(m.OWN, D, dtype=F32),
            shape(m.OWN, 128, dtype=F32),
        ],
        [*token_blocks, *packed_blocks, out_all, up_all, vecs],
        [pltpu.VMEM((m.IT, D), F32)],
        here=True,
        name="forward",
    )
    def shards(width, height=D):
        if m.fast:
            return [shape(nz, rows, width)] * 2
        return [shape(height, width), shape(8, 128)]

    def weight_grad(left, right, name):
        return pallas(
            fn(weight_grad_kernel, m),
            shards(D),
            [left, right],
            [pltpu.VMEM((D, D), F32)],
            here=True,
            name=name,
        )

    down_keep, down_send = weight_grad(cot, active, "down_grad")
    g_hidden, down_all, keep0, keep1, send = pallas(
        fn(hidden_back_kernel, m, len(down_parts)),
        [shape(m.RA, m.FD), shape(D, m.FD), shape(m.OWN, D), shape(m.OWN, D), shape(2, m.OWN, D)],
        [cot, gate(slope, down_keep), up_all, *down_parts],
        here=True,
        name="hidden_back",
    )

    def add_pair(keep, core, name):
        (out,) = pallas(fn(pair_kernel, m), [shape(*keep.shape)], [keep, core], name=name)
        return out

    def add(left, right, name):
        (out,) = pallas(fn(add_kernel, m), [shape(*left.shape, dtype=F32)], [left, right], name=name)
        return out

    core2 = seq_to(send, 1)
    pair2 = add_pair(keep1, core2, "pair2")
    far2 = seq_to(pair2, 2)

    up_keep, up_send = weight_grad(normed2, gate(g_hidden, pair2), "up_grad")
    def branch(after):
        return pallas(
            fn(branch_kernel, m),
            [shape(m.OWN, D), shape(m.OWN, D), shape(2, m.OWN, D), shape(8, D, dtype=F32)],
            [gate(active, after), down_all, g_hidden, cot],
            name="branch",
        )

    if not CFG["br"]:
        b_keep0, b_keep1, b_send, vec_ff = branch(up_keep)
    g_resid, *blocks, vec_mid = pallas(
        fn(middle_kernel, m),
        [shape(m.OWN, D, dtype=F32), *[shape(m.OWN, 2 * WH)] * S, shape(8, D, dtype=F32)],
        [gate(keep0, up_keep if CFG["br"] else b_keep0), core2, far2, xhat2, rstd2, cot, out_all, vecs],
        [pltpu.VMEM((m.OWN, D), LOW)],
        here=True,
        name="middle",
    )
    if CFG["br"]:
        b_keep0, b_keep1, b_send, vec_ff = branch(g_resid)
    blocks = [blocks[0]] + [seq_to(blocks[e], e) for e in range(1, S)]
    if CFG["br"] == 1:
        blocks[0] = gate(blocks[0], b_keep0)

    def sum_x(keep, got, width, name):
        return pallas(
            fn(sum_x_kernel, m),
            [shape(rows, width, dtype=F32)] + [shape(rows, width)] * (nz - 1),
            [keep, got],
            name=name,
        )

    def to_z(parts):
        return [z_shift(part, k + 1) for k, part in enumerate(parts)]

    def scatter(full):
        return lax.psum_scatter(full, "dp", scatter_dimension=0, tiled=True).astype(F32)

    if m.fast:
        down_got, up_got = x_swap(down_send), x_swap(up_send)
        down_own, *down_sums = sum_x(gate(down_keep, blocks[0]), down_got, D, "down_x")
        down_z = to_z(down_sums)
        blocks[0] = gate(blocks[0], down_own)
    g_value, g_mixed, vo_keep, vo_send = pallas(
        fn(value_back_kernel, m),
        [shape(m.RA, WH), shape(m.RA, WH), *shards(2 * WH)],
        [probs, *blocks, normed, mixed],
        [pltpu.VMEM((m.RA, WH), LOW), pltpu.VMEM((D, 2 * WH), F32)],
        here=True,
        name="value_back",
    )
    if m.fast:
        vo_got = x_swap(vo_send)

        def sum_down(after):
            return pallas(
                fn(sum_down_kernel, m),
                [shape(rows, m.FD // 2)] * 2,
                [gate(down_own, after), *down_z],
                here=True,
                name="sum_down",
            )

    (g_qk,) = pallas(
        fn(attend_back_kernel, m),
        [shape(m.RA, 2 * WH)],
        [qkv, probs, g_mixed],
        name="attend_back",
    )
    g_last = g_qk
    if m.fast:
        up_own, vo_own, *both = pallas(
            fn(both_x_kernel, m),
            [shape(rows, m.FD, dtype=F32), shape(rows, 2 * WH, dtype=F32)]
            + [shape(m.up_rows, m.FD)] * (nz - 1),
            [gate(up_keep, g_qk), up_got, vo_keep, vo_got],
            name="both_x",
        )
        both_z = to_z(both)
        halves = sum_down(up_own)
        down_halves = [exchange(halves[k], k) for k in range(2)]
        g_last = gate(g_qk, halves[0])

        def give_down(*after):
            (out,) = pallas(
                fn(give_down_kernel, m),
                [shape(WH, S * m.hrows, dtype=F32)],
                [gate(down_halves[0], *after), down_halves[1]],
                here=True,
                name="give_down",
            )
            return out

    def qk_grad(after):
        return pallas(
            fn(weight_grad_kernel, m),
            shards(2 * WH),
            [normed, gate(g_last, after)],
            [pltpu.VMEM((D, 2 * WH), F32)],
            here=True,
            name="qk_grad",
        )

    if not CFG["ord"]:
        qk_keep, qk_send = qk_grad(g_qk)
    keep0, keep1, send, vec = pallas(
        fn(input_back_kernel, m),
        [shape(m.OWN, D), shape(2 * m.OWN, D), shape(2, 2 * m.OWN, D), shape(VECS, D, dtype=F32)],
        [gate(g_last, *([] if CFG["ord"] else [qk_keep])), g_value, xhat, w_first, vec_mid, vec_ff, b_keep1, b_send],
        here=True,
        name="input_back",
    )
    if CFG["ord"]:
        qk_keep, qk_send = qk_grad(vec)
    vec_core, core1 = seq_to(vec, 1), seq_to(send, 1)
    vec = add(vec, vec_core, "add_core")
    vec_far = seq_to(vec, 2)
    pair1 = add_pair(gate(keep1, *([vec_far] if CFG["pair"] else [vec])), core1, "pair1")
    far1 = seq_to(pair1, 2)
    if m.fast:
        qk_got = x_swap(qk_send)

        def both_out(after):
            return pallas(
                fn(both_z_kernel, m),
                [shape(rows, m.FD, dtype=F32)] + [shape(rows, WH, dtype=F32)] * 2,
                [gate(up_own, after), vo_own, *both_z],
                name="both_out",
            )

        if CFG["gd"]:
            g_down = give_down(pair1)
        vec = add(gate(vec, *([pair1] if CFG["add"] else []), *([g_down] if CFG["gd"] == 1 else [])), vec_far, "add_far")
        vec_got = x_swap(vec)
        qk_own, vec_own, *qk_sums = pallas(
            fn(last_x_kernel, m),
            [shape(rows, 2 * WH, dtype=F32), shape(2 * VECS, D // 2, dtype=F32)]
            + [shape(rows + 2 * VECS, 2 * WH)] * (nz - 1),
            [qk_keep, qk_got, vec, vec_got],
            name="last_x",
        )
        if CFG["both"] == 2:
            g_up, g_value, g_out = both_out(qk_own)
            qk_sums[0] = gate(qk_sums[0], g_up)
            qk_sums[1] = gate(qk_sums[1], g_up)
            qk_sums[2] = gate(qk_sums[2], g_up)
        if CFG["gd"] == 2:
            qk_sums[0] = gate(qk_sums[0], g_down)
        qk_z = to_z(qk_sums)
        if CFG["both"] == 0:
            g_up, g_value, g_out = both_out(qk_own)
            keep0 = gate(keep0, g_up)
        keep0 = gate(keep0, qk_own)
    else:
        vec = lax.psum(vec + vec_far, "dp")
        vec = lax.dynamic_slice(vec, (0, dp * rows), (VECS, rows))
        g_vo, g_qk = scatter(vo_keep), scatter(qk_keep)
        g_value, g_out, g_query, g_key = g_vo[:, :WH], g_vo[:, WH:], g_qk[:, :WH], g_qk[:, WH:]
        g_up = scatter(up_keep)
        g_down = scatter(lax.all_to_all(down_keep.T, "seq", 1, 0, tiled=True))
        vec_outs = [vec[k] for k in range(8)] + [vec[8 : 8 + S].reshape(-1)]

    result, input_grad = pallas(
        fn(finish_kernel, m),
        [shape(m.B, m.R, D), shape(m.B, m.R, D)],
        [keep0, core1, far1, tokens, g_resid, vecs, b_keep0, resid],
        name="finish",
    )
    if m.fast:
        if CFG["both"] == 1:
            g_up, g_value, g_out = both_out(result)
        if not CFG["gd"]:
            g_down = give_down(g_value, result)
        g_down = g_down.T
        g_query, g_key, *vec_outs = pallas(
            fn(last_z_kernel, m),
            [shape(rows, WH, dtype=F32)] * 2 + [shape(rows, dtype=F32)] * 8 + [shape(S * m.hrows, dtype=F32)],
            [gate(qk_own, g_down), vec_own, *qk_z],
            [pltpu.VMEM((VECS, rows), F32)],
            here=True,
            name="query_key",
        )
    return (
        result,
        input_grad,
        g_query,
        g_key,
        g_value,
        g_out,
        g_up,
        g_down,
        *vec_outs[:7],
        vec_outs[8],
        vec_outs[7],
    )


def solution(mesh):
    rows3, mat, vec = P("dp", "seq", None), P("dp", "seq"), P("dp")
    return jax.shard_map(
        functools.partial(local, mesh),
        mesh=mesh,
        in_specs=(rows3, rows3, P("dp", None), vec) + (mat,) * 6 + (vec,) * 9,
        out_specs=(rows3, rows3) + (mat,) * 6 + (vec,) * 9,
        check_vma=False,
    )
```

```python
import functools
from types import SimpleNamespace

import jax
import jax.numpy as jnp
from jax import lax
from jax.experimental import pallas as pl
from jax.experimental.pallas import tpu as pltpu
from jax.sharding import PartitionSpec as P

HEADS = 12
COST = {'up_grad': 10000000000, 'branch': 10000000000, 'value_back': 10000000000, 'attend_back': 10000000000, 'finish': 10000000000, 'pack': 3000000000, 'sum_down': 1000, 'sum_up': 1000, 'last_x': 30000000000, 'hidden_back': 3000000000, 'qk_grad': 2000000000, 'stack_down': 5000000000, 'both_x': 500000000, 'split_down': 2000000000}
CFG = {'pair': 1, 'add': 1, 'za': 'direct', 'zu': 'bidir', 'zd': 'bidir', 'xu': 0, 'xd': 0, 'norm': 2, 'held': 0, 'split': 3, 'cot': 1, 'tok': 1, 'ord': 1, 'up': 0, 'vo': 0, 'br': 1, 'both': 0, 'og': 3, 'sa': 'each', 'su': 'each', 'sd': 'rest', 'gd': 2, 'gx': 0}
EPS = 1e-05
LOW = jnp.bfloat16
F32 = jnp.float32
VECS = 16
UP_BIAS = 12
SQRT_HALF = 0.7071067811865476
PDF_SCALE = 0.3989422804014327


def dot(left, right):
    return jnp.dot(left, right, preferred_element_type=F32)


def dot_t(left, right):
    return lax.dot_general(left, right, (((1,), (1,)), ((), ())), preferred_element_type=F32)


def t_dot(left, right):
    return lax.dot_general(left, right, (((0,), (0,)), ((), ())), preferred_element_type=F32)


def col_sum(values):
    return jnp.sum(values, axis=0, keepdims=True)


def ds(start, size, align=16):
    if not isinstance(start, int):
        start = pl.multiple_of(start, align)
    return pl.ds(start, size)


def pallas(body, outs, ins, scratch=(), smem=0, here=False, name=None, mib=8):
    flops = COST.get(name, 1000)
    nbytes = sum(a.size * a.dtype.itemsize for a in ins)
    nbytes += sum(s.size * jnp.dtype(s.dtype).itemsize for s in outs)
    near = pl.BlockSpec(memory_space=pltpu.VMEM)

    def run(*refs):
        if here:
            dp = lax.axis_index("dp")
            body((lax.axis_index("seq"), lax.div(dp, 2), lax.rem(dp, 2)), *refs)
        else:
            body(*refs)

    return pl.pallas_call(
        run,
        out_shape=outs,
        in_specs=[pl.BlockSpec(memory_space=pltpu.SMEM)] * smem + [near] * (len(ins) - smem),
        out_specs=[near] * len(outs),
        scratch_shapes=list(scratch),
        compiler_params=pltpu.CompilerParams(vmem_limit_bytes=mib * 2**20),
        cost_estimate=pl.CostEstimate(flops=flops, bytes_accessed=nbytes, transcendentals=0),
        name=name,
    )(*ins)


def shape(*dims, dtype=LOW):
    return jax.ShapeDtypeStruct(dims, dtype)


def part_index(m, sc, part):
    z, x = sc[1], sc[2]
    k = part % m.nz
    side = x if part < m.nz else 1 - x
    return lax.rem(z - k + m.nz, m.nz) * 2 + side


def spread(parts):
    out = []
    for part in parts:
        out += [part.at[k] for k in range(part.shape[0])] if len(part.shape) == 3 else [part]
    return out


def layer_norm(x):
    center = x - jnp.mean(x, axis=-1, keepdims=True)
    rstd = lax.rsqrt(jnp.mean(center * center, axis=-1, keepdims=True) + EPS)
    return center * rstd, rstd


def norm_back(grad, gain, xhat, rstd):
    scaled = grad * gain
    first = jnp.mean(scaled, axis=-1, keepdims=True)
    second = jnp.mean(scaled * xhat, axis=-1, keepdims=True)
    return rstd * (scaled - first - xhat * second)


def pack_kernel(m, query, key, value, *refs):
    vecs, first, rows = refs[:9], refs[9], refs[10]
    first[:, : m.WH] = query[...]
    first[:, m.WH : 2 * m.WH] = key[...]
    first[:, 2 * m.WH : 3 * m.WH] = value[...]
    first[:, 3 * m.WH :] = jnp.zeros((m.rows, m.wide - 3 * m.WH), LOW)
    rows[...] = jnp.zeros_like(rows)
    for k in range(8):
        rows[k : k + 1, :] = vecs[k][...].astype(F32).reshape(1, m.rows)
    up_bias = vecs[8][...].astype(F32).reshape(1, m.S * m.hrows)
    for c in range(m.S):
        rows[8 + c : 9 + c, :] = up_bias[:, c * m.hrows : (c + 1) * m.hrows]
    first[:, 3 * m.WH : 3 * m.WH + VECS] = rows[...].T.astype(LOW)


def pack_up_kernel(m, up, out, far, packed):
    half = m.rows // 2
    packed[: m.rows, :] = up[...]
    for side in range(2):
        at = slice(side * half, (side + 1) * half)
        packed[m.rows :, 2 * side * m.WH : (2 * side + 1) * m.WH] = out[at, :]
        packed[m.rows :, (2 * side + 1) * m.WH : (2 * side + 2) * m.WH] = far[at, :]


def split_down_kernel(m, sc, down_t, first, second):
    half = m.WH // 2
    for x in range(2):

        @pl.when(sc[2] == x)
        def _(x=x):
            first[...] = down_t[x * half : (x + 1) * half, :]
            second[...] = down_t[(1 - x) * half : (2 - x) * half, :]


def join_down_kernel(m, sc, first, second, down):
    width = m.FD // 2
    for x in range(2):

        @pl.when(sc[2] == x)
        def _(x=x):
            down[:, x * width : (x + 1) * width] = first[...]
            down[:, (1 - x) * width : (2 - x) * width] = second[...]


def stack_kernel(m, *refs):
    for k, ref in enumerate(refs[:-1]):
        refs[-1][k] = ref[...]


def norm_kernel(m, *refs):
    tokens, (xhat, x_scr) = refs[: m.S], refs[m.S :]
    x_scr[...] = jnp.zeros_like(x_scr)

    def item(b, carry):
        for d in range(m.S):
            x_scr[d * m.RP : d * m.RP + m.R, :] = tokens[d][b].astype(F32)
        xhat[ds(b * m.IT, m.IT), :], _ = layer_norm(x_scr[...])
        return carry

    lax.fori_loop(0, m.B, item, 0)


def attend_kernel(m, nparts, *refs):
    sc, text_mask, patch_count, xhat_ref = refs[:4]
    parts = refs[4 : 4 + nparts]
    qkv, normed, probs, packed, vecs, w_ref = refs[4 + nparts :]
    me = sc[0]
    if nparts == 1:
        w_ref[...] = parts[0][...]
    else:
        for p, part in enumerate(spread(parts)):
            w_ref[ds(part_index(m, sc, p) * m.rows, m.rows), :] = part[...]
    base = (3 * m.WH) // 128 * 128
    turned = w_ref[:, base : base + 128].astype(F32).T
    vecs[...] = turned[3 * m.WH - base : 3 * m.WH - base + VECS]
    for c in range(m.S):

        @pl.when(me == c)
        def _(c=c):
            for t in range(m.N // m.S):
                for k in range(m.S):
                    lanes = slice((t * m.S + k) * m.hrows, (t * m.S + k + 1) * m.hrows)
                    begin = c * m.WH + t * m.rows
                    vecs[UP_BIAS : UP_BIAS + 1, lanes] = vecs[8 + k : 9 + k, begin : begin + m.rows]

    gain, shift = vecs[0:1, :], vecs[1:2, :]
    q_bias = jnp.zeros((1, m.WH), F32)
    v_bias = jnp.zeros((1, m.WH), F32)
    for c in range(m.S):
        here = me == c
        q_bias = jnp.where(here, vecs[2:3, c * m.WH : (c + 1) * m.WH], q_bias)
        v_bias = jnp.where(here, vecs[3:4, c * m.WH : (c + 1) * m.WH], v_bias)
    bias = jnp.concatenate([q_bias, jnp.zeros((1, m.WH), F32), v_bias], axis=1)

    lane = lax.broadcasted_iota(jnp.int32, (1, m.IT), 1)
    place = jnp.full((1, m.IT), 1 << 20, jnp.int32)
    for d in range(m.S):
        row = lane - d * m.RP
        here = jnp.where(row < m.R, (me ^ d) * m.R + row, 1 << 20)
        place = jnp.where(row < 0, place, here)

    def item(b, carry):
        at = ds(b * m.IT, m.IT)
        low = (xhat_ref[at, :] * gain + shift).astype(LOW)
        normed[at, :] = low
        qkv[at, :] = (dot(low, w_ref[:, : 3 * m.WH]) + bias).astype(LOW)
        words = text_mask[b, 0]
        for k in range(1, m.TXT):
            words = words + text_mask[b, k]
        masked = jnp.where(
            place < m.TXT,
            jnp.where(place < words, 0.0, -1e30),
            jnp.where(place - m.TXT < patch_count[b], 0.0, -1e30),
        )
        half = m.IT // 2
        for h in range(m.H):
            q = qkv[at, h * m.hd : (h + 1) * m.hd] * LOW(m.hd**-0.5)
            k = qkv[at, m.WH + h * m.hd : m.WH + (h + 1) * m.hd]
            v = qkv[at, 2 * m.WH + h * m.hd : 2 * m.WH + (h + 1) * m.hd]
            s = dot_t(q, k) + masked
            e = jnp.exp(s - jnp.max(s, axis=-1, keepdims=True))
            p = (e * (1.0 / jnp.sum(e, axis=-1, keepdims=True))).astype(LOW)
            probs[b * m.H + h] = p
            o = dot(p, v).astype(LOW)
            packed[ds(b * half, half), h * m.hd : (h + 1) * m.hd] = o[:half]
            packed[ds(b * half, half), m.WH + h * m.hd : m.WH + (h + 1) * m.hd] = o[half:]
        return carry

    lax.fori_loop(0, m.B, item, 0)


def assemble_kernel(m, nparts, *refs):
    sc = refs[0]
    parts = refs[1 : 1 + nparts]
    w_up, w_out = refs[1 + nparts :]
    half = m.rows // 2
    per = m.N // m.S
    for p, part in enumerate(spread(parts)):
        i = part_index(m, sc, p)
        w_up[ds(i * m.rows, m.rows), :] = part[: m.rows]
        start = (sc[0] ^ lax.div(i, per)) * m.WH + lax.rem(i, per) * m.rows
        w_out[ds(start, half), :] = part[m.rows :, : 2 * m.WH]
        w_out[ds(start + half, half), :] = part[m.rows :, 2 * m.WH :]


def join_kernel(m, sc, own, other, *refs):
    cots = refs[: m.S]
    w_out, cot = refs[m.S :]
    for c in range(m.S):

        @pl.when(sc[0] == c)
        def _(c=c):
            for d in range(m.S):
                half = (own, other)[d % 2]
                lanes = slice((c ^ d) * m.WH, ((c ^ d) + 1) * m.WH)
                for e in range(m.S):
                    rows = slice((e ^ (d % 2)) * m.WH, ((e ^ (d % 2)) + 1) * m.WH)
                    w_out[e * m.WH : (e + 1) * m.WH, lanes] = half[rows, d // 2 * m.WH : (d // 2 + 1) * m.WH]

    pad_cot(m, cots, cot)


def pad_cot(m, cots, cot):
    cot[...] = jnp.zeros_like(cot)
    for b in range(m.B):
        for d in range(m.S):
            start = (b * m.S + d) * m.RP
            cot[start : start + m.R, :] = cots[d][b]


def forward_kernel(m, *refs):
    sc = refs[0]
    tokens = refs[1 : 1 + m.S]
    packed = refs[1 + m.S : 1 + 2 * m.S]
    w_out, w_up, vecs = refs[1 + 2 * m.S : 4 + 2 * m.S]
    normed, active, slope, mixed, resid_own, xhat_own, rstd_own, x_scr = refs[4 + 2 * m.S :]
    me = sc[0]
    out_bias, gain, shift = vecs[4:5, :], vecs[5:6, :], vecs[6:7, :]
    up_bias = vecs[UP_BIAS : UP_BIAS + 1, :]
    x_scr[...] = jnp.zeros_like(x_scr)

    def item(b, carry):
        at = ds(b * m.IT, m.IT)
        half = m.IT // 2
        for d in range(m.S):
            x_scr[d * m.RP : d * m.RP + m.R, :] = tokens[d][b].astype(F32)
        for e in range(m.S):
            for side in range(2):
                piece = packed[e][ds(b * half, half), side * m.WH : (side + 1) * m.WH]
                for t in range(2):
                    d = (2 * side + t) ^ e
                    mixed[ds(b * m.IT + d * m.RP, m.RP), e * m.WH : (e + 1) * m.WH] = piece[
                        t * m.RP : (t + 1) * m.RP
                    ]
        resid = x_scr[...] + (dot(mixed[at, :], w_out[...]) + out_bias)
        xhat, rstd = layer_norm(resid)
        own = ds(b * m.RP, m.RP)
        resid_own[own, :] = resid[: m.RP]
        xhat_own[own, :] = xhat[: m.RP]
        rstd_own[own, :] = jnp.broadcast_to(rstd[: m.RP], (m.RP, 128))
        low = (xhat * gain + shift).astype(LOW)
        normed[at, :] = low
        hidden = dot(low, w_up[...]) + up_bias
        cdf = 0.5 + 0.5 * lax.erf(hidden * SQRT_HALF)
        active[at, :] = (hidden * cdf).astype(LOW)
        slope[at, :] = cdf + hidden * (PDF_SCALE * jnp.exp(-0.5 * hidden * hidden))
        return carry

    lax.fori_loop(0, m.B, item, 0)


def hidden_back_kernel(m, nparts, *refs):
    sc, cot, slope, w_up = refs[:4]
    parts = refs[4 : 4 + nparts]
    g_hidden, w_down, keep0, keep1, send = refs[4 + nparts :]
    if nparts == 1:
        w_down[...] = parts[0][...]
    else:
        for p, part in enumerate(spread(parts)):
            w_down[ds(part_index(m, sc, p) * m.rows, m.rows), :] = part[...]

    def item(b, carry):
        at = ds(b * m.IT, m.IT)
        back = (dot(cot[at, :], w_down[...]) * slope[at, :]).astype(LOW)
        g_hidden[at, :] = back
        give_rows(m, b, dot_t(back, w_up[...]).astype(LOW), keep0, keep1, send)
        return carry

    lax.fori_loop(0, m.B, item, 0)


def give_shards(m, sc, total, keep, send):
    for k in range(m.nz):
        z = lax.rem(sc[1] + k, m.nz)
        keep[k] = total[ds((2 * z + sc[2]) * m.rows, m.rows), :].astype(LOW)
        send[k] = total[ds((2 * z + 1 - sc[2]) * m.rows, m.rows), :].astype(LOW)


def give(m, sc, total, keep, send):
    if m.fast:
        give_shards(m, sc, total, keep, send)
    else:
        keep[...] = total[...].astype(LOW)
        send[...] = jnp.zeros_like(send)


def give_rows(m, b, values, keep0, keep1, send):
    own = ds(b * m.RP, m.RP)
    keep0[own, :] = values[: m.RP]
    send[0, own, :] = values[m.RP : 2 * m.RP]
    keep1[own, :] = values[2 * m.RP : 3 * m.RP]
    send[1, own, :] = values[3 * m.RP : 4 * m.RP]


def weight_grad_kernel(m, sc, left, right, keep, send, total):
    step = 256
    for begin in range(0, m.D, step):
        total[begin : begin + step, :] = t_dot(left[:, begin : begin + step], right[...])
    give(m, sc, total, keep, send)


def branch_kernel(m, active, w_down, g_hidden, cot, keep0, keep1, send, vec):
    vec[...] = jnp.zeros_like(vec)

    def item(b, carry):
        at = ds(b * m.IT, m.IT)
        give_rows(m, b, dot_t(active[at, :], w_down[...]).astype(LOW), keep0, keep1, send)
        vec[0:1, :] += col_sum(cot[ds(b * m.IT, m.RP), :].astype(F32))
        vec[1:2, :] += col_sum(g_hidden[at, :].astype(F32))
        return carry

    lax.fori_loop(0, m.B, item, 0)


def pair_kernel(m, keep, core, out):
    out[...] = (keep[...].astype(F32) + core[1].astype(F32)).astype(LOW)


def add_kernel(m, left, right, out):
    out[...] = left[...] + right[...]


def middle_kernel(m, *refs):
    sc, keep0, core, far, xhat_own, rstd_own, cot, w_out, vecs = refs[:9]
    g_resid = refs[9]
    blocks = refs[10 : 10 + m.S]
    vec, low_scr = refs[10 + m.S :]
    me = sc[0]
    gain = vecs[5:6, :]
    grad = keep0[...].astype(F32) + core[0].astype(F32) + far[...].astype(F32)
    xhat = xhat_own[...]
    back = norm_back(grad, gain, xhat, rstd_own[:, 0:1])
    vec[...] = jnp.zeros_like(vec)
    vec[0:1, :] = col_sum(grad * xhat)
    vec[1:2, :] = col_sum(grad)
    for b in range(m.B):
        own = slice(b * m.RP, (b + 1) * m.RP)
        full = back[own] + cot[b * m.IT : b * m.IT + m.RP, :].astype(F32)
        g_resid[own, :] = full
        low_scr[own, :] = full.astype(LOW)
    low = low_scr[...]
    vec[2:3, :] = col_sum(low.astype(F32))
    g_mixed = dot_t(low, w_out[...]).astype(LOW)
    for e in range(m.S):
        blocks[e][:, : m.WH] = g_mixed[:, e * m.WH : (e + 1) * m.WH]
        picked = low[:, : m.WH]
        for c in range(1, m.S):
            picked = jnp.where((me ^ e) == c, low[:, c * m.WH : (c + 1) * m.WH], picked)
        blocks[e][:, m.WH :] = picked


def value_back_kernel(m, *refs):
    sc, probs = refs[:2]
    blocks = refs[2 : 2 + m.S]
    normed, mixed = refs[2 + m.S : 4 + m.S]
    g_value, g_mixed, keep, send, ga_scr, total = refs[4 + m.S :]

    def item(b, carry):
        at = ds(b * m.IT, m.IT)
        own = ds(b * m.RP, m.RP)
        for d in range(m.S):
            ga_scr[ds(b * m.IT + d * m.RP, m.RP), :] = blocks[d][own, m.WH :]
            g_mixed[ds(b * m.IT + d * m.RP, m.RP), :] = blocks[d][own, : m.WH]
        for h in range(m.H):
            lanes = slice(h * m.hd, (h + 1) * m.hd)
            g_value[at, lanes] = t_dot(probs[b * m.H + h], g_mixed[at, lanes]).astype(LOW)
        return carry

    lax.fori_loop(0, m.B, item, 0)
    total[:, : m.WH] = t_dot(normed[...], g_value[...])
    g_out = t_dot(mixed[...], ga_scr[...])
    for e in range(m.S):
        total[ds((sc[0] ^ e) * m.WH, m.WH), m.WH :] = g_out[e * m.WH : (e + 1) * m.WH]
    give(m, sc, total, keep, send)


def attend_back_kernel(m, qkv, probs, g_mixed, g_qk):
    scale = m.hd**-0.5

    def item(b, carry):
        at = ds(b * m.IT, m.IT)
        for h in range(m.H):
            lanes = slice(h * m.hd, (h + 1) * m.hd)
            q = qkv[at, h * m.hd : (h + 1) * m.hd]
            k = qkv[at, m.WH + h * m.hd : m.WH + (h + 1) * m.hd]
            v = qkv[at, 2 * m.WH + h * m.hd : 2 * m.WH + (h + 1) * m.hd]
            p = probs[b * m.H + h].astype(F32)
            gp = dot_t(g_mixed[at, lanes], v)
            gs = (p * (gp - jnp.sum(p * gp, axis=-1, keepdims=True))).astype(LOW)
            g_qk[at, h * m.hd : (h + 1) * m.hd] = (dot(gs, k) * scale).astype(LOW)
            g_qk[at, m.WH + h * m.hd : m.WH + (h + 1) * m.hd] = (t_dot(gs, q) * scale).astype(LOW)
        return carry

    lax.fori_loop(0, m.B, item, 0)


def input_back_kernel(m, sc, g_qk, g_value, xhat, w, vec_mid, vec_ff, b_keep1, b_send, keep0, keep1, send, v_scr):
    me = sc[0]
    v_scr[...] = jnp.zeros_like(v_scr)

    def item(b, carry):
        at = ds(b * m.IT, m.IT)
        grad = dot_t(g_qk[at, :], w[:, : 2 * m.WH]) + dot_t(g_value[at, :], w[:, 2 * m.WH : 3 * m.WH])
        v_scr[0:1, :] += col_sum(grad * xhat[at, :])
        v_scr[1:2, :] += col_sum(grad)
        give_rows(m, b, grad.astype(LOW), keep0, keep1, send)
        return carry

    lax.fori_loop(0, m.B, item, 0)
    q_sum = col_sum(g_qk[:, : m.WH].astype(F32))
    v_sum = col_sum(g_value[...].astype(F32))
    for c in range(m.S):
        here = me == c
        lanes = slice(c * m.WH, (c + 1) * m.WH)
        v_scr[2:3, lanes] = jnp.where(here, q_sum, 0.0)
        v_scr[3:4, lanes] = jnp.where(here, v_sum, 0.0)
        for t in range(m.N // m.S):
            for k in range(m.S):
                begin = c * m.WH + t * m.rows
                part = vec_ff[1:2, (t * m.S + k) * m.hrows : (t * m.S + k + 1) * m.hrows]
                v_scr[8 + k : 9 + k, begin : begin + m.rows] = jnp.where(here, part, 0.0)
    v_scr[4:5, :] = vec_mid[2:3, :]
    v_scr[5:6, :] = vec_mid[0:1, :]
    v_scr[6:7, :] = vec_mid[1:2, :]
    v_scr[7:8, :] = vec_ff[0:1, :]
    keep1[m.OWN :, :] = b_keep1[...]
    send[0, m.OWN :, :] = b_send[0]
    send[1, m.OWN :, :] = b_send[1]


def sum_x_kernel(m, keep, got, own, *outs):
    own[...] = keep[0].astype(F32) + got[0].astype(F32)
    for k, out in enumerate(outs):
        out[...] = (keep[k + 1].astype(F32) + got[k + 1].astype(F32)).astype(LOW)


def both_x_kernel(m, up_keep, up_got, vo_keep, vo_got, up_own, vo_own, *outs):
    half = m.rows // 2
    up_own[...] = up_keep[0].astype(F32) + up_got[0].astype(F32)
    vo_own[...] = vo_keep[0].astype(F32) + vo_got[0].astype(F32)
    for k, out in enumerate(outs):
        out[: m.rows, :] = (up_keep[k + 1].astype(F32) + up_got[k + 1].astype(F32)).astype(LOW)
        total = (vo_keep[k + 1].astype(F32) + vo_got[k + 1].astype(F32)).astype(LOW)
        out[m.rows :, : 2 * m.WH] = total[:half]
        out[m.rows :, 2 * m.WH :] = total[half:]


def both_z_kernel(m, up_own, vo_own, *refs):
    rest, (g_up, first, second) = refs[: m.nz - 1], refs[m.nz - 1 :]
    half = m.rows // 2
    total = up_own[...]
    for r in rest:
        total = total + r[: m.rows, :].astype(F32)
    g_up[...] = total
    for side in range(2):
        at = slice(side * half, (side + 1) * half)
        total = vo_own[at, :]
        for r in rest:
            total = total + r[m.rows :, 2 * m.WH * side : 2 * m.WH * (side + 1)].astype(F32)
        first[at, :] = total[:, : m.WH]
        second[at, :] = total[:, m.WH :]


def last_x_kernel(m, keep, got, vec, vec_got, own, vec_own, *outs):
    own[...] = keep[0].astype(F32) + got[0].astype(F32)
    values = vec[...] + vec_got[...]
    half = m.D // 2
    vec_own[:VECS, :] = values[:, :half]
    vec_own[VECS:, :] = values[:, half:]
    for k, out in enumerate(outs):
        out[: m.rows, :] = (keep[k + 1].astype(F32) + got[k + 1].astype(F32)).astype(LOW)
        out[m.rows :, :] = vec_own[...].astype(LOW)


def sum_z_kernel(m, *refs):
    own, rest, outs = refs[0], refs[1 : m.nz], refs[m.nz :]
    total = own[...]
    for r in rest:
        total = total + r[...].astype(F32)
    outs[0][...] = total[:, : m.WH]
    outs[1][...] = total[:, m.WH :]


def last_z_kernel(m, sc, own, vec_own, *refs):
    rest, (first, second), vecs, picked = refs[: m.nz - 1], refs[m.nz - 1 : m.nz + 1], refs[m.nz + 1 : -1], refs[-1]
    total, values = own[...], vec_own[...]
    for r in rest:
        total = total + r[: m.rows, :].astype(F32)
        values = values + r[m.rows :, :].astype(F32)
    first[...] = total[:, : m.WH]
    second[...] = total[:, m.WH :]
    for i in range(m.N):

        @pl.when(2 * sc[1] + sc[2] == i)
        def _(i=i):
            side, lane = divmod(i * m.rows, m.D // 2)
            picked[...] = values[side * VECS : (side + 1) * VECS, lane : lane + m.rows]

    for k in range(8):
        vecs[k][...] = picked[k : k + 1, :].reshape(m.rows)
    vecs[8][...] = jnp.concatenate([picked[8 + c : 9 + c, :] for c in range(m.S)], axis=1).reshape(m.S * m.rows)


def sum_down_kernel(m, sc, own, *refs):
    rest, (first, second) = refs[:-2], refs[-2:]
    total = own[...]
    for r in rest:
        total = total + r[...].astype(F32)
    width = m.FD // 2
    for x in range(2):

        @pl.when(sc[2] == x)
        def _(x=x):
            first[...] = total[:, x * width : (x + 1) * width].astype(LOW)
            second[...] = total[:, (1 - x) * width : (2 - x) * width].astype(LOW)


def sum_up_kernel(m, own, *refs):
    rest, out = refs[:-1], refs[-1]
    total = own[...]
    for r in rest:
        total = total + r[...].astype(F32)
    out[...] = total


def give_down_kernel(m, sc, first, second, g_down):
    for x in range(2):

        @pl.when(sc[2] == x)
        def _(x=x):
            g_down[x * m.rows : (x + 1) * m.rows, :] = first[...].astype(F32)
            g_down[(1 - x) * m.rows : (2 - x) * m.rows, :] = second[...].astype(F32)


def finish_kernel(m, *refs):
    keep0, core, far, tokens, g_resid, vecs, b_keep, resid = refs[:8]
    result, input_grad = refs[8:]
    gain, down_bias = vecs[0:1, :], vecs[7:8, :]
    for b in range(m.B):
        own = slice(b * m.RP, b * m.RP + m.R)
        also = slice(m.OWN + b * m.RP, m.OWN + b * m.RP + m.R)
        grad = keep0[own, :].astype(F32) + core[0, own, :].astype(F32) + far[own, :].astype(F32)
        xhat, rstd = layer_norm(tokens[b].astype(F32))
        back = norm_back(grad, gain, xhat, rstd)
        input_grad[b] = (g_resid[own, :] + back).astype(LOW)
        branch = b_keep[own, :].astype(F32) + core[0, also, :].astype(F32) + far[also, :].astype(F32)
        result[b] = (resid[own, :] + (branch + down_bias)).astype(LOW)


def plan(mesh, tokens, text_mask, w_query, w_up):
    m = SimpleNamespace()
    m.N, m.S = mesh.shape["dp"], mesh.shape["seq"]
    m.B, m.R, m.D = tokens.shape
    m.RP = -(-m.R // 16) * 16
    m.IT = m.S * m.RP
    m.RA = m.B * m.IT
    m.OWN = m.B * m.RP
    m.TXT = text_mask.shape[1]
    m.rows, m.WH = w_query.shape
    m.hd = m.D // HEADS
    m.H = HEADS // m.S
    m.FD = w_up.shape[1]
    m.hrows = m.FD // m.N
    m.fast = m.N == 2 * m.S
    m.nz = m.N // 2
    m.wide = -(-(3 * m.WH + VECS) // 128) * 128
    m.up_rows = m.rows + m.rows // 2
    return m


def local(
    mesh,
    tokens,
    cotangent,
    text_mask,
    patch_count,
    w_query,
    w_key,
    w_value,
    w_out,
    w_up,
    w_down,
    norm1_gain,
    norm1_bias,
    query_bias,
    value_bias,
    out_bias,
    norm2_gain,
    norm2_bias,
    up_bias,
    down_bias,
):
    m = plan(mesh, tokens, text_mask, w_query, w_up)
    N, S, rows, WH, D, nz = m.N, m.S, m.rows, m.WH, m.D, m.nz
    dp = lax.axis_index("dp").astype(jnp.int32)
    me = lax.axis_index("seq").astype(jnp.int32)
    fn = functools.partial

    def seq_to(x, e):
        return lax.ppermute(x, "seq", [(i, i ^ e) for i in range(S)])

    def x_swap(x):
        return lax.ppermute(x, "dp", [(i, i ^ 1) for i in range(N)])

    def z_shift(x, k):
        return lax.ppermute(x, "dp", [(i, (i + 2 * k) % N) for i in range(N)])

    def gate(x, *others):
        return lax.optimization_barrier((x, *others))[0]

    def direct(x):
        same = [x] + [z_shift(x, k) for k in range(1, nz)]
        return same + [x_swap(v) for v in same]

    def around(x, kind):
        if kind == "direct":
            return [x] + [z_shift(x, k) for k in range(1, nz)]
        if kind == "ring":
            out = [x]
            for _ in range(1, nz):
                out.append(z_shift(out[-1], 1))
            return out
        a, b = z_shift(x, 1), z_shift(x, nz - 1)
        return [x, a, z_shift(a, 1), b]

    def swapped(same, kind, name, after=()):
        if kind == "each":
            return [x_swap(same[0])] + [x_swap(gate(v, *after)) for v in same[1:]]
        begin = 1 if kind == "rest" else 0
        rest = [gate(same[begin], *after), *same[begin + 1 :]]
        (stacked,) = pallas(fn(stack_kernel, m), [shape(len(rest), *same[0].shape)], rest, name=name)
        return [x_swap(same[0])] * begin + [x_swap(stacked)]

    def exchange(x, k):
        pairs = []
        for i in range(N):
            for j in range(S):
                to = 2 * j + (i + k) % 2
                pairs.append((i * S + j, to * S + i // 2))
        return lax.ppermute(x, ("dp", "seq"), pairs)

    def gather_seq(x):
        far = seq_to(x, 2)
        return [x, seq_to(x, 1), far, seq_to(far, 1)]

    vectors = [norm1_gain, norm1_bias, query_bias, value_bias, out_bias, norm2_gain, norm2_bias, down_bias, up_bias]
    if m.fast:
        (first,) = pallas(
            fn(pack_kernel, m),
            [shape(rows, m.wide)],
            [w_query, w_key, w_value, *vectors],
            [pltpu.VMEM((VECS, rows), F32)],
            name="pack",
            mib=60,
        )
        first_same = around(first, CFG["za"])
        first_parts = first_same + swapped(first_same, CFG["sa"], "stack_first")
        out_far = seq_to(gate(w_out, *{0: [], 1: [first_parts[nz]], 2: [first_same[1]], 3: [first]}[CFG["og"]]), 2)
        (up_out,) = pallas(
            fn(pack_up_kernel, m), [shape(m.up_rows, D)], [gate(w_up, first), w_out, out_far], name="pack_up"
        )
        halves = pallas(
            fn(split_down_kernel, m),
            [shape(WH // 2, S * m.hrows)] * 2,
            [gate(w_down.T, *{0: [], 1: [first], 2: [up_out], 3: [first_same[1]], 4: first_same[1:]}[CFG["split"]])],
            here=True,
            name="split_down",
        )
        (down,) = pallas(
            fn(join_down_kernel, m),
            [shape(rows, m.FD)],
            [exchange(halves[k], k) for k in range(2)],
            here=True,
            name="join_down",
        )
        token_blocks = gather_seq(gate(tokens, *{0: [], 1: [first]}[CFG["tok"]]))
        cot_blocks = gather_seq(gate(cotangent, *{0: [first], 1: [token_blocks[2]], 2: [up_out]}[CFG["cot"]]))
        up_same = around(up_out, CFG["zu"])
        down_same = around(down, CFG["zd"])
        norm_after = {0: [], 1: [up_out], 2: [up_out, down], 3: [up_out, *first_same[1:]], 4: [up_out, down, *first_same[1:]]}[CFG["norm"]]
        held = {0: [], 1: [cot_blocks[2]], 2: [up_same[1]], 3: [up_same[1], up_same[-1]], 4: [down]}[CFG["held"]]
    else:
        token_blocks = gather_seq(tokens)
        cot_blocks = gather_seq(cotangent)
        held = norm_after = []
        pad = jnp.zeros((rows, m.wide - 3 * WH - VECS), LOW)
        vec_rows = jnp.concatenate(vectors + [jnp.zeros(((VECS - 8 - S) * rows,), LOW)]).reshape(VECS, rows)
        first = jnp.concatenate([w_query, w_key, w_value, vec_rows.T, pad], axis=1)
        first_parts = [lax.all_gather(first, "dp", axis=0, tiled=True)]
        up_all = lax.all_gather(w_up, "dp", axis=0, tiled=True)
        down_all = lax.all_gather(w_down, "dp", axis=0, tiled=True)
        down_parts = [lax.all_to_all(down_all, "seq", 0, 1, tiled=True).T]
        heads = lax.all_gather(lax.all_gather(w_out, "seq", axis=1, tiled=True), "dp", axis=0, tiled=True)
        heads = heads.reshape(S, WH, D)
        out_all = jnp.concatenate([lax.dynamic_index_in_dim(heads, me ^ e, keepdims=False) for e in range(S)])

    (xhat,) = pallas(
        fn(norm_kernel, m),
        [shape(m.RA, D, dtype=F32)],
        [gate(token_blocks[0], *norm_after), *token_blocks[1:]],
        [pltpu.VMEM((m.IT, D), F32)],
        name="norm",
    )
    qkv, normed, probs, packed, vecs, w_first = pallas(
        fn(attend_kernel, m, len(first_parts)),
        [
            shape(m.RA, 3 * WH),
            shape(m.RA, D),
            shape(m.B * m.H, m.IT, m.IT),
            shape(m.B * m.IT // 2, 2 * WH),
            shape(VECS, D, dtype=F32),
            shape(D, m.wide),
        ],
        [text_mask, patch_count, gate(xhat, *held), *first_parts],
        smem=2,
        here=True,
        name="attend",
    )
    packed_blocks = gather_seq(packed)
    if m.fast:
        after = [packed] if CFG["xu"] else []
        up_parts = up_same + swapped(up_same, CFG["su"], "stack_up", after)
        after = [packed] if CFG["xd"] else []
        down_parts = down_same + swapped(down_same, CFG["sd"], "stack_down", after)

    if m.fast:
        up_all, half = pallas(
            fn(assemble_kernel, m, len(up_parts)),
            [shape(D, m.FD), shape(D, 2 * WH)],
            [*up_parts],
            here=True,
            name="assemble",
        )
        out_all, cot = pallas(
            fn(join_kernel, m),
            [shape(D, D), shape(m.RA, D)],
            [half, seq_to(half, 1), *cot_blocks],
            here=True,
            name="join",
        )
    else:

        def only_pad(*refs):
            pad_cot(m, refs[:S], refs[S])

        (cot,) = pallas(only_pad, [shape(m.RA, D)], cot_blocks, name="pad_cot")

    normed2, active, slope, mixed, resid, xhat2, rstd2 = pallas(
        fn(forward_kernel, m),
        [
            shape(m.RA, D),
            shape(m.RA, m.FD),
            shape(m.RA, m.FD, dtype=F32),
            shape(m.RA, D),
            shape(m.OWN, D, dtype=F32),
            shape(m.OWN, D, dtype=F32),
            shape(m.OWN, 128, dtype=F32),
        ],
        [*token_blocks, *packed_blocks, out_all, up_all, vecs],
        [pltpu.VMEM((m.IT, D), F32)],
        here=True,
        name="forward",
    )
    def shards(width, height=D):
        if m.fast:
            return [shape(nz, rows, width)] * 2
        return [shape(height, width), shape(8, 128)]

    def weight_grad(left, right, name):
        return pallas(
            fn(weight_grad_kernel, m),
            shards(D),
            [left, right],
            [pltpu.VMEM((D, D), F32)],
            here=True,
            name=name,
        )

    down_keep, down_send = weight_grad(cot, active, "down_grad")
    g_hidden, down_all, keep0, keep1, send = pallas(
        fn(hidden_back_kernel, m, len(down_parts)),
        [shape(m.RA, m.FD), shape(D, m.FD), shape(m.OWN, D), shape(m.OWN, D), shape(2, m.OWN, D)],
        [cot, gate(slope, down_keep), up_all, *down_parts],
        here=True,
        name="hidden_back",
    )

    def add_pair(keep, core, name):
        (out,) = pallas(fn(pair_kernel, m), [shape(*keep.shape)], [keep, core], name=name)
        return out

    def add(left, right, name):
        (out,) = pallas(fn(add_kernel, m), [shape(*left.shape, dtype=F32)], [left, right], name=name)
        return out

    core2 = seq_to(send, 1)
    pair2 = add_pair(keep1, core2, "pair2")
    far2 = seq_to(pair2, 2)

    up_keep, up_send = weight_grad(normed2, gate(g_hidden, pair2), "up_grad")
    def branch(after):
        return pallas(
            fn(branch_kernel, m),
            [shape(m.OWN, D), shape(m.OWN, D), shape(2, m.OWN, D), shape(8, D, dtype=F32)],
            [gate(active, after), down_all, g_hidden, cot],
            name="branch",
        )

    if not CFG["br"]:
        b_keep0, b_keep1, b_send, vec_ff = branch(up_keep)
    g_resid, *blocks, vec_mid = pallas(
        fn(middle_kernel, m),
        [shape(m.OWN, D, dtype=F32), *[shape(m.OWN, 2 * WH)] * S, shape(8, D, dtype=F32)],
        [gate(keep0, up_keep if CFG["br"] else b_keep0), core2, far2, xhat2, rstd2, cot, out_all, vecs],
        [pltpu.VMEM((m.OWN, D), LOW)],
        here=True,
        name="middle",
    )
    if CFG["br"]:
        b_keep0, b_keep1, b_send, vec_ff = branch(g_resid)
    blocks = [blocks[0]] + [seq_to(blocks[e], e) for e in range(1, S)]
    if CFG["br"] == 1:
        blocks[0] = gate(blocks[0], b_keep0)

    def sum_x(keep, got, width, name):
        return pallas(
            fn(sum_x_kernel, m),
            [shape(rows, width, dtype=F32)] + [shape(rows, width)] * (nz - 1),
            [keep, got],
            name=name,
        )

    def to_z(parts):
        return [z_shift(part, k + 1) for k, part in enumerate(parts)]

    def scatter(full):
        return lax.psum_scatter(full, "dp", scatter_dimension=0, tiled=True).astype(F32)

    if m.fast:
        down_got, up_got = x_swap(down_send), x_swap(up_send)
        down_own, *down_sums = sum_x(gate(down_keep, blocks[0]), down_got, D, "down_x")
        down_z = to_z(down_sums)
        blocks[0] = gate(blocks[0], down_own)
    g_value, g_mixed, vo_keep, vo_send = pallas(
        fn(value_back_kernel, m),
        [shape(m.RA, WH), shape(m.RA, WH), *shards(2 * WH)],
        [probs, *blocks, normed, mixed],
        [pltpu.VMEM((m.RA, WH), LOW), pltpu.VMEM((D, 2 * WH), F32)],
        here=True,
        name="value_back",
    )
    if m.fast:
        vo_got = x_swap(vo_send)

        def sum_down(after):
            return pallas(
                fn(sum_down_kernel, m),
                [shape(rows, m.FD // 2)] * 2,
                [gate(down_own, after), *down_z],
                here=True,
                name="sum_down",
            )

    (g_qk,) = pallas(
        fn(attend_back_kernel, m),
        [shape(m.RA, 2 * WH)],
        [qkv, probs, g_mixed],
        name="attend_back",
    )
    g_last = g_qk
    if m.fast:
        up_own, vo_own, *both = pallas(
            fn(both_x_kernel, m),
            [shape(rows, m.FD, dtype=F32), shape(rows, 2 * WH, dtype=F32)]
            + [shape(m.up_rows, m.FD)] * (nz - 1),
            [gate(up_keep, g_qk), up_got, vo_keep, vo_got],
            name="both_x",
        )
        both_z = to_z(both)
        halves = sum_down(up_own)
        g_last = gate(g_qk, halves[0])

        def give_down(*after, start=()):
            down_halves = [exchange(gate(halves[k], *start), k) for k in range(2)]
            (out,) = pallas(
                fn(give_down_kernel, m),
                [shape(WH, S * m.hrows, dtype=F32)],
                [gate(down_halves[0], *after), down_halves[1]],
                here=True,
                name="give_down",
            )
            return out

    def qk_grad(after):
        return pallas(
            fn(weight_grad_kernel, m),
            shards(2 * WH),
            [normed, gate(g_last, after)],
            [pltpu.VMEM((D, 2 * WH), F32)],
            here=True,
            name="qk_grad",
        )

    if not CFG["ord"]:
        qk_keep, qk_send = qk_grad(g_qk)
    keep0, keep1, send, vec = pallas(
        fn(input_back_kernel, m),
        [shape(m.OWN, D), shape(2 * m.OWN, D), shape(2, 2 * m.OWN, D), shape(VECS, D, dtype=F32)],
        [gate(g_last, *([] if CFG["ord"] else [qk_keep])), g_value, xhat, w_first, vec_mid, vec_ff, b_keep1, b_send],
        here=True,
        name="input_back",
    )
    if CFG["ord"]:
        qk_keep, qk_send = qk_grad(vec)
    vec_core, core1 = seq_to(vec, 1), seq_to(send, 1)
    vec = add(vec, vec_core, "add_core")
    vec_far = seq_to(vec, 2)
    if m.fast and CFG["gd"] == 3:
        g_down = give_down(vec)
        keep1 = gate(keep1, g_down)
    pair1 = add_pair(gate(keep1, *([vec_far] if CFG["pair"] else [vec])), core1, "pair1")
    far1 = seq_to(pair1, 2)
    if m.fast:
        qk_got = x_swap(qk_send)

        def both_out(after):
            return pallas(
                fn(both_z_kernel, m),
                [shape(rows, m.FD, dtype=F32)] + [shape(rows, WH, dtype=F32)] * 2,
                [gate(up_own, after), vo_own, *both_z],
                name="both_out",
            )

        if CFG["gd"] in (1, 2):
            g_down = give_down(pair1)
        vec = add(gate(vec, *([pair1] if CFG["add"] else []), *([g_down] if CFG["gd"] == 1 else [])), vec_far, "add_far")
        vec_got = x_swap(vec)
        qk_own, vec_own, *qk_sums = pallas(
            fn(last_x_kernel, m),
            [shape(rows, 2 * WH, dtype=F32), shape(2 * VECS, D // 2, dtype=F32)]
            + [shape(rows + 2 * VECS, 2 * WH)] * (nz - 1),
            [qk_keep, qk_got, vec, vec_got],
            name="last_x",
        )
        if CFG["both"] == 2:
            g_up, g_value, g_out = both_out(qk_own)
            qk_sums[0] = gate(qk_sums[0], g_up)
            qk_sums[1] = gate(qk_sums[1], g_up)
            qk_sums[2] = gate(qk_sums[2], g_up)
        if CFG["gd"] == 2:
            qk_sums[0] = gate(qk_sums[0], g_down)
        qk_z = to_z(qk_sums)
        if CFG["both"] == 0:
            g_up, g_value, g_out = both_out(qk_own)
            keep0 = gate(keep0, g_up)
        keep0 = gate(keep0, qk_own)
    else:
        vec = lax.psum(vec + vec_far, "dp")
        vec = lax.dynamic_slice(vec, (0, dp * rows), (VECS, rows))
        g_vo, g_qk = scatter(vo_keep), scatter(qk_keep)
        g_value, g_out, g_query, g_key = g_vo[:, :WH], g_vo[:, WH:], g_qk[:, :WH], g_qk[:, WH:]
        g_up = scatter(up_keep)
        g_down = scatter(lax.all_to_all(down_keep.T, "seq", 1, 0, tiled=True))
        vec_outs = [vec[k] for k in range(8)] + [vec[8 : 8 + S].reshape(-1)]

    result, input_grad = pallas(
        fn(finish_kernel, m),
        [shape(m.B, m.R, D), shape(m.B, m.R, D)],
        [keep0, core1, far1, tokens, g_resid, vecs, b_keep0, resid],
        name="finish",
    )
    if m.fast:
        if CFG["both"] == 1:
            g_up, g_value, g_out = both_out(result)
        if not CFG["gd"]:
            g_down = give_down(g_value, result, start=[qk_own] if CFG["gx"] == 1 else qk_z if CFG["gx"] == 2 else [])
        g_down = g_down.T
        g_query, g_key, *vec_outs = pallas(
            fn(last_z_kernel, m),
            [shape(rows, WH, dtype=F32)] * 2 + [shape(rows, dtype=F32)] * 8 + [shape(S * m.hrows, dtype=F32)],
            [gate(qk_own, g_down), vec_own, *qk_z],
            [pltpu.VMEM((VECS, rows), F32)],
            here=True,
            name="query_key",
        )
    return (
        result,
        input_grad,
        g_query,
        g_key,
        g_value,
        g_out,
        g_up,
        g_down,
        *vec_outs[:7],
        vec_outs[8],
        vec_outs[7],
    )


def solution(mesh):
    rows3, mat, vec = P("dp", "seq", None), P("dp", "seq"), P("dp")
    return jax.shard_map(
        functools.partial(local, mesh),
        mesh=mesh,
        in_specs=(rows3, rows3, P("dp", None), vec) + (mat,) * 6 + (vec,) * 9,
        out_specs=(rows3, rows3) + (mat,) * 6 + (vec,) * 9,
        check_vma=False,
    )
```

```python
import functools
from types import SimpleNamespace

import jax
import jax.numpy as jnp
from jax import lax
from jax.experimental import pallas as pl
from jax.experimental.pallas import tpu as pltpu
from jax.sharding import PartitionSpec as P

HEADS = 12
COST = {'up_grad': 10000000000, 'branch': 10000000000, 'value_back': 10000000000, 'attend_back': 10000000000, 'finish': 10000000000, 'pack': 3000000000, 'sum_down': 1000, 'sum_up': 1000, 'last_x': 30000000000, 'hidden_back': 3000000000, 'qk_grad': 2000000000, 'stack_down': 5000000000, 'both_x': 500000000, 'split_down': 2000000000}
CFG = {'pair': 1, 'add': 1, 'za': 'direct', 'zu': 'bidir', 'zd': 'bidir', 'xu': 0, 'xd': 0, 'norm': 2, 'held': 0, 'split': 3, 'cot': 1, 'tok': 1, 'ord': 1, 'up': 0, 'vo': 0, 'br': 1, 'both': 0, 'og': 3, 'sa': 'each', 'su': 'each', 'sd': 'rest', 'gd': 2, 'gx': 0}
EPS = 1e-05
LOW = jnp.bfloat16
F32 = jnp.float32
VECS = 16
UP_BIAS = 12
SQRT_HALF = 0.7071067811865476
PDF_SCALE = 0.3989422804014327


def dot(left, right):
    return jnp.dot(left, right, preferred_element_type=F32)


def dot_t(left, right):
    return lax.dot_general(left, right, (((1,), (1,)), ((), ())), preferred_element_type=F32)


def t_dot(left, right):
    return lax.dot_general(left, right, (((0,), (0,)), ((), ())), preferred_element_type=F32)


def col_sum(values):
    return jnp.sum(values, axis=0, keepdims=True)


def ds(start, size, align=16):
    if not isinstance(start, int):
        start = pl.multiple_of(start, align)
    return pl.ds(start, size)


def pallas(body, outs, ins, scratch=(), smem=0, here=False, name=None, mib=8):
    flops = COST.get(name, 1000)
    nbytes = sum(a.size * a.dtype.itemsize for a in ins)
    nbytes += sum(s.size * jnp.dtype(s.dtype).itemsize for s in outs)
    near = pl.BlockSpec(memory_space=pltpu.VMEM)

    def run(*refs):
        if here:
            dp = lax.axis_index("dp")
            body((lax.axis_index("seq"), lax.div(dp, 2), lax.rem(dp, 2)), *refs)
        else:
            body(*refs)

    return pl.pallas_call(
        run,
        out_shape=outs,
        in_specs=[pl.BlockSpec(memory_space=pltpu.SMEM)] * smem + [near] * (len(ins) - smem),
        out_specs=[near] * len(outs),
        scratch_shapes=list(scratch),
        compiler_params=pltpu.CompilerParams(vmem_limit_bytes=mib * 2**20),
        cost_estimate=pl.CostEstimate(flops=flops, bytes_accessed=nbytes, transcendentals=0),
        name=name,
    )(*ins)


def shape(*dims, dtype=LOW):
    return jax.ShapeDtypeStruct(dims, dtype)


def part_index(m, sc, part):
    z, x = sc[1], sc[2]
    k = part % m.nz
    side = x if part < m.nz else 1 - x
    return lax.rem(z - k + m.nz, m.nz) * 2 + side


def spread(parts):
    out = []
    for part in parts:
        out += [part.at[k] for k in range(part.shape[0])] if len(part.shape) == 3 else [part]
    return out


def layer_norm(x):
    center = x - jnp.mean(x, axis=-1, keepdims=True)
    rstd = lax.rsqrt(jnp.mean(center * center, axis=-1, keepdims=True) + EPS)
    return center * rstd, rstd


def norm_back(grad, gain, xhat, rstd):
    scaled = grad * gain
    first = jnp.mean(scaled, axis=-1, keepdims=True)
    second = jnp.mean(scaled * xhat, axis=-1, keepdims=True)
    return rstd * (scaled - first - xhat * second)


def pack_kernel(m, query, key, value, *refs):
    vecs, first, rows = refs[:9], refs[9], refs[10]
    first[:, : m.WH] = query[...]
    first[:, m.WH : 2 * m.WH] = key[...]
    first[:, 2 * m.WH : 3 * m.WH] = value[...]
    first[:, 3 * m.WH :] = jnp.zeros((m.rows, m.wide - 3 * m.WH), LOW)
    rows[...] = jnp.zeros_like(rows)
    for k in range(8):
        rows[k : k + 1, :] = vecs[k][...].astype(F32).reshape(1, m.rows)
    up_bias = vecs[8][...].astype(F32).reshape(1, m.S * m.hrows)
    for c in range(m.S):
        rows[8 + c : 9 + c, :] = up_bias[:, c * m.hrows : (c + 1) * m.hrows]
    first[:, 3 * m.WH : 3 * m.WH + VECS] = rows[...].T.astype(LOW)


def pack_up_kernel(m, up, out, far, packed):
    half = m.rows // 2
    packed[: m.rows, :] = up[...]
    for side in range(2):
        at = slice(side * half, (side + 1) * half)
        packed[m.rows :, 2 * side * m.WH : (2 * side + 1) * m.WH] = out[at, :]
        packed[m.rows :, (2 * side + 1) * m.WH : (2 * side + 2) * m.WH] = far[at, :]


def split_down_kernel(m, sc, down_t, first, second):
    half = m.WH // 2
    for x in range(2):

        @pl.when(sc[2] == x)
        def _(x=x):
            first[...] = down_t[x * half : (x + 1) * half, :]
            second[...] = down_t[(1 - x) * half : (2 - x) * half, :]


def join_down_kernel(m, sc, first, second, down):
    width = m.FD // 2
    for x in range(2):

        @pl.when(sc[2] == x)
        def _(x=x):
            down[:, x * width : (x + 1) * width] = first[...]
            down[:, (1 - x) * width : (2 - x) * width] = second[...]


def stack_kernel(m, *refs):
    for k, ref in enumerate(refs[:-1]):
        refs[-1][k] = ref[...]


def norm_kernel(m, *refs):
    tokens, (xhat, x_scr) = refs[: m.S], refs[m.S :]
    x_scr[...] = jnp.zeros_like(x_scr)

    def item(b, carry):
        for d in range(m.S):
            x_scr[d * m.RP : d * m.RP + m.R, :] = tokens[d][b].astype(F32)
        xhat[ds(b * m.IT, m.IT), :], _ = layer_norm(x_scr[...])
        return carry

    lax.fori_loop(0, m.B, item, 0)


def attend_kernel(m, nparts, *refs):
    sc, text_mask, patch_count, xhat_ref = refs[:4]
    parts = refs[4 : 4 + nparts]
    qkv, normed, probs, packed, vecs, w_ref = refs[4 + nparts :]
    me = sc[0]
    if nparts == 1:
        w_ref[...] = parts[0][...]
    else:
        for p, part in enumerate(spread(parts)):
            w_ref[ds(part_index(m, sc, p) * m.rows, m.rows), :] = part[...]
    base = (3 * m.WH) // 128 * 128
    turned = w_ref[:, base : base + 128].astype(F32).T
    vecs[...] = turned[3 * m.WH - base : 3 * m.WH - base + VECS]
    for c in range(m.S):

        @pl.when(me == c)
        def _(c=c):
            for t in range(m.N // m.S):
                for k in range(m.S):
                    lanes = slice((t * m.S + k) * m.hrows, (t * m.S + k + 1) * m.hrows)
                    begin = c * m.WH + t * m.rows
                    vecs[UP_BIAS : UP_BIAS + 1, lanes] = vecs[8 + k : 9 + k, begin : begin + m.rows]

    gain, shift = vecs[0:1, :], vecs[1:2, :]
    q_bias = jnp.zeros((1, m.WH), F32)
    v_bias = jnp.zeros((1, m.WH), F32)
    for c in range(m.S):
        here = me == c
        q_bias = jnp.where(here, vecs[2:3, c * m.WH : (c + 1) * m.WH], q_bias)
        v_bias = jnp.where(here, vecs[3:4, c * m.WH : (c + 1) * m.WH], v_bias)
    bias = jnp.concatenate([q_bias, jnp.zeros((1, m.WH), F32), v_bias], axis=1)

    lane = lax.broadcasted_iota(jnp.int32, (1, m.IT), 1)
    place = jnp.full((1, m.IT), 1 << 20, jnp.int32)
    for d in range(m.S):
        row = lane - d * m.RP
        here = jnp.where(row < m.R, (me ^ d) * m.R + row, 1 << 20)
        place = jnp.where(row < 0, place, here)

    def item(b, carry):
        at = ds(b * m.IT, m.IT)
        low = (xhat_ref[at, :] * gain + shift).astype(LOW)
        normed[at, :] = low
        qkv[at, :] = (dot(low, w_ref[:, : 3 * m.WH]) + bias).astype(LOW)
        words = text_mask[b, 0]
        for k in range(1, m.TXT):
            words = words + text_mask[b, k]
        masked = jnp.where(
            place < m.TXT,
            jnp.where(place < words, 0.0, -1e30),
            jnp.where(place - m.TXT < patch_count[b], 0.0, -1e30),
        )
        half = m.IT // 2
        for h in range(m.H):
            q = qkv[at, h * m.hd : (h + 1) * m.hd] * LOW(m.hd**-0.5)
            k = qkv[at, m.WH + h * m.hd : m.WH + (h + 1) * m.hd]
            v = qkv[at, 2 * m.WH + h * m.hd : 2 * m.WH + (h + 1) * m.hd]
            s = dot_t(q, k) + masked
            e = jnp.exp(s - jnp.max(s, axis=-1, keepdims=True))
            p = (e * (1.0 / jnp.sum(e, axis=-1, keepdims=True))).astype(LOW)
            probs[b * m.H + h] = p
            o = dot(p, v).astype(LOW)
            packed[ds(b * half, half), h * m.hd : (h + 1) * m.hd] = o[:half]
            packed[ds(b * half, half), m.WH + h * m.hd : m.WH + (h + 1) * m.hd] = o[half:]
        return carry

    lax.fori_loop(0, m.B, item, 0, unroll=True)


def assemble_kernel(m, nparts, *refs):
    sc = refs[0]
    parts = refs[1 : 1 + nparts]
    w_up, w_out = refs[1 + nparts :]
    half = m.rows // 2
    per = m.N // m.S
    for p, part in enumerate(spread(parts)):
        i = part_index(m, sc, p)
        w_up[ds(i * m.rows, m.rows), :] = part[: m.rows]
        start = (sc[0] ^ lax.div(i, per)) * m.WH + lax.rem(i, per) * m.rows
        w_out[ds(start, half), :] = part[m.rows :, : 2 * m.WH]
        w_out[ds(start + half, half), :] = part[m.rows :, 2 * m.WH :]


def join_kernel(m, sc, own, other, *refs):
    cots = refs[: m.S]
    w_out, cot = refs[m.S :]
    for c in range(m.S):

        @pl.when(sc[0] == c)
        def _(c=c):
            for d in range(m.S):
                half = (own, other)[d % 2]
                lanes = slice((c ^ d) * m.WH, ((c ^ d) + 1) * m.WH)
                for e in range(m.S):
                    rows = slice((e ^ (d % 2)) * m.WH, ((e ^ (d % 2)) + 1) * m.WH)
                    w_out[e * m.WH : (e + 1) * m.WH, lanes] = half[rows, d // 2 * m.WH : (d // 2 + 1) * m.WH]

    pad_cot(m, cots, cot)


def pad_cot(m, cots, cot):
    cot[...] = jnp.zeros_like(cot)
    for b in range(m.B):
        for d in range(m.S):
            start = (b * m.S + d) * m.RP
            cot[start : start + m.R, :] = cots[d][b]


def forward_kernel(m, *refs):
    sc = refs[0]
    tokens = refs[1 : 1 + m.S]
    packed = refs[1 + m.S : 1 + 2 * m.S]
    w_out, w_up, vecs = refs[1 + 2 * m.S : 4 + 2 * m.S]
    normed, active, slope, mixed, resid_own, xhat_own, rstd_own, x_scr = refs[4 + 2 * m.S :]
    me = sc[0]
    out_bias, gain, shift = vecs[4:5, :], vecs[5:6, :], vecs[6:7, :]
    up_bias = vecs[UP_BIAS : UP_BIAS + 1, :]
    x_scr[...] = jnp.zeros_like(x_scr)

    def item(b, carry):
        at = ds(b * m.IT, m.IT)
        half = m.IT // 2
        for d in range(m.S):
            x_scr[d * m.RP : d * m.RP + m.R, :] = tokens[d][b].astype(F32)
        for e in range(m.S):
            for side in range(2):
                piece = packed[e][ds(b * half, half), side * m.WH : (side + 1) * m.WH]
                for t in range(2):
                    d = (2 * side + t) ^ e
                    mixed[ds(b * m.IT + d * m.RP, m.RP), e * m.WH : (e + 1) * m.WH] = piece[
                        t * m.RP : (t + 1) * m.RP
                    ]
        resid = x_scr[...] + (dot(mixed[at, :], w_out[...]) + out_bias)
        xhat, rstd = layer_norm(resid)
        own = ds(b * m.RP, m.RP)
        resid_own[own, :] = resid[: m.RP]
        xhat_own[own, :] = xhat[: m.RP]
        rstd_own[own, :] = jnp.broadcast_to(rstd[: m.RP], (m.RP, 128))
        low = (xhat * gain + shift).astype(LOW)
        normed[at, :] = low
        hidden = dot(low, w_up[...]) + up_bias
        cdf = 0.5 + 0.5 * lax.erf(hidden * SQRT_HALF)
        active[at, :] = (hidden * cdf).astype(LOW)
        slope[at, :] = cdf + hidden * (PDF_SCALE * jnp.exp(-0.5 * hidden * hidden))
        return carry

    lax.fori_loop(0, m.B, item, 0)


def hidden_back_kernel(m, nparts, *refs):
    sc, cot, slope, w_up = refs[:4]
    parts = refs[4 : 4 + nparts]
    g_hidden, w_down, keep0, keep1, send = refs[4 + nparts :]
    if nparts == 1:
        w_down[...] = parts[0][...]
    else:
        for p, part in enumerate(spread(parts)):
            w_down[ds(part_index(m, sc, p) * m.rows, m.rows), :] = part[...]

    def item(b, carry):
        at = ds(b * m.IT, m.IT)
        back = (dot(cot[at, :], w_down[...]) * slope[at, :]).astype(LOW)
        g_hidden[at, :] = back
        give_rows(m, b, dot_t(back, w_up[...]).astype(LOW), keep0, keep1, send)
        return carry

    lax.fori_loop(0, m.B, item, 0)


def give_shards(m, sc, total, keep, send):
    for k in range(m.nz):
        z = lax.rem(sc[1] + k, m.nz)
        keep[k] = total[ds((2 * z + sc[2]) * m.rows, m.rows), :].astype(LOW)
        send[k] = total[ds((2 * z + 1 - sc[2]) * m.rows, m.rows), :].astype(LOW)


def give(m, sc, total, keep, send):
    if m.fast:
        give_shards(m, sc, total, keep, send)
    else:
        keep[...] = total[...].astype(LOW)
        send[...] = jnp.zeros_like(send)


def give_rows(m, b, values, keep0, keep1, send):
    own = ds(b * m.RP, m.RP)
    keep0[own, :] = values[: m.RP]
    send[0, own, :] = values[m.RP : 2 * m.RP]
    keep1[own, :] = values[2 * m.RP : 3 * m.RP]
    send[1, own, :] = values[3 * m.RP : 4 * m.RP]


def weight_grad_kernel(m, sc, left, right, keep, send, total):
    step = 256
    for begin in range(0, m.D, step):
        total[begin : begin + step, :] = t_dot(left[:, begin : begin + step], right[...])
    give(m, sc, total, keep, send)


def branch_kernel(m, active, w_down, g_hidden, cot, keep0, keep1, send, vec):
    vec[...] = jnp.zeros_like(vec)

    def item(b, carry):
        at = ds(b * m.IT, m.IT)
        give_rows(m, b, dot_t(active[at, :], w_down[...]).astype(LOW), keep0, keep1, send)
        vec[0:1, :] += col_sum(cot[ds(b * m.IT, m.RP), :].astype(F32))
        vec[1:2, :] += col_sum(g_hidden[at, :].astype(F32))
        return carry

    lax.fori_loop(0, m.B, item, 0)


def pair_kernel(m, keep, core, out):
    out[...] = (keep[...].astype(F32) + core[1].astype(F32)).astype(LOW)


def add_kernel(m, left, right, out):
    out[...] = left[...] + right[...]


def middle_kernel(m, *refs):
    sc, keep0, core, far, xhat_own, rstd_own, cot, w_out, vecs = refs[:9]
    g_resid = refs[9]
    blocks = refs[10 : 10 + m.S]
    vec, low_scr = refs[10 + m.S :]
    me = sc[0]
    gain = vecs[5:6, :]
    grad = keep0[...].astype(F32) + core[0].astype(F32) + far[...].astype(F32)
    xhat = xhat_own[...]
    back = norm_back(grad, gain, xhat, rstd_own[:, 0:1])
    vec[...] = jnp.zeros_like(vec)
    vec[0:1, :] = col_sum(grad * xhat)
    vec[1:2, :] = col_sum(grad)
    for b in range(m.B):
        own = slice(b * m.RP, (b + 1) * m.RP)
        full = back[own] + cot[b * m.IT : b * m.IT + m.RP, :].astype(F32)
        g_resid[own, :] = full
        low_scr[own, :] = full.astype(LOW)
    low = low_scr[...]
    vec[2:3, :] = col_sum(low.astype(F32))
    g_mixed = dot_t(low, w_out[...]).astype(LOW)
    for e in range(m.S):
        blocks[e][:, : m.WH] = g_mixed[:, e * m.WH : (e + 1) * m.WH]
        picked = low[:, : m.WH]
        for c in range(1, m.S):
            picked = jnp.where((me ^ e) == c, low[:, c * m.WH : (c + 1) * m.WH], picked)
        blocks[e][:, m.WH :] = picked


def value_back_kernel(m, *refs):
    sc, probs = refs[:2]
    blocks = refs[2 : 2 + m.S]
    normed, mixed = refs[2 + m.S : 4 + m.S]
    g_value, g_mixed, keep, send, ga_scr, total = refs[4 + m.S :]

    def item(b, carry):
        at = ds(b * m.IT, m.IT)
        own = ds(b * m.RP, m.RP)
        for d in range(m.S):
            ga_scr[ds(b * m.IT + d * m.RP, m.RP), :] = blocks[d][own, m.WH :]
            g_mixed[ds(b * m.IT + d * m.RP, m.RP), :] = blocks[d][own, : m.WH]
        for h in range(m.H):
            lanes = slice(h * m.hd, (h + 1) * m.hd)
            g_value[at, lanes] = t_dot(probs[b * m.H + h], g_mixed[at, lanes]).astype(LOW)
        return carry

    lax.fori_loop(0, m.B, item, 0, unroll=True)
    total[:, : m.WH] = t_dot(normed[...], g_value[...])
    g_out = t_dot(mixed[...], ga_scr[...])
    for e in range(m.S):
        total[ds((sc[0] ^ e) * m.WH, m.WH), m.WH :] = g_out[e * m.WH : (e + 1) * m.WH]
    give(m, sc, total, keep, send)


def attend_back_kernel(m, qkv, probs, g_mixed, g_qk):
    scale = m.hd**-0.5

    def item(b, carry):
        at = ds(b * m.IT, m.IT)
        for h in range(m.H):
            lanes = slice(h * m.hd, (h + 1) * m.hd)
            q = qkv[at, h * m.hd : (h + 1) * m.hd]
            k = qkv[at, m.WH + h * m.hd : m.WH + (h + 1) * m.hd]
            v = qkv[at, 2 * m.WH + h * m.hd : 2 * m.WH + (h + 1) * m.hd]
            p = probs[b * m.H + h].astype(F32)
            gp = dot_t(g_mixed[at, lanes], v)
            gs = (p * (gp - jnp.sum(p * gp, axis=-1, keepdims=True))).astype(LOW)
            g_qk[at, h * m.hd : (h + 1) * m.hd] = (dot(gs, k) * scale).astype(LOW)
            g_qk[at, m.WH + h * m.hd : m.WH + (h + 1) * m.hd] = (t_dot(gs, q) * scale).astype(LOW)
        return carry

    lax.fori_loop(0, m.B, item, 0, unroll=True)


def input_back_kernel(m, sc, g_qk, g_value, xhat, w, vec_mid, vec_ff, b_keep1, b_send, keep0, keep1, send, v_scr):
    me = sc[0]
    v_scr[...] = jnp.zeros_like(v_scr)

    def item(b, carry):
        at = ds(b * m.IT, m.IT)
        grad = dot_t(g_qk[at, :], w[:, : 2 * m.WH]) + dot_t(g_value[at, :], w[:, 2 * m.WH : 3 * m.WH])
        v_scr[0:1, :] += col_sum(grad * xhat[at, :])
        v_scr[1:2, :] += col_sum(grad)
        give_rows(m, b, grad.astype(LOW), keep0, keep1, send)
        return carry

    lax.fori_loop(0, m.B, item, 0)
    q_sum = col_sum(g_qk[:, : m.WH].astype(F32))
    v_sum = col_sum(g_value[...].astype(F32))
    for c in range(m.S):
        here = me == c
        lanes = slice(c * m.WH, (c + 1) * m.WH)
        v_scr[2:3, lanes] = jnp.where(here, q_sum, 0.0)
        v_scr[3:4, lanes] = jnp.where(here, v_sum, 0.0)
        for t in range(m.N // m.S):
            for k in range(m.S):
                begin = c * m.WH + t * m.rows
                part = vec_ff[1:2, (t * m.S + k) * m.hrows : (t * m.S + k + 1) * m.hrows]
                v_scr[8 + k : 9 + k, begin : begin + m.rows] = jnp.where(here, part, 0.0)
    v_scr[4:5, :] = vec_mid[2:3, :]
    v_scr[5:6, :] = vec_mid[0:1, :]
    v_scr[6:7, :] = vec_mid[1:2, :]
    v_scr[7:8, :] = vec_ff[0:1, :]
    keep1[m.OWN :, :] = b_keep1[...]
    send[0, m.OWN :, :] = b_send[0]
    send[1, m.OWN :, :] = b_send[1]


def sum_x_kernel(m, keep, got, own, *outs):
    own[...] = keep[0].astype(F32) + got[0].astype(F32)
    for k, out in enumerate(outs):
        out[...] = (keep[k + 1].astype(F32) + got[k + 1].astype(F32)).astype(LOW)


def both_x_kernel(m, up_keep, up_got, vo_keep, vo_got, up_own, vo_own, *outs):
    half = m.rows // 2
    up_own[...] = up_keep[0].astype(F32) + up_got[0].astype(F32)
    vo_own[...] = vo_keep[0].astype(F32) + vo_got[0].astype(F32)
    for k, out in enumerate(outs):
        out[: m.rows, :] = (up_keep[k + 1].astype(F32) + up_got[k + 1].astype(F32)).astype(LOW)
        total = (vo_keep[k + 1].astype(F32) + vo_got[k + 1].astype(F32)).astype(LOW)
        out[m.rows :, : 2 * m.WH] = total[:half]
        out[m.rows :, 2 * m.WH :] = total[half:]


def both_z_kernel(m, up_own, vo_own, *refs):
    rest, (g_up, first, second) = refs[: m.nz - 1], refs[m.nz - 1 :]
    half = m.rows // 2
    total = up_own[...]
    for r in rest:
        total = total + r[: m.rows, :].astype(F32)
    g_up[...] = total
    for side in range(2):
        at = slice(side * half, (side + 1) * half)
        total = vo_own[at, :]
        for r in rest:
            total = total + r[m.rows :, 2 * m.WH * side : 2 * m.WH * (side + 1)].astype(F32)
        first[at, :] = total[:, : m.WH]
        second[at, :] = total[:, m.WH :]


def last_x_kernel(m, keep, got, vec, vec_got, own, vec_own, *outs):
    own[...] = keep[0].astype(F32) + got[0].astype(F32)
    values = vec[...] + vec_got[...]
    half = m.D // 2
    vec_own[:VECS, :] = values[:, :half]
    vec_own[VECS:, :] = values[:, half:]
    for k, out in enumerate(outs):
        out[: m.rows, :] = (keep[k + 1].astype(F32) + got[k + 1].astype(F32)).astype(LOW)
        out[m.rows :, :] = vec_own[...].astype(LOW)


def sum_z_kernel(m, *refs):
    own, rest, outs = refs[0], refs[1 : m.nz], refs[m.nz :]
    total = own[...]
    for r in rest:
        total = total + r[...].astype(F32)
    outs[0][...] = total[:, : m.WH]
    outs[1][...] = total[:, m.WH :]


def last_z_kernel(m, sc, own, vec_own, *refs):
    rest, (first, second), vecs, picked = refs[: m.nz - 1], refs[m.nz - 1 : m.nz + 1], refs[m.nz + 1 : -1], refs[-1]
    total, values = own[...], vec_own[...]
    for r in rest:
        total = total + r[: m.rows, :].astype(F32)
        values = values + r[m.rows :, :].astype(F32)
    first[...] = total[:, : m.WH]
    second[...] = total[:, m.WH :]
    for i in range(m.N):

        @pl.when(2 * sc[1] + sc[2] == i)
        def _(i=i):
            side, lane = divmod(i * m.rows, m.D // 2)
            picked[...] = values[side * VECS : (side + 1) * VECS, lane : lane + m.rows]

    for k in range(8):
        vecs[k][...] = picked[k : k + 1, :].reshape(m.rows)
    vecs[8][...] = jnp.concatenate([picked[8 + c : 9 + c, :] for c in range(m.S)], axis=1).reshape(m.S * m.rows)


def sum_down_kernel(m, sc, own, *refs):
    rest, (first, second) = refs[:-2], refs[-2:]
    total = own[...]
    for r in rest:
        total = total + r[...].astype(F32)
    width = m.FD // 2
    for x in range(2):

        @pl.when(sc[2] == x)
        def _(x=x):
            first[...] = total[:, x * width : (x + 1) * width].astype(LOW)
            second[...] = total[:, (1 - x) * width : (2 - x) * width].astype(LOW)


def sum_up_kernel(m, own, *refs):
    rest, out = refs[:-1], refs[-1]
    total = own[...]
    for r in rest:
        total = total + r[...].astype(F32)
    out[...] = total


def give_down_kernel(m, sc, first, second, g_down):
    for x in range(2):

        @pl.when(sc[2] == x)
        def _(x=x):
            g_down[x * m.rows : (x + 1) * m.rows, :] = first[...].astype(F32)
            g_down[(1 - x) * m.rows : (2 - x) * m.rows, :] = second[...].astype(F32)


def finish_kernel(m, *refs):
    keep0, core, far, tokens, g_resid, vecs, b_keep, resid = refs[:8]
    result, input_grad = refs[8:]
    gain, down_bias = vecs[0:1, :], vecs[7:8, :]
    for b in range(m.B):
        own = slice(b * m.RP, b * m.RP + m.R)
        also = slice(m.OWN + b * m.RP, m.OWN + b * m.RP + m.R)
        grad = keep0[own, :].astype(F32) + core[0, own, :].astype(F32) + far[own, :].astype(F32)
        xhat, rstd = layer_norm(tokens[b].astype(F32))
        back = norm_back(grad, gain, xhat, rstd)
        input_grad[b] = (g_resid[own, :] + back).astype(LOW)
        branch = b_keep[own, :].astype(F32) + core[0, also, :].astype(F32) + far[also, :].astype(F32)
        result[b] = (resid[own, :] + (branch + down_bias)).astype(LOW)


def plan(mesh, tokens, text_mask, w_query, w_up):
    m = SimpleNamespace()
    m.N, m.S = mesh.shape["dp"], mesh.shape["seq"]
    m.B, m.R, m.D = tokens.shape
    m.RP = -(-m.R // 16) * 16
    m.IT = m.S * m.RP
    m.RA = m.B * m.IT
    m.OWN = m.B * m.RP
    m.TXT = text_mask.shape[1]
    m.rows, m.WH = w_query.shape
    m.hd = m.D // HEADS
    m.H = HEADS // m.S
    m.FD = w_up.shape[1]
    m.hrows = m.FD // m.N
    m.fast = m.N == 2 * m.S
    m.nz = m.N // 2
    m.wide = -(-(3 * m.WH + VECS) // 128) * 128
    m.up_rows = m.rows + m.rows // 2
    return m


def local(
    mesh,
    tokens,
    cotangent,
    text_mask,
    patch_count,
    w_query,
    w_key,
    w_value,
    w_out,
    w_up,
    w_down,
    norm1_gain,
    norm1_bias,
    query_bias,
    value_bias,
    out_bias,
    norm2_gain,
    norm2_bias,
    up_bias,
    down_bias,
):
    m = plan(mesh, tokens, text_mask, w_query, w_up)
    N, S, rows, WH, D, nz = m.N, m.S, m.rows, m.WH, m.D, m.nz
    dp = lax.axis_index("dp").astype(jnp.int32)
    me = lax.axis_index("seq").astype(jnp.int32)
    fn = functools.partial

    def seq_to(x, e):
        return lax.ppermute(x, "seq", [(i, i ^ e) for i in range(S)])

    def x_swap(x):
        return lax.ppermute(x, "dp", [(i, i ^ 1) for i in range(N)])

    def z_shift(x, k):
        return lax.ppermute(x, "dp", [(i, (i + 2 * k) % N) for i in range(N)])

    def gate(x, *others):
        return lax.optimization_barrier((x, *others))[0]

    def direct(x):
        same = [x] + [z_shift(x, k) for k in range(1, nz)]
        return same + [x_swap(v) for v in same]

    def around(x, kind):
        if kind == "direct":
            return [x] + [z_shift(x, k) for k in range(1, nz)]
        if kind == "ring":
            out = [x]
            for _ in range(1, nz):
                out.append(z_shift(out[-1], 1))
            return out
        a, b = z_shift(x, 1), z_shift(x, nz - 1)
        return [x, a, z_shift(a, 1), b]

    def swapped(same, kind, name, after=()):
        if kind == "each":
            return [x_swap(same[0])] + [x_swap(gate(v, *after)) for v in same[1:]]
        begin = 1 if kind == "rest" else 0
        rest = [gate(same[begin], *after), *same[begin + 1 :]]
        (stacked,) = pallas(fn(stack_kernel, m), [shape(len(rest), *same[0].shape)], rest, name=name)
        return [x_swap(same[0])] * begin + [x_swap(stacked)]

    def exchange(x, k):
        pairs = []
        for i in range(N):
            for j in range(S):
                to = 2 * j + (i + k) % 2
                pairs.append((i * S + j, to * S + i // 2))
        return lax.ppermute(x, ("dp", "seq"), pairs)

    def gather_seq(x):
        far = seq_to(x, 2)
        return [x, seq_to(x, 1), far, seq_to(far, 1)]

    vectors = [norm1_gain, norm1_bias, query_bias, value_bias, out_bias, norm2_gain, norm2_bias, down_bias, up_bias]
    if m.fast:
        (first,) = pallas(
            fn(pack_kernel, m),
            [shape(rows, m.wide)],
            [w_query, w_key, w_value, *vectors],
            [pltpu.VMEM((VECS, rows), F32)],
            name="pack",
            mib=60,
        )
        first_same = around(first, CFG["za"])
        first_parts = first_same + swapped(first_same, CFG["sa"], "stack_first")
        out_far = seq_to(gate(w_out, *{0: [], 1: [first_parts[nz]], 2: [first_same[1]], 3: [first]}[CFG["og"]]), 2)
        (up_out,) = pallas(
            fn(pack_up_kernel, m), [shape(m.up_rows, D)], [gate(w_up, first), w_out, out_far], name="pack_up"
        )
        halves = pallas(
            fn(split_down_kernel, m),
            [shape(WH // 2, S * m.hrows)] * 2,
            [gate(w_down.T, *{0: [], 1: [first], 2: [up_out], 3: [first_same[1]], 4: first_same[1:]}[CFG["split"]])],
            here=True,
            name="split_down",
        )
        (down,) = pallas(
            fn(join_down_kernel, m),
            [shape(rows, m.FD)],
            [exchange(halves[k], k) for k in range(2)],
            here=True,
            name="join_down",
        )
        token_blocks = gather_seq(gate(tokens, *{0: [], 1: [first]}[CFG["tok"]]))
        cot_blocks = gather_seq(gate(cotangent, *{0: [first], 1: [token_blocks[2]], 2: [up_out]}[CFG["cot"]]))
        up_same = around(up_out, CFG["zu"])
        down_same = around(down, CFG["zd"])
        norm_after = {0: [], 1: [up_out], 2: [up_out, down], 3: [up_out, *first_same[1:]], 4: [up_out, down, *first_same[1:]]}[CFG["norm"]]
        held = {0: [], 1: [cot_blocks[2]], 2: [up_same[1]], 3: [up_same[1], up_same[-1]], 4: [down]}[CFG["held"]]
    else:
        token_blocks = gather_seq(tokens)
        cot_blocks = gather_seq(cotangent)
        held = norm_after = []
        pad = jnp.zeros((rows, m.wide - 3 * WH - VECS), LOW)
        vec_rows = jnp.concatenate(vectors + [jnp.zeros(((VECS - 8 - S) * rows,), LOW)]).reshape(VECS, rows)
        first = jnp.concatenate([w_query, w_key, w_value, vec_rows.T, pad], axis=1)
        first_parts = [lax.all_gather(first, "dp", axis=0, tiled=True)]
        up_all = lax.all_gather(w_up, "dp", axis=0, tiled=True)
        down_all = lax.all_gather(w_down, "dp", axis=0, tiled=True)
        down_parts = [lax.all_to_all(down_all, "seq", 0, 1, tiled=True).T]
        heads = lax.all_gather(lax.all_gather(w_out, "seq", axis=1, tiled=True), "dp", axis=0, tiled=True)
        heads = heads.reshape(S, WH, D)
        out_all = jnp.concatenate([lax.dynamic_index_in_dim(heads, me ^ e, keepdims=False) for e in range(S)])

    (xhat,) = pallas(
        fn(norm_kernel, m),
        [shape(m.RA, D, dtype=F32)],
        [gate(token_blocks[0], *norm_after), *token_blocks[1:]],
        [pltpu.VMEM((m.IT, D), F32)],
        name="norm",
    )
    qkv, normed, probs, packed, vecs, w_first = pallas(
        fn(attend_kernel, m, len(first_parts)),
        [
            shape(m.RA, 3 * WH),
            shape(m.RA, D),
            shape(m.B * m.H, m.IT, m.IT),
            shape(m.B * m.IT // 2, 2 * WH),
            shape(VECS, D, dtype=F32),
            shape(D, m.wide),
        ],
        [text_mask, patch_count, gate(xhat, *held), *first_parts],
        smem=2,
        here=True,
        name="attend",
    )
    packed_blocks = gather_seq(packed)
    if m.fast:
        after = [packed] if CFG["xu"] else []
        up_parts = up_same + swapped(up_same, CFG["su"], "stack_up", after)
        after = [packed] if CFG["xd"] else []
        down_parts = down_same + swapped(down_same, CFG["sd"], "stack_down", after)

    if m.fast:
        up_all, half = pallas(
            fn(assemble_kernel, m, len(up_parts)),
            [shape(D, m.FD), shape(D, 2 * WH)],
            [*up_parts],
            here=True,
            name="assemble",
        )
        out_all, cot = pallas(
            fn(join_kernel, m),
            [shape(D, D), shape(m.RA, D)],
            [half, seq_to(half, 1), *cot_blocks],
            here=True,
            name="join",
        )
    else:

        def only_pad(*refs):
            pad_cot(m, refs[:S], refs[S])

        (cot,) = pallas(only_pad, [shape(m.RA, D)], cot_blocks, name="pad_cot")

    normed2, active, slope, mixed, resid, xhat2, rstd2 = pallas(
        fn(forward_kernel, m),
        [
            shape(m.RA, D),
            shape(m.RA, m.FD),
            shape(m.RA, m.FD, dtype=F32),
            shape(m.RA, D),
            shape(m.OWN, D, dtype=F32),
            shape(m.OWN, D, dtype=F32),
            shape(m.OWN, 128, dtype=F32),
        ],
        [*token_blocks, *packed_blocks, out_all, up_all, vecs],
        [pltpu.VMEM((m.IT, D), F32)],
        here=True,
        name="forward",
    )
    def shards(width, height=D):
        if m.fast:
            return [shape(nz, rows, width)] * 2
        return [shape(height, width), shape(8, 128)]

    def weight_grad(left, right, name):
        return pallas(
            fn(weight_grad_kernel, m),
            shards(D),
            [left, right],
            [pltpu.VMEM((D, D), F32)],
            here=True,
            name=name,
        )

    down_keep, down_send = weight_grad(cot, active, "down_grad")
    g_hidden, down_all, keep0, keep1, send = pallas(
        fn(hidden_back_kernel, m, len(down_parts)),
        [shape(m.RA, m.FD), shape(D, m.FD), shape(m.OWN, D), shape(m.OWN, D), shape(2, m.OWN, D)],
        [cot, gate(slope, down_keep), up_all, *down_parts],
        here=True,
        name="hidden_back",
    )

    def add_pair(keep, core, name):
        (out,) = pallas(fn(pair_kernel, m), [shape(*keep.shape)], [keep, core], name=name)
        return out

    def add(left, right, name):
        (out,) = pallas(fn(add_kernel, m), [shape(*left.shape, dtype=F32)], [left, right], name=name)
        return out

    core2 = seq_to(send, 1)
    pair2 = add_pair(keep1, core2, "pair2")
    far2 = seq_to(pair2, 2)

    up_keep, up_send = weight_grad(normed2, gate(g_hidden, pair2), "up_grad")
    def branch(after):
        return pallas(
            fn(branch_kernel, m),
            [shape(m.OWN, D), shape(m.OWN, D), shape(2, m.OWN, D), shape(8, D, dtype=F32)],
            [gate(active, after), down_all, g_hidden, cot],
            name="branch",
        )

    if not CFG["br"]:
        b_keep0, b_keep1, b_send, vec_ff = branch(up_keep)
    g_resid, *blocks, vec_mid = pallas(
        fn(middle_kernel, m),
        [shape(m.OWN, D, dtype=F32), *[shape(m.OWN, 2 * WH)] * S, shape(8, D, dtype=F32)],
        [gate(keep0, up_keep if CFG["br"] else b_keep0), core2, far2, xhat2, rstd2, cot, out_all, vecs],
        [pltpu.VMEM((m.OWN, D), LOW)],
        here=True,
        name="middle",
    )
    if CFG["br"]:
        b_keep0, b_keep1, b_send, vec_ff = branch(g_resid)
    blocks = [blocks[0]] + [seq_to(blocks[e], e) for e in range(1, S)]
    if CFG["br"] == 1:
        blocks[0] = gate(blocks[0], b_keep0)

    def sum_x(keep, got, width, name):
        return pallas(
            fn(sum_x_kernel, m),
            [shape(rows, width, dtype=F32)] + [shape(rows, width)] * (nz - 1),
            [keep, got],
            name=name,
        )

    def to_z(parts):
        return [z_shift(part, k + 1) for k, part in enumerate(parts)]

    def scatter(full):
        return lax.psum_scatter(full, "dp", scatter_dimension=0, tiled=True).astype(F32)

    if m.fast:
        down_got, up_got = x_swap(down_send), x_swap(up_send)
        down_own, *down_sums = sum_x(gate(down_keep, blocks[0]), down_got, D, "down_x")
        down_z = to_z(down_sums)
        blocks[0] = gate(blocks[0], down_own)
    g_value, g_mixed, vo_keep, vo_send = pallas(
        fn(value_back_kernel, m),
        [shape(m.RA, WH), shape(m.RA, WH), *shards(2 * WH)],
        [probs, *blocks, normed, mixed],
        [pltpu.VMEM((m.RA, WH), LOW), pltpu.VMEM((D, 2 * WH), F32)],
        here=True,
        name="value_back",
    )
    if m.fast:
        vo_got = x_swap(vo_send)

        def sum_down(after):
            return pallas(
                fn(sum_down_kernel, m),
                [shape(rows, m.FD // 2)] * 2,
                [gate(down_own, after), *down_z],
                here=True,
                name="sum_down",
            )

    (g_qk,) = pallas(
        fn(attend_back_kernel, m),
        [shape(m.RA, 2 * WH)],
        [qkv, probs, g_mixed],
        name="attend_back",
    )
    g_last = g_qk
    if m.fast:
        up_own, vo_own, *both = pallas(
            fn(both_x_kernel, m),
            [shape(rows, m.FD, dtype=F32), shape(rows, 2 * WH, dtype=F32)]
            + [shape(m.up_rows, m.FD)] * (nz - 1),
            [gate(up_keep, g_qk), up_got, vo_keep, vo_got],
            name="both_x",
        )
        both_z = to_z(both)
        halves = sum_down(up_own)
        g_last = gate(g_qk, halves[0])

        def give_down(*after, start=()):
            down_halves = [exchange(gate(halves[k], *start), k) for k in range(2)]
            (out,) = pallas(
                fn(give_down_kernel, m),
                [shape(WH, S * m.hrows, dtype=F32)],
                [gate(down_halves[0], *after), down_halves[1]],
                here=True,
                name="give_down",
            )
            return out

    def qk_grad(after):
        return pallas(
            fn(weight_grad_kernel, m),
            shards(2 * WH),
            [normed, gate(g_last, after)],
            [pltpu.VMEM((D, 2 * WH), F32)],
            here=True,
            name="qk_grad",
        )

    if not CFG["ord"]:
        qk_keep, qk_send = qk_grad(g_qk)
    keep0, keep1, send, vec = pallas(
        fn(input_back_kernel, m),
        [shape(m.OWN, D), shape(2 * m.OWN, D), shape(2, 2 * m.OWN, D), shape(VECS, D, dtype=F32)],
        [gate(g_last, *([] if CFG["ord"] else [qk_keep])), g_value, xhat, w_first, vec_mid, vec_ff, b_keep1, b_send],
        here=True,
        name="input_back",
    )
    if CFG["ord"]:
        qk_keep, qk_send = qk_grad(vec)
    vec_core, core1 = seq_to(vec, 1), seq_to(send, 1)
    vec = add(vec, vec_core, "add_core")
    vec_far = seq_to(vec, 2)
    if m.fast and CFG["gd"] == 3:
        g_down = give_down(vec)
        keep1 = gate(keep1, g_down)
    pair1 = add_pair(gate(keep1, *([vec_far] if CFG["pair"] else [vec])), core1, "pair1")
    far1 = seq_to(pair1, 2)
    if m.fast:
        qk_got = x_swap(qk_send)

        def both_out(after):
            return pallas(
                fn(both_z_kernel, m),
                [shape(rows, m.FD, dtype=F32)] + [shape(rows, WH, dtype=F32)] * 2,
                [gate(up_own, after), vo_own, *both_z],
                name="both_out",
            )

        if CFG["gd"] in (1, 2):
            g_down = give_down(pair1)
        vec = add(gate(vec, *([pair1] if CFG["add"] else []), *([g_down] if CFG["gd"] == 1 else [])), vec_far, "add_far")
        vec_got = x_swap(vec)
        qk_own, vec_own, *qk_sums = pallas(
            fn(last_x_kernel, m),
            [shape(rows, 2 * WH, dtype=F32), shape(2 * VECS, D // 2, dtype=F32)]
            + [shape(rows + 2 * VECS, 2 * WH)] * (nz - 1),
            [qk_keep, qk_got, vec, vec_got],
            name="last_x",
        )
        if CFG["both"] == 2:
            g_up, g_value, g_out = both_out(qk_own)
            qk_sums[0] = gate(qk_sums[0], g_up)
            qk_sums[1] = gate(qk_sums[1], g_up)
            qk_sums[2] = gate(qk_sums[2], g_up)
        if CFG["gd"] == 2:
            qk_sums[0] = gate(qk_sums[0], g_down)
        qk_z = to_z(qk_sums)
        if CFG["both"] == 0:
            g_up, g_value, g_out = both_out(qk_own)
            keep0 = gate(keep0, g_up)
        keep0 = gate(keep0, qk_own)
    else:
        vec = lax.psum(vec + vec_far, "dp")
        vec = lax.dynamic_slice(vec, (0, dp * rows), (VECS, rows))
        g_vo, g_qk = scatter(vo_keep), scatter(qk_keep)
        g_value, g_out, g_query, g_key = g_vo[:, :WH], g_vo[:, WH:], g_qk[:, :WH], g_qk[:, WH:]
        g_up = scatter(up_keep)
        g_down = scatter(lax.all_to_all(down_keep.T, "seq", 1, 0, tiled=True))
        vec_outs = [vec[k] for k in range(8)] + [vec[8 : 8 + S].reshape(-1)]

    result, input_grad = pallas(
        fn(finish_kernel, m),
        [shape(m.B, m.R, D), shape(m.B, m.R, D)],
        [keep0, core1, far1, tokens, g_resid, vecs, b_keep0, resid],
        name="finish",
    )
    if m.fast:
        if CFG["both"] == 1:
            g_up, g_value, g_out = both_out(result)
        if not CFG["gd"]:
            g_down = give_down(g_value, result, start=[qk_own] if CFG["gx"] == 1 else qk_z if CFG["gx"] == 2 else [])
        g_down = g_down.T
        g_query, g_key, *vec_outs = pallas(
            fn(last_z_kernel, m),
            [shape(rows, WH, dtype=F32)] * 2 + [shape(rows, dtype=F32)] * 8 + [shape(S * m.hrows, dtype=F32)],
            [gate(qk_own, g_down), vec_own, *qk_z],
            [pltpu.VMEM((VECS, rows), F32)],
            here=True,
            name="query_key",
        )
    return (
        result,
        input_grad,
        g_query,
        g_key,
        g_value,
        g_out,
        g_up,
        g_down,
        *vec_outs[:7],
        vec_outs[8],
        vec_outs[7],
    )


def solution(mesh):
    rows3, mat, vec = P("dp", "seq", None), P("dp", "seq"), P("dp")
    return jax.shard_map(
        functools.partial(local, mesh),
        mesh=mesh,
        in_specs=(rows3, rows3, P("dp", None), vec) + (mat,) * 6 + (vec,) * 9,
        out_specs=(rows3, rows3) + (mat,) * 6 + (vec,) * 9,
        check_vma=False,
    )
```
